128 devices in a mesh: ind: 64 (over y, x, z), snp: 2 (over core).
Axes of the slice: x: 4, y: 4, z: 4, core: 2. Of those that a mesh axis runs over, the one named last changes fastest.
Arguments:
- genotypes: bfloat16 [2, 249856, 1024], P(None, 'ind', 'snp'), may hold values from -0.013387887 to 0.013387887
- residual: float32 [32, 249856], P(None, 'ind'), may hold values from -7 to 7
- effects: float32 [2, 32, 1024], P(None, None, 'snp'), may hold values from -6 to 6
- noise: float32 [2, 32, 1024], replicated, may hold values from -6 to 6
- prior_var: float32 [2048], replicated, may hold values from 0.1 to 2
- block_snps: int32 [2048], replicated, may hold values from 0 to 2047, each once
- noise_var: float32 [32], replicated, may hold values from 0.5 to 2
- chi_scaled: float32 [32], replicated, may hold values from 0.8 to 1.25
Outputs:
- new_effects: float32 [2, 32, 1024], P(None, None, 'snp')
- new_residual: float32 [32, 249856], P(None, 'ind')
- variance_draw: float32 [32], replicated
The draws below stay inside these ranges and needn't reach their ends.
Inputs may be any that keep to these rules, and one draw needn't show every extreme that they name: `block_snps`: every table row appears once; entries b * 1024 to (b + 1) * 1024 - 1 belong to block b.
All inputs are finite; a program needn't handle non-finite values.
Results may differ from the reference program's by a relative error of at most 0.004.
Values may be sent and summed in bfloat16 or wider, within the bound.
No kernel may reach another device: no remote copies, remote signals or barrier semaphores. Data moves between devices by JAX's collectives and lax.ppermute only.
A program may use at most 192 MiB of HBM per device.

```python
import math
import jax
import jax.numpy as jnp
from jax import lax

BLOCK = 1024
BLOCKS = 2
CHAINS = 32
IND = 249856
SNP_TOT = 2048


def draw_genotypes(key, part):
    key = jax.random.fold_in(key, 11)
    first_key = jax.random.fold_in(key, 0)
    base_noise = jax.random.truncated_normal(first_key, -4.0, 4.0, (BLOCKS, IND, BLOCK), jnp.float32)
    mixed = base_noise + 0.8 * jnp.roll(base_noise, 1, axis=2) + 0.5 * jnp.roll(base_noise, 2, axis=2)
    return (mixed / jnp.sqrt(1.89 * IND)).astype(jnp.bfloat16)


def draw_residual(key, part):
    key = jax.random.fold_in(key, 23)
    position = jnp.arange(IND, dtype=jnp.float32)[None, :] / (IND - 1)
    values = jax.random.truncated_normal(key, -4.0, 4.0, (CHAINS, IND), jnp.float32)
    return values * jnp.sqrt(1.0 + 2.0 * position)


def block_scale(own_key, dims, pieces, smallest, largest):
    level = 1.0
    for dim, parts in pieces:
        steps = jax.random.uniform(jax.random.fold_in(jax.random.fold_in(own_key, 6), dim), (parts,), jnp.float32, smallest / len(pieces), largest / len(pieces))
        level = level * jnp.repeat(jnp.exp(steps), dims[dim] // parts).reshape((-1,) + (1,) * (len(dims) - 1 - dim))
    return level


def gaussian(rng, extent, scale, most, cuts=(), held_as=jnp.bfloat16):
    array = scale * jax.random.normal(rng, extent, jnp.float32)
    if cuts:
        array = array * block_scale(rng, extent, cuts, -0.22, 0.18)
    return jnp.clip(array, -most, most).astype(held_as)


def setup_inputs(seed: int = 0) -> dict:
    seeds = jax.random.split(jax.random.key(seed), 9)
    genotypes = draw_genotypes(jax.random.fold_in(seeds[8], 71), 0)
    residual = draw_residual(jax.random.fold_in(seeds[8], 71), 0)
    effects = gaussian(seeds[2], (BLOCKS, CHAINS, BLOCK), 1.0, 6.0, ((2, 2),), jnp.float32)
    noise = gaussian(seeds[3], (BLOCKS, CHAINS, BLOCK), 1.0, 6.0, (), jnp.float32)
    prior_var = jnp.clip(jnp.exp(jax.random.uniform(seeds[4], (SNP_TOT,), jnp.float32, math.log(0.1), math.log(2.0))), 0.1, 2.0)
    block_snps = jax.random.permutation(seeds[5], SNP_TOT).astype(jnp.int32)
    noise_var = jnp.clip(jnp.exp(jax.random.uniform(seeds[6], (CHAINS,), jnp.float32, math.log(0.5), math.log(2.0))), 0.5, 2.0)
    chi_scaled = jnp.clip(jax.random.uniform(seeds[7], (CHAINS,), jnp.float32, 0.8, 1.25), 0.8, 1.25)
    return {"genotypes": genotypes, "residual": residual, "effects": effects, "noise": noise, "prior_var": prior_var, "block_snps": block_snps, "noise_var": noise_var, "chi_scaled": chi_scaled}


def sample_effects(factor, right_side, noise_rows, chain_scale):
    whitened = jax.scipy.linalg.solve_triangular(factor, right_side.T, lower=True)
    moved = whitened + chain_scale * noise_rows.T
    return jax.scipy.linalg.solve_triangular(factor, moved, lower=True, trans=1).T

def reference(genotypes, residual, effects, noise, prior_var, block_snps, noise_var, chi_scaled):
    table_rows = block_snps.reshape(BLOCKS, BLOCK)
    chain_scale = jnp.sqrt(noise_var)[None, :]
    contract_rows = (((0,), (0,)), ((), ()))
    contract_cols = (((1,), (1,)), ((), ()))
    sampled_list = []
    for block_index in range(BLOCKS):
        genotype_block = genotypes[block_index]
        gram_matrix = lax.dot_general(genotype_block.astype(jnp.float32), genotype_block.astype(jnp.float32), contract_rows, preferred_element_type=jnp.float32)
        inverse_prior = 1.0 / jnp.take(prior_var, table_rows[block_index])
        factor = jnp.linalg.cholesky(gram_matrix + jnp.diag(inverse_prior))
        rounded = residual.astype(jnp.bfloat16)
        scores = jnp.dot(rounded.astype(jnp.float32), genotype_block.astype(jnp.float32), preferred_element_type=jnp.float32)
        previous = effects[block_index]
        right_side = scores + jnp.dot(previous, gram_matrix, precision=lax.Precision.HIGHEST)
        sampled = sample_effects(factor, right_side, noise[block_index], chain_scale)
        change = (sampled - previous).astype(jnp.bfloat16)
        residual = residual - lax.dot_general(change.astype(jnp.float32), genotype_block.astype(jnp.float32), contract_cols, preferred_element_type=jnp.float32)
        sampled_list.append(sampled)
    squares_sum = lax.optimization_barrier(jnp.sum(residual * residual, axis=1))
    variance_draw = squares_sum / (IND * chi_scaled)
    return (jnp.stack(sampled_list), residual, variance_draw)
```

```python
import jax
import jax.numpy as jnp
from jax import lax
from jax.experimental import pallas as pl
from jax.experimental.pallas import tpu as pltpu
from jax.sharding import PartitionSpec as P

F32 = jnp.float32
BF16 = jnp.bfloat16
TILE = 128
SUB = 8
STRIP = 256
NT = (((1,), (1,)), ((), ()))
NN = (((1,), (0,)), ((), ()))
TN = (((0,), (0,)), ((), ()))
VMEM = pl.BlockSpec(memory_space=pltpu.VMEM)
SMEM = pl.BlockSpec(memory_space=pltpu.SMEM)
ANY = pl.BlockSpec(memory_space=pl.ANY)
PARAMS = pltpu.CompilerParams(vmem_limit_bytes=52 * 2**20)


def dot_exact(left, right, dims):
    return lax.dot_general(
        left, right, dims, preferred_element_type=F32, precision=lax.Precision.HIGHEST
    )


def dot_bf16(left, right, dims):
    return lax.dot_general(left, right, dims, preferred_element_type=F32)


def tile_slot(row, col):
    return row * (row + 1) // 2 + col


def row_chunks(rows):
    return [(lo, min(lo + 1024, rows)) for lo in range(0, rows, 1024)]


def reciprocal(value):
    guess = pltpu.reciprocal(value, approx=True)
    guess = guess * (2.0 - value * guess)
    return guess * (2.0 - value * guess)


def spread(row):
    return jnp.broadcast_to(row, (SUB, TILE))


def inverse_factor(tile):
    groups = TILE // SUB
    sub = lax.broadcasted_iota(jnp.int32, (SUB, TILE), 0)
    lane = lax.broadcasted_iota(jnp.int32, (SUB, TILE), 1)
    left = [tile[SUB * r : SUB * r + SUB, :] for r in range(groups)]
    unit = [jnp.where(lane == sub + SUB * r, 1.0, 0.0).astype(F32) for r in range(groups)]
    done = []
    for g in range(groups):
        first = g * SUB
        cols = [[spread(left[r][:, first + j : first + j + 1]) for r in range(g, groups)] for j in range(SUB)]
        left_rows = [spread(left[g][j : j + 1, :]) for j in range(SUB)]
        unit_rows = [spread(unit[g][j : j + 1, :]) for j in range(SUB)]
        pivots = None
        finished = None
        for j in range(SUB):
            pivot = spread(cols[j][0][j : j + 1, :])
            inverse = reciprocal(pivot)
            for later in range(j + 1, SUB):
                share = spread(cols[later][0][j : j + 1, :]) * inverse
                for r in range(groups - g):
                    changed = cols[later][r] - cols[j][r] * share
                    cols[later][r] = jnp.where(sub > j, changed, cols[later][r]) if r == 0 else changed
                left_rows[later] = left_rows[later] - left_rows[j] * share
                unit_rows[later] = unit_rows[later] - unit_rows[j] * share
            pivots = pivot if j == 0 else jnp.where(sub == j, pivot, pivots)
            finished = unit_rows[j] if j == 0 else jnp.where(sub == j, unit_rows[j], finished)
            left_row = left_rows[j] * inverse
            unit_row = unit_rows[j] * inverse
            for r in range(1, groups - g):
                left[g + r] = left[g + r] - cols[j][r] * left_row
                unit[g + r] = unit[g + r] - cols[j][r] * unit_row
        root = lax.rsqrt(pivots)
        root = root * (1.5 - 0.5 * pivots * root * root)
        done.append(finished * root)
    return jnp.concatenate(done, axis=0)


def gram_kernel(core_ref, own_ref, other_ref, residual_ref, packed_ref, columns, total, sems):
    core = core_ref[0]
    rows, half = own_ref.shape[1:]
    chunks = row_chunks(rows)
    copies = []
    for i, (lo, hi) in enumerate(chunks):
        pair = []
        for k, (source, place) in enumerate(((own_ref, core), (other_ref, 1 - core))):
            at = pl.ds(pl.multiple_of(place * half, half), half)
            copy = pltpu.make_async_copy(source.at[core, lo:hi, :], columns.at[lo:hi, at], sems.at[i, k])
            copy.start()
            pair.append(copy)
        copies.append(pair)
    width = 2 * half
    base = packed_ref.shape[0]
    score = jnp.zeros((residual_ref.shape[0], width), F32)
    low_weight = core.astype(F32)
    for i, (lo, hi) in enumerate(chunks):
        for copy in copies[i]:
            copy.wait()
        values = residual_ref[:, lo:hi]
        high = values.astype(BF16)
        low = ((values - high.astype(F32)) * low_weight).astype(BF16)
        x = columns[lo:hi, :]
        score = score + (dot_bf16(high, x, NN) + dot_bf16(low, x, NN))
        for c in range(0, width, STRIP):
            part = dot_bf16(columns[lo:hi, c:], columns[lo:hi, c : c + STRIP], TN)
            if i == 0:
                total[c:, c : c + STRIP] = part
            else:
                total[c:, c : c + STRIP] = total[c:, c : c + STRIP] + part
    count = width // TILE
    for row in range(count):
        for col in range(row + 1):
            at = tile_slot(row, col) * TILE
            packed_ref[at : at + TILE, :] = total[row * TILE : row * TILE + TILE, col * TILE : col * TILE + TILE]
    at = tile_slot(count, 0) * TILE
    chains = residual_ref.shape[0]
    for col in range(count):
        packed_ref[at + col * chains : at + col * chains + chains, :] = score[:, col * TILE : col * TILE + TILE]
    end = at + count * chains
    packed_ref[end:, :] = jnp.zeros((base - end, TILE), F32)


def cross_kernel(core_ref, own_ref, other_ref, cross_ref, mine, theirs, second, sems):
    rows, half = own_ref.shape[1:]
    chunks = row_chunks(rows)
    copies = []
    for i, (lo, hi) in enumerate(chunks):
        trio = []
        for k, (source, place) in enumerate(((own_ref.at[0], mine), (other_ref.at[0], theirs), (own_ref.at[1], second))):
            copy = pltpu.make_async_copy(source.at[lo:hi, :], place.at[lo:hi, :], sems.at[i, k])
            copy.start()
            trio.append(copy)
        copies.append(trio)
    for i, (lo, hi) in enumerate(chunks):
        for copy in copies[i]:
            copy.wait()
        for k, place in enumerate((mine, theirs)):
            part = dot_bf16(place[lo:hi, :], second[lo:hi, :], TN)
            if i == 0:
                cross_ref[k] = part
            else:
                cross_ref[k] = cross_ref[k] + part


def backward(moved, factor_ref, inverse_ref, count):
    solved = [None] * count
    for k in reversed(range(count)):
        solved[k] = dot_exact(moved[k], inverse_ref[k], NN)
        if k:
            share = dot_exact(solved[k], factor_ref[k * TILE : k * TILE + TILE, : k * TILE], NN)
            for j in range(k):
                moved[j] = moved[j] - share[:, j * TILE : j * TILE + TILE]
    return solved


def factor_kernel(packed_ref, prior_ref, rows_ref, effects_ref, noise_ref, scale_ref, factor_ref, inverse_ref, shift_ref):
    width = factor_ref.shape[1]
    count = width // TILE
    chains = effects_ref.shape[0]
    table_rows = rows_ref[...]
    high = lax.shift_right_logical(table_rows, 7)
    low = lax.bitwise_and(table_rows, TILE - 1)
    prior = jnp.zeros((count, TILE), F32)
    for t in range(prior_ref.shape[0]):
        entry = jnp.broadcast_to(prior_ref[t : t + 1, :], (count, TILE))
        prior = jnp.where(high == t, jnp.take_along_axis(entry, low, axis=1), prior)
    inverse_prior = 1.0 / prior
    diagonal = lax.broadcasted_iota(jnp.int32, (TILE, TILE), 0) == lax.broadcasted_iota(jnp.int32, (TILE, TILE), 1)
    score_at = tile_slot(count, 0) * TILE
    for row in range(count):
        for col in range(row + 1):
            at = tile_slot(row, col) * TILE
            tile = packed_ref[at : at + TILE, :]
            if row == col:
                tile = tile + jnp.where(diagonal, inverse_prior[row : row + 1, :], 0.0)
            factor_ref[row * TILE : row * TILE + TILE, col * TILE : col * TILE + TILE] = tile
        at = score_at + row * chains
        cols = slice(row * TILE, row * TILE + TILE)
        factor_ref[width : width + chains, cols] = (
            packed_ref[at : at + chains, :] - inverse_prior[row : row + 1, :] * effects_ref[:, cols]
        )

    @pl.loop(0, count)
    def _(k):
        at = pl.multiple_of(k * TILE, TILE)
        inverse_ref[k] = inverse_factor(factor_ref[pl.ds(at, TILE), pl.ds(at, TILE)])
        for step in range(count):

            @pl.when(k == step)
            def _():
                lo = (step + 1) * TILE
                panel = dot_exact(factor_ref[lo:, step * TILE : lo], inverse_ref[step], NT)
                factor_ref[lo:, step * TILE : lo] = panel
                for c in range(lo, width, STRIP):
                    end = min(c + STRIP, width)
                    factor_ref[c:, c:end] = factor_ref[c:, c:end] - dot_exact(
                        panel[c - lo :, :], panel[c - lo : end - lo, :], NT
                    )

    scale = scale_ref[...]
    moved = [
        factor_ref[width : width + chains, j * TILE : j * TILE + TILE] + scale * noise_ref[:, j * TILE : j * TILE + TILE]
        for j in range(count)
    ]
    for j, part in enumerate(backward(moved, factor_ref, inverse_ref, count)):
        shift_ref[:, j * TILE : j * TILE + TILE] = part


def cross_share_kernel(core_ref, shift_ref, cross_ref, share_ref):
    core = core_ref[0]
    half = cross_ref.shape[1]
    change = shift_ref[...].astype(BF16).astype(F32)
    first, last = change[:, :half], change[:, half:]
    mine = jnp.where(core == 0, first, last)
    theirs = jnp.where(core == 0, last, first)
    share_ref[...] = dot_exact(mine, cross_ref[0], NN) + dot_exact(theirs, cross_ref[1], NN)


def second_kernel(core_ref, shift_ref, got_ref, cross_ref, factor_ref, inverse_ref, final_ref):
    width = factor_ref.shape[1]
    count = width // TILE
    half = cross_ref.shape[1]
    change = got_ref[:, :width].astype(BF16).astype(F32)
    share = dot_exact(change[:, half:], cross_ref[0], NN) + dot_exact(change[:, :half], cross_ref[1], NN)
    keep = jnp.where(core_ref[0] == 1, 1.0, 0.0)
    right = jnp.concatenate([got_ref[:, width:], share], axis=1) * keep
    moved = [right[:, j * TILE : j * TILE + TILE] for j in range(count)]
    for k in range(count):
        moved[k] = dot_exact(moved[k], inverse_ref[k], NT)
        lo = (k + 1) * TILE
        if lo < width:
            change_by = dot_exact(moved[k], factor_ref[lo:width, k * TILE : lo], NT)
            for j in range(k + 1, count):
                moved[j] = moved[j] - change_by[:, (j - k - 1) * TILE : (j - k) * TILE]
    for j, part in enumerate(backward(moved, factor_ref, inverse_ref, count)):
        cols = slice(j * TILE, j * TILE + TILE)
        final_ref[:, cols] = shift_ref[:, cols] - part


def update_kernel(own_ref, other_ref, change_ref, residual_ref, new_ref, squares_ref, x, sems):
    rows, half = own_ref.shape[1:]
    chunks = row_chunks(rows)
    copies = []
    for i, (lo, hi) in enumerate(chunks):
        group = []
        for b in range(2):
            for k, source in enumerate((own_ref, other_ref)):
                copy = pltpu.make_async_copy(source.at[b, lo:hi, :], x.at[2 * b + k, lo:hi, :], sems.at[i, 2 * b + k])
                copy.start()
                group.append(copy)
        copies.append(group)
    squares = jnp.zeros((residual_ref.shape[0], 1), F32)
    for i, (lo, hi) in enumerate(chunks):
        for copy in copies[i]:
            copy.wait()
        update = dot_bf16(change_ref[0], x[0, lo:hi, :], NT)
        for q in range(1, 4):
            update = update + dot_bf16(change_ref[q], x[q, lo:hi, :], NT)
        value = residual_ref[:, lo:hi] - update
        new_ref[:, lo:hi] = value
        squares = squares + jnp.sum(value * value, axis=1, keepdims=True)
    squares_ref[...] = jnp.broadcast_to(squares, squares_ref.shape)


def local(genotypes, residual, effects, noise, prior_var, block_snps, noise_var, chi_scaled):
    blocks, rows, half = genotypes.shape
    chains = residual.shape[0]
    width = 2 * half
    count = width // TILE
    spots = lax.axis_size("ind")
    core = lax.axis_index("snp")
    core_arg = jnp.reshape(core.astype(jnp.int32), (1,))
    swap = [(0, 1), (1, 0)]
    pieces = len(row_chunks(rows))

    other = lax.ppermute(genotypes, "snp", swap)
    other_effects = lax.ppermute(effects, "snp", swap)

    used = tile_slot(count, 0) * TILE + count * chains
    piece = -(-used // (spots * SUB)) * SUB
    packed = pl.pallas_call(
        gram_kernel,
        out_shape=jax.ShapeDtypeStruct((spots * piece, TILE), F32),
        in_specs=[SMEM, ANY, ANY, VMEM],
        out_specs=VMEM,
        scratch_shapes=[
            pltpu.VMEM((rows, width), BF16),
            pltpu.VMEM((width, width), F32),
            pltpu.SemaphoreType.DMA((pieces, 2)),
        ],
        compiler_params=PARAMS,
        cost_estimate=pl.CostEstimate(flops=rows * width * width * 5 // 4, bytes_accessed=2 * rows * width, transcendentals=0),
        name="gram",
    )(core_arg, genotypes, other, residual)
    cross = pl.pallas_call(
        cross_kernel,
        out_shape=jax.ShapeDtypeStruct((2, half, half), F32),
        in_specs=[SMEM, ANY, ANY],
        out_specs=VMEM,
        scratch_shapes=[
            pltpu.VMEM((rows, half), BF16),
            pltpu.VMEM((rows, half), BF16),
            pltpu.VMEM((rows, half), BF16),
            pltpu.SemaphoreType.DMA((pieces, 3)),
        ],
        compiler_params=PARAMS,
        cost_estimate=pl.CostEstimate(flops=rows * width * width, bytes_accessed=3 * rows * width, transcendentals=0),
        name="cross",
    )(core_arg, genotypes, other)
    cross = lax.psum(cross, "ind")

    packed = lax.all_to_all(packed.reshape(spots, piece, TILE), "ind", 0, 0)
    packed = jnp.sum(packed, axis=0)
    packed = lax.all_to_all(jnp.broadcast_to(packed[None], (spots, piece, TILE)), "ind", 0, 0)
    packed = packed.reshape(spots * piece, TILE)

    own_effects = lax.dynamic_index_in_dim(effects, core, 0, keepdims=False)
    got_effects = lax.dynamic_index_in_dim(other_effects, core, 0, keepdims=False)
    block_effects = jnp.where(
        core == 0,
        jnp.concatenate([own_effects, got_effects], axis=1),
        jnp.concatenate([got_effects, own_effects], axis=1),
    )
    block_noise = lax.dynamic_index_in_dim(noise, core, 0, keepdims=False)
    block_rows = lax.dynamic_index_in_dim(block_snps.reshape(blocks, count, TILE), core, 0, keepdims=False)
    scale = jnp.sqrt(noise_var)[:, None]
    factor, inverse, shift = pl.pallas_call(
        factor_kernel,
        out_shape=(
            jax.ShapeDtypeStruct((width + chains, width), F32),
            jax.ShapeDtypeStruct((count, TILE, TILE), F32),
            jax.ShapeDtypeStruct((chains, width), F32),
        ),
        in_specs=[VMEM] * 6,
        out_specs=(VMEM,) * 3,
        compiler_params=PARAMS,
        cost_estimate=pl.CostEstimate(flops=10 * width**3, bytes_accessed=8 * width**2, transcendentals=0),
        name="factor",
    )(packed, prior_var.reshape(-1, TILE), block_rows, block_effects, block_noise, scale)

    share = pl.pallas_call(
        cross_share_kernel,
        out_shape=jax.ShapeDtypeStruct((chains, half), F32),
        in_specs=[SMEM, VMEM, VMEM],
        out_specs=VMEM,
        compiler_params=PARAMS,
        name="cross_share",
    )(core_arg, shift, cross)
    got = lax.ppermute(jnp.concatenate([shift, share], axis=1), "snp", swap)
    final = pl.pallas_call(
        second_kernel,
        out_shape=jax.ShapeDtypeStruct((chains, width), F32),
        in_specs=[SMEM] + [VMEM] * 5,
        out_specs=VMEM,
        compiler_params=PARAMS,
        name="second",
    )(core_arg, shift, got, cross, factor, inverse)
    got_final = lax.ppermute(final, "snp", swap)
    shifts = jnp.where(core == 0, jnp.stack([final, got_final]), jnp.stack([got_final, final]))
    halves = shifts.reshape(blocks, chains, 2, half)
    own_shift = lax.dynamic_index_in_dim(halves, core, 2, keepdims=False)
    far_shift = lax.dynamic_index_in_dim(halves, 1 - core, 2, keepdims=False)
    change = jnp.stack([own_shift[0], far_shift[0], own_shift[1], far_shift[1]]).astype(BF16)

    new_residual, squares = pl.pallas_call(
        update_kernel,
        out_shape=(
            jax.ShapeDtypeStruct(residual.shape, F32),
            jax.ShapeDtypeStruct((chains, TILE), F32),
        ),
        in_specs=[ANY, ANY, VMEM, VMEM],
        out_specs=(VMEM, VMEM),
        scratch_shapes=[
            pltpu.VMEM((4, rows, half), BF16),
            pltpu.SemaphoreType.DMA((pieces, 4)),
        ],
        compiler_params=PARAMS,
        name="update",
    )(genotypes, other, change, residual)
    spread_squares = jnp.broadcast_to(squares[None, :, 0], (spots, chains))
    squares_sum = jnp.sum(lax.all_to_all(spread_squares, "ind", 0, 0, tiled=True), axis=0)
    variance_draw = squares_sum / (rows * spots * chi_scaled)
    return (effects + own_shift, new_residual, variance_draw)


def solution(mesh):
    placed = (P(None, "ind", "snp"), P(None, "ind"), P(None, None, "snp"), P(), P(), P(), P(), P())
    return jax.shard_map(
        local,
        mesh=mesh,
        in_specs=placed,
        out_specs=(P(None, None, "snp"), P(None, "ind"), P()),
        check_vma=False,
    )
```

```python
import jax
import jax.numpy as jnp
from jax import lax
from jax.experimental import pallas as pl
from jax.experimental.pallas import tpu as pltpu
from jax.sharding import PartitionSpec as P

F32 = jnp.float32
BF16 = jnp.bfloat16
TILE = 128
SUB = 8
STRIP = 256
CHUNK = 1024
LINE = 4
NT = (((1,), (1,)), ((), ()))
NN = (((1,), (0,)), ((), ()))
TN = (((0,), (0,)), ((), ()))
VMEM = pl.BlockSpec(memory_space=pltpu.VMEM)
SMEM = pl.BlockSpec(memory_space=pltpu.SMEM)
ANY = pl.BlockSpec(memory_space=pl.ANY)
PARAMS = pltpu.CompilerParams(vmem_limit_bytes=52 * 2**20)


def dot_exact(left, right, dims):
    return lax.dot_general(
        left, right, dims, preferred_element_type=F32, precision=lax.Precision.HIGHEST
    )


def dot_bf16(left, right, dims):
    return lax.dot_general(left, right, dims, preferred_element_type=F32)


def tile_slot(row, col):
    return row * (row + 1) // 2 + col


def row_chunks(rows):
    return [(lo, min(lo + 1024, rows)) for lo in range(0, rows, 1024)]


def spread(row):
    return jnp.broadcast_to(row, (SUB, TILE))


def inverse_factor(tile):
    groups = TILE // SUB
    sub = lax.broadcasted_iota(jnp.int32, (SUB, TILE), 0)
    lane = lax.broadcasted_iota(jnp.int32, (SUB, TILE), 1)
    left = [tile[SUB * r : SUB * r + SUB, :] for r in range(groups)]
    unit = [jnp.where(lane == sub + SUB * r, 1.0, 0.0).astype(F32) for r in range(groups)]
    done = []
    for g in range(groups):
        first = g * SUB
        cols = [[spread(left[r][:, first + j : first + j + 1]) for r in range(g, groups)] for j in range(SUB)]
        left_rows = [spread(left[g][j : j + 1, :]) for j in range(SUB)]
        unit_rows = [spread(unit[g][j : j + 1, :]) for j in range(SUB)]
        pivots = jnp.zeros((SUB, TILE), F32)
        finished = pivots
        for j in range(0, SUB, 2):
            p, q = spread(cols[j][0][j : j + 1, :]), spread(cols[j + 1][0][j : j + 1, :])
            r = spread(cols[j + 1][0][j + 1 : j + 2, :])
            minor = p * r - q * q
            over_minor = pltpu.reciprocal(minor, approx=True)
            over_p = pltpu.reciprocal(p, approx=True)
            ip, iq, ir = r * over_minor, -q * over_minor, p * over_minor
            pivots = jnp.where(sub == j, p, jnp.where(sub == j + 1, minor * over_p, pivots))
            second_row = unit_rows[j + 1] - (q * over_p) * unit_rows[j]
            finished = jnp.where(sub == j, unit_rows[j], jnp.where(sub == j + 1, second_row, finished))
            for later in range(j + 2, SUB):
                upper, lower = spread(cols[later][0][j : j + 1, :]), spread(cols[later][0][j + 1 : j + 2, :])
                one, two = upper * ip + lower * iq, upper * iq + lower * ir
                for r in range(groups - g):
                    changed = cols[later][r] - (cols[j][r] * one + cols[j + 1][r] * two)
                    cols[later][r] = jnp.where(sub > j + 1, changed, cols[later][r]) if r == 0 else changed
                left_rows[later] = left_rows[later] - (left_rows[j] * one + left_rows[j + 1] * two)
                unit_rows[later] = unit_rows[later] - (unit_rows[j] * one + unit_rows[j + 1] * two)
            left_one = left_rows[j] * ip + left_rows[j + 1] * iq
            left_two = left_rows[j] * iq + left_rows[j + 1] * ir
            unit_one = unit_rows[j] * ip + unit_rows[j + 1] * iq
            unit_two = unit_rows[j] * iq + unit_rows[j + 1] * ir
            for r in range(1, groups - g):
                left[g + r] = left[g + r] - (cols[j][r] * left_one + cols[j + 1][r] * left_two)
                unit[g + r] = unit[g + r] - (cols[j][r] * unit_one + cols[j + 1][r] * unit_two)
        root = lax.rsqrt(pivots)
        root = root * (1.5 - 0.5 * pivots * root * root)
        done.append(finished * root)
    return jnp.concatenate(done, axis=0)


def split_scores(residual, x, low_weight):
    high = residual.astype(BF16)
    low = ((residual - high.astype(F32)) * low_weight).astype(BF16)
    return dot_bf16(high, x, NN) + dot_bf16(low, x, NN)


def chunk_loop(rows, body):
    whole = rows // CHUNK

    @pl.loop(0, whole)
    def _(i):
        body(i, pl.multiple_of(i * CHUNK, CHUNK), CHUNK)

    if rows % CHUNK:
        body(whole, whole * CHUNK, rows % CHUNK)


def start_copies(sources, places, sems, rows):
    copies = []
    for i, lo in enumerate(range(0, rows, CHUNK)):
        at = pl.ds(lo, min(CHUNK, rows - lo))
        for k, (source, place) in enumerate(zip(sources, places)):
            pltpu.make_async_copy(source.at[at, :], place.at[at, :], sems.at[i, k]).start()


def wait_copies(sources, places, sems, i, start, size):
    at = pl.ds(start, size)
    for k, (source, place) in enumerate(zip(sources, places)):
        pltpu.make_async_copy(source.at[at, :], place.at[at, :], sems.at[i, k]).wait()


def own_kernel(core_ref, own_ref, residual_ref, square_ref, score_ref, cross_ref, mine, sems):
    core = core_ref[0]
    rows, half = own_ref.shape[1:]
    sources, places = [own_ref.at[0], own_ref.at[1]], [mine.at[0], mine.at[1]]
    start_copies(sources, places, sems, rows)
    low_weight = core.astype(F32)
    for ref in (square_ref, score_ref, cross_ref):
        ref[...] = jnp.zeros_like(ref)

    def body(i, start, size):
        wait_copies(sources, places, sems, i, start, size)
        at = pl.ds(start, size)
        score_ref[...] += split_scores(residual_ref[:, at], mine[core, at, :], low_weight)
        cross_ref[...] += dot_bf16(mine[0, at, :], mine[1, at, :], TN)
        for c in range(0, half, STRIP):
            square_ref[c:, c : c + STRIP] += dot_bf16(mine[core, at, c:], mine[core, at, c : c + STRIP], TN)

    chunk_loop(rows, body)


def put_tiles(packed_ref, row_at, col_at, tiles, lower_only):
    for r in range(tiles.shape[0] // TILE):
        for c in range(r + 1 if lower_only else tiles.shape[1] // TILE):
            row, col = row_at + r, col_at + c
            at = pl.multiple_of((lax.shift_right_logical(row * (row + 1), 1) + col) * TILE, TILE)
            packed_ref[pl.ds(at, TILE), :] = tiles[r * TILE : r * TILE + TILE, c * TILE : c * TILE + TILE]


def gram_kernel(
    core_ref, own_ref, other_ref, residual_ref, square_ref, own_score_ref, packed_ref, x, total, mixed, score, sems
):
    core = core_ref[0]
    rows, half = own_ref.shape[1:]
    sources, places = [own_ref.at[core], other_ref.at[core]], [x.at[core], x.at[1 - core]]
    start_copies(sources, places, sems, rows)
    low_weight = core.astype(F32)
    for ref in (total, mixed, score):
        ref[...] = jnp.zeros_like(ref)

    def body(i, start, size):
        wait_copies(sources, places, sems, i, start, size)
        at = pl.ds(start, size)
        mixed[...] += dot_bf16(x[1, at, :], x[0, at, :], TN)
        score[...] += split_scores(residual_ref[:, at], x[1 - core, at, :], low_weight)
        for c in range(0, half, STRIP):
            total[c:, c : c + STRIP] += dot_bf16(x[1 - core, at, c:], x[1 - core, at, c : c + STRIP], TN)

    chunk_loop(rows, body)
    count = 2 * half // TILE
    own_at = core * (count // 2)
    put_tiles(packed_ref, own_at, own_at, square_ref, True)
    put_tiles(packed_ref, count // 2 - own_at, count // 2 - own_at, total, True)
    put_tiles(packed_ref, count // 2, 0, mixed, False)
    at = tile_slot(count, 0) * TILE
    chains = residual_ref.shape[0]
    for k, part in ((core, own_score_ref), (1 - core, score)):
        for col in range(count // 2):
            start_row = pl.multiple_of(at + (k * (count // 2) + col) * chains, chains)
            packed_ref[pl.ds(start_row, chains), :] = part[:, col * TILE : col * TILE + TILE]
    end = at + count * chains
    packed_ref[end:, :] = jnp.zeros((packed_ref.shape[0] - end, TILE), F32)


def cross_kernel(own_ref, other_ref, own_cross_ref, cross_ref, x, sems):
    rows = own_ref.shape[1]
    sources, places = [other_ref.at[0], own_ref.at[1]], [x.at[0], x.at[1]]
    start_copies(sources, places, sems, rows)
    cross_ref[0] = own_cross_ref[...]
    cross_ref[1] = jnp.zeros(own_cross_ref.shape, F32)

    def body(i, start, size):
        wait_copies(sources, places, sems, i, start, size)
        at = pl.ds(start, size)
        cross_ref[1] += dot_bf16(x[0, at, :], x[1, at, :], TN)

    chunk_loop(rows, body)


def backward(moved, factor_ref, inverse_ref, count):
    solved = [None] * count
    for k in reversed(range(count)):
        solved[k] = dot_exact(moved[k], inverse_ref[k], NN)
        if k:
            share = dot_exact(solved[k], factor_ref[k * TILE : k * TILE + TILE, : k * TILE], NN)
            for j in range(k):
                moved[j] = moved[j] - share[:, j * TILE : j * TILE + TILE]
    return solved


def factor_kernel(packed_ref, prior_ref, rows_ref, effects_ref, noise_ref, scale_ref, factor_ref, inverse_ref, shift_ref):
    width = factor_ref.shape[1]
    count = width // TILE
    chains = effects_ref.shape[0]
    table_rows = rows_ref[...]
    high = lax.shift_right_logical(table_rows, 7)
    low = lax.bitwise_and(table_rows, TILE - 1)
    prior = jnp.zeros((count, TILE), F32)
    for t in range(prior_ref.shape[0]):
        entry = jnp.broadcast_to(prior_ref[t : t + 1, :], (count, TILE))
        prior = jnp.where(high == t, jnp.take_along_axis(entry, low, axis=1), prior)
    inverse_prior = 1.0 / prior
    diagonal = lax.broadcasted_iota(jnp.int32, (TILE, TILE), 0) == lax.broadcasted_iota(jnp.int32, (TILE, TILE), 1)
    score_at = tile_slot(count, 0) * TILE
    for row in range(count):
        for col in range(row + 1):
            at = tile_slot(row, col) * TILE
            tile = packed_ref[at : at + TILE, :]
            if row == col:
                tile = tile + jnp.where(diagonal, inverse_prior[row : row + 1, :], 0.0)
            factor_ref[row * TILE : row * TILE + TILE, col * TILE : col * TILE + TILE] = tile
        at = score_at + row * chains
        cols = slice(row * TILE, row * TILE + TILE)
        factor_ref[width : width + chains, cols] = (
            packed_ref[at : at + chains, :] - inverse_prior[row : row + 1, :] * effects_ref[:, cols]
        )

    @pl.loop(0, count)
    def _(k):
        at = pl.multiple_of(k * TILE, TILE)
        inverse_ref[k] = inverse_factor(factor_ref[pl.ds(at, TILE), pl.ds(at, TILE)])
        for step in range(count):

            @pl.when(k == step)
            def _():
                lo = (step + 1) * TILE
                panel = dot_exact(factor_ref[lo:, step * TILE : lo], inverse_ref[step], NT)
                factor_ref[lo:, step * TILE : lo] = panel
                for c in range(lo, width, STRIP):
                    end = min(c + STRIP, width)
                    factor_ref[c:, c:end] = factor_ref[c:, c:end] - dot_exact(
                        panel[c - lo :, :], panel[c - lo : end - lo, :], NT
                    )

    scale = scale_ref[...]
    moved = [
        factor_ref[width : width + chains, j * TILE : j * TILE + TILE] + scale * noise_ref[:, j * TILE : j * TILE + TILE]
        for j in range(count)
    ]
    for j, part in enumerate(backward(moved, factor_ref, inverse_ref, count)):
        shift_ref[:, j * TILE : j * TILE + TILE] = part


def cross_share_kernel(core_ref, shift_ref, got_ref, cross_ref, share_ref):
    core = core_ref[0]
    half = cross_ref.shape[1]
    shift = jnp.where(core == 0, shift_ref[...], got_ref[...])
    change = shift.astype(BF16).astype(F32)
    first, last = change[:, :half], change[:, half:]
    mine = jnp.where(core == 0, first, last)
    theirs = jnp.where(core == 0, last, first)
    share_ref[...] = dot_exact(mine, cross_ref[0], NN) + dot_exact(theirs, cross_ref[1], NN)


def second_kernel(core_ref, shift_ref, share_ref, got_ref, factor_ref, inverse_ref, final_ref):
    width = factor_ref.shape[1]
    count = width // TILE
    keep = jnp.where(core_ref[0] == 1, 1.0, 0.0)
    right = jnp.concatenate([got_ref[...], share_ref[...]], axis=1) * keep
    moved = [right[:, j * TILE : j * TILE + TILE] for j in range(count)]
    for k in range(count):
        moved[k] = dot_exact(moved[k], inverse_ref[k], NT)
        lo = (k + 1) * TILE
        if lo < width:
            change_by = dot_exact(moved[k], factor_ref[lo:width, k * TILE : lo], NT)
            for j in range(k + 1, count):
                moved[j] = moved[j] - change_by[:, (j - k - 1) * TILE : (j - k) * TILE]
    for j, part in enumerate(backward(moved, factor_ref, inverse_ref, count)):
        cols = slice(j * TILE, j * TILE + TILE)
        final_ref[:, cols] = shift_ref[:, cols] - part


def update_kernel(own_ref, other_ref, change_ref, residual_ref, new_ref, squares_ref, x, sems):
    rows, half = own_ref.shape[1:]
    chunks = row_chunks(rows)
    copies = []
    for i, (lo, hi) in enumerate(chunks):
        group = []
        for b in range(2):
            for k, source in enumerate((own_ref, other_ref)):
                copy = pltpu.make_async_copy(source.at[b, lo:hi, :], x.at[2 * b + k, lo:hi, :], sems.at[i, 2 * b + k])
                copy.start()
                group.append(copy)
        copies.append(group)
    squares = jnp.zeros((residual_ref.shape[0], 1), F32)
    for i, (lo, hi) in enumerate(chunks):
        for copy in copies[i]:
            copy.wait()
        update = dot_bf16(change_ref[0], x[0, lo:hi, :], NT)
        for q in range(1, 4):
            update = update + dot_bf16(change_ref[q], x[q, lo:hi, :], NT)
        value = residual_ref[:, lo:hi] - update
        new_ref[:, lo:hi] = value
        squares = squares + jnp.sum(value * value, axis=1, keepdims=True)
    squares_ref[...] = jnp.broadcast_to(squares, squares_ref.shape)


def line_sums(value, spots):
    stride = 1
    while stride < spots:
        moves = []
        for step in range(1, LINE):
            ends = [(i, i // stride % LINE) for i in range(spots)]
            moves.append([(i, i + ((at + step) % LINE - at) * stride) for i, at in ends])
        value = value + sum([lax.ppermute(value, "ind", move) for move in moves])
        stride *= LINE
    return value


def local(genotypes, residual, effects, noise, prior_var, block_snps, noise_var, chi_scaled):
    blocks, rows, half = genotypes.shape
    chains = residual.shape[0]
    width = 2 * half
    count = width // TILE
    spots = lax.axis_size("ind")
    core = lax.axis_index("snp")
    core_arg = jnp.reshape(core.astype(jnp.int32), (1,))
    swap = [(0, 1), (1, 0)]
    pieces = len(row_chunks(rows))

    other = lax.ppermute(genotypes, "snp", swap)
    other_effects = lax.ppermute(effects, "snp", swap)

    used = tile_slot(count, 0) * TILE + count * chains
    piece = -(-used // (spots * SUB)) * SUB
    square, own_score, own_cross = pl.pallas_call(
        own_kernel,
        out_shape=(
            jax.ShapeDtypeStruct((half, half), F32),
            jax.ShapeDtypeStruct((chains, half), F32),
            jax.ShapeDtypeStruct((half, half), F32),
        ),
        in_specs=[SMEM, ANY, VMEM],
        out_specs=(VMEM,) * 3,
        scratch_shapes=[pltpu.VMEM((2, rows, half), BF16), pltpu.SemaphoreType.DMA((pieces, 2))],
        compiler_params=PARAMS,
        cost_estimate=pl.CostEstimate(flops=2 * rows * half * half, bytes_accessed=2 * rows * half, transcendentals=0),
        name="own",
    )(core_arg, genotypes, residual)
    packed = pl.pallas_call(
        gram_kernel,
        out_shape=jax.ShapeDtypeStruct((spots * piece, TILE), F32),
        in_specs=[SMEM, ANY, ANY, VMEM, VMEM, VMEM],
        out_specs=VMEM,
        scratch_shapes=[
            pltpu.VMEM((2, rows, half), BF16),
            pltpu.VMEM((half, half), F32),
            pltpu.VMEM((half, half), F32),
            pltpu.VMEM((chains, half), F32),
            pltpu.SemaphoreType.DMA((pieces, 2)),
        ],
        compiler_params=PARAMS,
        cost_estimate=pl.CostEstimate(flops=0, bytes_accessed=0, transcendentals=0),
        name="gram",
    )(core_arg, genotypes, other, residual, square, own_score)
    late_other, packed = lax.optimization_barrier((other, packed))
    cross = pl.pallas_call(
        cross_kernel,
        out_shape=jax.ShapeDtypeStruct((2, half, half), F32),
        in_specs=[ANY, ANY, VMEM],
        out_specs=VMEM,
        scratch_shapes=[
            pltpu.VMEM((2, rows, half), BF16),
            pltpu.SemaphoreType.DMA((pieces, 2)),
        ],
        compiler_params=PARAMS,
        cost_estimate=pl.CostEstimate(flops=2 * rows * half * half, bytes_accessed=4 * rows * half, transcendentals=0),
        name="cross",
    )(genotypes, late_other, own_cross)
    packed = lax.all_to_all(packed.reshape(spots, piece, TILE), "ind", 0, 0)
    packed, cross = lax.optimization_barrier((packed, cross))
    packed = jnp.broadcast_to(jnp.sum(packed, axis=0)[None], (spots, piece, TILE))
    packed = lax.all_to_all(packed, "ind", 0, 0).reshape(spots * piece, TILE)

    own_effects = lax.dynamic_index_in_dim(effects, core, 0, keepdims=False)
    got_effects = lax.dynamic_index_in_dim(other_effects, core, 0, keepdims=False)
    block_effects = jnp.where(
        core == 0,
        jnp.concatenate([own_effects, got_effects], axis=1),
        jnp.concatenate([got_effects, own_effects], axis=1),
    )
    block_noise = lax.dynamic_index_in_dim(noise, core, 0, keepdims=False)
    block_rows = lax.dynamic_index_in_dim(block_snps.reshape(blocks, count, TILE), core, 0, keepdims=False)
    scale = jnp.sqrt(noise_var)[:, None]
    factor, inverse, shift = pl.pallas_call(
        factor_kernel,
        out_shape=(
            jax.ShapeDtypeStruct((width + chains, width), F32),
            jax.ShapeDtypeStruct((count, TILE, TILE), F32),
            jax.ShapeDtypeStruct((chains, width), F32),
        ),
        in_specs=[VMEM] * 6,
        out_specs=(VMEM,) * 3,
        compiler_params=PARAMS,
        cost_estimate=pl.CostEstimate(flops=0, bytes_accessed=0, transcendentals=0),
        name="factor",
    )(packed, prior_var.reshape(-1, TILE), block_rows, block_effects, block_noise, scale)

    got_shift = lax.ppermute(shift, "snp", swap)
    share = pl.pallas_call(
        cross_share_kernel,
        out_shape=jax.ShapeDtypeStruct((chains, half), F32),
        in_specs=[SMEM] + [VMEM] * 3,
        out_specs=VMEM,
        compiler_params=PARAMS,
        name="cross_share",
    )(core_arg, shift, got_shift, cross)
    share = line_sums(share, spots)
    got = lax.ppermute(share, "snp", swap)
    final = pl.pallas_call(
        second_kernel,
        out_shape=jax.ShapeDtypeStruct((chains, width), F32),
        in_specs=[SMEM] + [VMEM] * 5,
        out_specs=VMEM,
        compiler_params=PARAMS,
        name="second",
    )(core_arg, shift, share, got, factor, inverse)
    got_final = lax.ppermute(final, "snp", swap)
    shifts = jnp.where(core == 0, jnp.stack([final, got_final]), jnp.stack([got_final, final]))
    halves = shifts.reshape(blocks, chains, 2, half)
    own_shift = lax.dynamic_index_in_dim(halves, core, 2, keepdims=False)
    far_shift = lax.dynamic_index_in_dim(halves, 1 - core, 2, keepdims=False)
    change = jnp.stack([own_shift[0], far_shift[0], own_shift[1], far_shift[1]]).astype(BF16)

    new_residual, squares = pl.pallas_call(
        update_kernel,
        out_shape=(
            jax.ShapeDtypeStruct(residual.shape, F32),
            jax.ShapeDtypeStruct((chains, TILE), F32),
        ),
        in_specs=[ANY, ANY, VMEM, VMEM],
        out_specs=(VMEM, VMEM),
        scratch_shapes=[
            pltpu.VMEM((4, rows, half), BF16),
            pltpu.SemaphoreType.DMA((pieces, 4)),
        ],
        compiler_params=PARAMS,
        name="update",
    )(genotypes, other, change, residual)
    spread_squares = jnp.broadcast_to(squares[None, :, 0], (spots, chains))
    squares_sum = jnp.sum(lax.all_to_all(spread_squares, "ind", 0, 0, tiled=True), axis=0)
    variance_draw = squares_sum / (rows * spots * chi_scaled)
    return (effects + own_shift, new_residual, variance_draw)


def solution(mesh):
    placed = (P(None, "ind", "snp"), P(None, "ind"), P(None, None, "snp"), P(), P(), P(), P(), P())
    return jax.shard_map(
        local,
        mesh=mesh,
        in_specs=placed,
        out_specs=(P(None, None, "snp"), P(None, "ind"), P()),
        check_vma=False,
    )
```

```python
import functools

import jax
import jax.numpy as jnp
from jax import lax
from jax.experimental import pallas as pl
from jax.experimental.pallas import tpu as pltpu
from jax.sharding import PartitionSpec as P

F32 = jnp.float32
BF16 = jnp.bfloat16
TILE = 128
SUB = 8
STRIP = 256
CHUNK = 1024
LINE = 4
NT = (((1,), (1,)), ((), ()))
NN = (((1,), (0,)), ((), ()))
TN = (((0,), (0,)), ((), ()))
VMEM = pl.BlockSpec(memory_space=pltpu.VMEM)
SMEM = pl.BlockSpec(memory_space=pltpu.SMEM)
ANY = pl.BlockSpec(memory_space=pl.ANY)
PARAMS = pltpu.CompilerParams(vmem_limit_bytes=52 * 2**20)


def dot_exact(left, right, dims):
    return lax.dot_general(
        left, right, dims, preferred_element_type=F32, precision=lax.Precision.HIGHEST
    )


def dot_bf16(left, right, dims):
    return lax.dot_general(left, right, dims, preferred_element_type=F32)


def spread(row):
    return jnp.broadcast_to(row, (SUB, TILE))


def pieces_of(value):
    high = value.astype(BF16)
    rest = value - high.astype(F32)
    middle = rest.astype(BF16)
    return high, middle, (rest - middle.astype(F32)).astype(BF16)


def dot_rows(left, right, dims):
    rows = left.shape[0]
    parts = pieces_of(left)
    high, middle, low = pieces_of(right)
    one = dot_bf16(jnp.concatenate(parts, axis=0), high, dims)
    two = dot_bf16(jnp.concatenate(parts[:2], axis=0), middle, dims)
    three = dot_bf16(parts[0], low, dims)
    return one[:rows] + ((one[rows : 2 * rows] + two[:rows]) + (one[2 * rows :] + two[rows:] + three))


def tree_sum(terms):
    while len(terms) > 1:
        terms = [terms[i] + terms[i + 1] if i + 1 < len(terms) else terms[i] for i in range(0, len(terms), 2)]
    return terms[0]


def inverse_factor(tile, zero):
    groups = TILE // SUB
    sub = lax.broadcasted_iota(jnp.int32, (SUB, TILE), 0)
    lane = lax.broadcasted_iota(jnp.int32, (SUB, TILE), 1)
    left = [tile[SUB * r : SUB * r + SUB, :] for r in range(groups)]
    done = []
    for g in range(groups):
        first = g * SUB
        inside = (lane >= first) & (lane < first + SUB)
        pivot_cols = [spread(left[g][:, first + j : first + j + 1]) + zero for j in range(SUB)]
        cols = [[spread(left[r][:, first + j : first + j + 1]) for r in range(g + 1, groups)] for j in range(SUB)]
        square = {(i, j): spread(pivot_cols[j][i : i + 1, :]) for j in range(SUB) for i in range(j + 1)}
        own = jnp.where(inside, jnp.where(lane == sub + first, 1.0, 0.0), left[g])
        rows = [spread(own[j : j + 1, :]) for j in range(SUB)]
        last = g + 1 == groups
        near = None if last else [cols[j][0] for j in range(SUB)]
        near_terms = []
        share = {}
        solved = [None] * SUB
        pivots = jnp.zeros((SUB, TILE), F32)
        finished = pivots
        for j in range(0, SUB, 2):
            p, q, r = square[j, j], square[j, j + 1], square[j + 1, j + 1]
            minor = p * r - q * q
            over_minor = pltpu.reciprocal(minor, approx=True)
            over_p = pltpu.reciprocal(p, approx=True)
            ip, iq, ir = r * over_minor, -q * over_minor, p * over_minor
            pivots = jnp.where(sub == j, p, jnp.where(sub == j + 1, minor * over_p, pivots))
            second_row = rows[j + 1] - (q * over_p) * rows[j]
            finished = jnp.where(sub == j, rows[j], jnp.where(sub == j + 1, second_row, finished))
            for k in range(j + 2, SUB):
                upper, lower = square[j, k], square[j + 1, k]
                share[j, k], share[j + 1, k] = upper * ip + lower * iq, upper * iq + lower * ir
            for k in range(j + 2, SUB):
                one, two = share[j, k], share[j + 1, k]
                for i in range(j + 2, k + 1):
                    square[i, k] = square[i, k] - (square[j, i] * one + square[j + 1, i] * two)
                rows[k] = rows[k] - (rows[j] * one + rows[j + 1] * two)
                if not last:
                    near[k] = near[k] - (near[j] * one + near[j + 1] * two)
            solved[j], solved[j + 1] = rows[j] * ip + rows[j + 1] * iq, rows[j] * iq + rows[j + 1] * ir
            if not last:
                near_terms.append(near[j] * solved[j] + near[j + 1] * solved[j + 1])
        if not last:
            left[g + 1] = jnp.where(inside, 0.0, left[g + 1]) - tree_sum(near_terms)
        for j in (4, 5, 2, 3, 0, 1):
            solved[j] = solved[j] - tree_sum([share[j, k] * solved[k] for k in range(j // 2 * 2 + 2, SUB)])
        for r in range(g + 2, groups):
            left[r] = jnp.where(inside, 0.0, left[r]) - tree_sum([cols[j][r - g - 1] * solved[j] for j in range(SUB)])
        root = lax.rsqrt(pivots)
        root = root * (1.5 - 0.5 * pivots * root * root)
        done.append(jnp.where(lane < first + SUB, finished * root, 0.0))
    return jnp.concatenate(done, axis=0)


def split_scores(residual, x):
    high, middle, _ = pieces_of(residual)
    return dot_bf16(high, x, NN) + dot_bf16(middle, x, NN)


def chunk_loop(rows, body):
    whole = rows // CHUNK

    @pl.loop(0, whole)
    def _(i):
        body(i, pl.multiple_of(i * CHUNK, CHUNK), CHUNK)

    if rows % CHUNK:
        body(whole, whole * CHUNK, rows % CHUNK)


def start_copies(sources, places, sems, rows):
    copies = []
    for i, lo in enumerate(range(0, rows, CHUNK)):
        at = pl.ds(lo, min(CHUNK, rows - lo))
        for k, (source, place) in enumerate(zip(sources, places)):
            pltpu.make_async_copy(source.at[at, :], place.at[at, :], sems.at[i, k]).start()


def wait_copies(sources, places, sems, i, start, size):
    at = pl.ds(start, size)
    for k, (source, place) in enumerate(zip(sources, places)):
        pltpu.make_async_copy(source.at[at, :], place.at[at, :], sems.at[i, k]).wait()


def own_kernel(core_ref, own_ref, residual_ref, square_ref, score_ref, cross_ref, mine, sems):
    core = core_ref[0]
    rows, half = own_ref.shape[1:]
    sources, places = [own_ref.at[0], own_ref.at[1]], [mine.at[0], mine.at[1]]
    start_copies(sources, places, sems, rows)
    for ref in (square_ref, score_ref, cross_ref):
        ref[...] = jnp.zeros_like(ref)

    def body(i, start, size):
        wait_copies(sources, places, sems, i, start, size)
        at = pl.ds(start, size)
        score_ref[...] += split_scores(residual_ref[:, at], mine[core, at, :])
        cross_ref[...] += dot_bf16(mine[0, at, :], mine[1, at, :], TN)
        for c in range(0, half, STRIP):
            square_ref[c:, c : c + STRIP] += dot_bf16(mine[core, at, c:], mine[core, at, c : c + STRIP], TN)

    chunk_loop(rows, body)


class Layout:
    def __init__(self, count, chains, spots):
        self.count, self.chains = count, chains
        self.pairs = count * (count - 1) // 2 * TILE
        self.diagonals = self.pairs + count // 2 * TILE
        self.scores = self.diagonals + SUB
        self.squares = self.scores + count * chains
        self.used = self.squares + chains
        self.piece = -(-self.used // (spots * SUB)) * SUB
        self.rows = self.piece * spots

    def lower(self, row, col):
        return (row * (row - 1) // 2 + col) * TILE


def put_diagonal(packed_ref, layout, half_at, block):
    count = layout.count // 2
    row_id = lax.broadcasted_iota(jnp.int32, (TILE, TILE), 0)
    col_id = lax.broadcasted_iota(jnp.int32, (TILE, TILE), 1)
    for r in range(count):
        for c in range(r):
            row, col = half_at * count + r, half_at * count + c
            at = pl.multiple_of((lax.shift_right_logical(row * (row - 1), 1) + col) * TILE, TILE)
            packed_ref[pl.ds(at, TILE), :] = block[r * TILE : r * TILE + TILE, c * TILE : c * TILE + TILE]
    for r in range(0, count, 2):
        one = block[r * TILE : r * TILE + TILE, r * TILE : r * TILE + TILE]
        two = block[(r + 1) * TILE : (r + 2) * TILE, (r + 1) * TILE : (r + 2) * TILE]
        place = half_at * (count // 2) + r // 2
        at = pl.multiple_of(layout.pairs + place * TILE, TILE)
        packed_ref[pl.ds(at, TILE), :] = jnp.where(row_id > col_id, one, two)
        packed_ref[pl.ds(layout.diagonals + place, 1), :] = jnp.sum(
            jnp.where(row_id == col_id, one, 0.0), axis=0, keepdims=True
        )


def get_diagonal(packed_ref, layout, tile):
    row_id = lax.broadcasted_iota(jnp.int32, (TILE, TILE), 0)
    col_id = lax.broadcasted_iota(jnp.int32, (TILE, TILE), 1)
    at = layout.pairs + tile // 2 * TILE
    pair = packed_ref[at : at + TILE, :]
    if tile % 2:
        return jnp.where(row_id < col_id, pair, 0.0), jnp.where(row_id == col_id, pair, 0.0)
    row = layout.diagonals + tile // 2
    return jnp.where(row_id > col_id, pair, 0.0), jnp.where(row_id == col_id, packed_ref[row : row + 1, :], 0.0)


def gram_kernel(
    layout, core_ref, own_ref, other_ref, residual_ref, square_ref, own_score_ref, packed_ref, x, total, score, norm, sems
):
    core = core_ref[0]
    rows, half = own_ref.shape[1:]
    sources = [own_ref.at[core], other_ref.at[core]]
    places = [x.at[:, :half], x.at[:, half:]]
    start_copies(sources, places, sems, rows)
    for ref in (total, score, norm):
        ref[...] = jnp.zeros_like(ref)

    def body(i, start, size):
        wait_copies(sources, places, sems, i, start, size)
        at = pl.ds(start, size)
        total[...] += dot_bf16(x[at, half:], x[at, :], TN)
        score[...] += split_scores(residual_ref[:, at], x[at, half:])
        norm[...] += jnp.sum(jnp.square(residual_ref[:, at]), axis=1, keepdims=True)

    chunk_loop(rows, body)
    count, chains = layout.count, layout.chains
    put_diagonal(packed_ref, layout, core, square_ref)
    put_diagonal(packed_ref, layout, 1 - core, total.at[:, half:])
    for r in range(count // 2):
        for c in range(count // 2):
            at = layout.lower(count // 2 + r, c)

            @pl.when(core == 0)
            def _():
                packed_ref[at : at + TILE, :] = total[r * TILE : r * TILE + TILE, c * TILE : c * TILE + TILE]

            @pl.when(core == 1)
            def _():
                packed_ref[at : at + TILE, :] = total[c * TILE : c * TILE + TILE, r * TILE : r * TILE + TILE].T

    for k, part in ((core, own_score_ref), (1 - core, score)):
        for col in range(count // 2):
            start_row = pl.multiple_of(layout.scores + (k * (count // 2) + col) * chains, SUB)
            packed_ref[pl.ds(start_row, chains), :] = part[:, col * TILE : col * TILE + TILE]
    packed_ref[layout.squares : layout.used, :] = jnp.broadcast_to(norm[...], (chains, TILE))
    packed_ref[layout.used :, :] = jnp.zeros((layout.rows - layout.used, TILE), F32)


def cross_kernel(own_ref, other_ref, own_cross_ref, cross_ref, x, sems):
    rows = own_ref.shape[1]
    sources, places = [other_ref.at[0], own_ref.at[1]], [x.at[0], x.at[1]]
    start_copies(sources, places, sems, rows)
    cross_ref[0] = own_cross_ref[...]
    cross_ref[1] = jnp.zeros(own_cross_ref.shape, F32)

    def body(i, start, size):
        wait_copies(sources, places, sems, i, start, size)
        at = pl.ds(start, size)
        cross_ref[1] += dot_bf16(x[0, at, :], x[1, at, :], TN)

    chunk_loop(rows, body)


def backward(moved, factor_ref, inverse_ref, count):
    solved = [None] * count
    for k in reversed(range(count)):
        solved[k] = dot_rows(moved[k], inverse_ref[k], NN)
        if k:
            share = dot_rows(solved[k], factor_ref[k * TILE : k * TILE + TILE, : k * TILE], NN)
            for j in range(k):
                moved[j] = moved[j] - share[:, j * TILE : j * TILE + TILE]
    return solved


def factor_kernel(
    layout, packed_ref, prior_ref, rows_ref, effects_ref, noise_ref, scale_ref, factor_ref, inverse_ref, shift_ref, zero_ref
):
    width = factor_ref.shape[1]
    count = width // TILE
    chains = effects_ref.shape[0]
    table_rows = rows_ref[...]
    high = lax.shift_right_logical(table_rows, 7)
    low = lax.bitwise_and(table_rows, TILE - 1)
    prior = jnp.zeros((count, TILE), F32)
    for t in range(prior_ref.shape[0]):
        entry = jnp.broadcast_to(prior_ref[t : t + 1, :], (count, TILE))
        prior = jnp.where(high == t, jnp.take_along_axis(entry, low, axis=1), prior)
    inverse_prior = 1.0 / prior
    diagonal = lax.broadcasted_iota(jnp.int32, (TILE, TILE), 0) == lax.broadcasted_iota(jnp.int32, (TILE, TILE), 1)
    for row in range(count):
        rows = slice(row * TILE, row * TILE + TILE)
        for col in range(row):
            at = layout.lower(row, col)
            factor_ref[rows, col * TILE : col * TILE + TILE] = packed_ref[at : at + TILE, :]
        triangle, middle = get_diagonal(packed_ref, layout, row)
        middle = middle + jnp.where(diagonal, inverse_prior[row : row + 1, :], 0.0)
        factor_ref[rows, rows] = triangle + triangle.T + middle
        at = layout.scores + row * chains
        factor_ref[width : width + chains, rows] = (
            packed_ref[at : at + chains, :] - inverse_prior[row : row + 1, :] * effects_ref[:, rows]
        )
    zero_ref[...] = jnp.zeros_like(zero_ref)

    @pl.loop(0, count)
    def _(k):
        at = pl.multiple_of(k * TILE, TILE)
        inverse_ref[k] = inverse_factor(factor_ref[pl.ds(at, TILE), pl.ds(at, TILE)], zero_ref[...])
        for step in range(count):

            @pl.when(k == step)
            def _():
                lo = (step + 1) * TILE
                factor_ref[lo:, step * TILE : lo] = dot_exact(factor_ref[lo:, step * TILE : lo], inverse_ref[step], NT)
                if step % 2 == 0:
                    panel = factor_ref[lo:, step * TILE : lo]
                    factor_ref[lo:, lo : lo + TILE] = factor_ref[lo:, lo : lo + TILE] - dot_exact(panel, panel[:TILE, :], NT)
                else:
                    for c in range(lo, width, STRIP):
                        end = min(c + STRIP, width)
                        panel = factor_ref[c:, (step - 1) * TILE : lo]
                        factor_ref[c:, c:end] = factor_ref[c:, c:end] - dot_exact(panel, panel[: end - c, :], NT)

    scale = scale_ref[...]
    moved = [
        factor_ref[width : width + chains, j * TILE : j * TILE + TILE] + scale * noise_ref[:, j * TILE : j * TILE + TILE]
        for j in range(count)
    ]
    for j, part in enumerate(backward(moved, factor_ref, inverse_ref, count)):
        shift_ref[:, j * TILE : j * TILE + TILE] = part


def cross_share_kernel(core_ref, shift_ref, got_ref, cross_ref, share_ref):
    core = core_ref[0]
    half = cross_ref.shape[1]
    shift = jnp.where(core == 0, shift_ref[...], got_ref[...])
    change = shift.astype(BF16)
    first, last = change[:, :half], change[:, half:]
    mine = jnp.where(core == 0, first, last)
    theirs = jnp.where(core == 0, last, first)
    share_ref[...] = sum(
        dot_bf16(change, part, NN) for change, ref in ((mine, cross_ref[0]), (theirs, cross_ref[1])) for part in pieces_of(ref)
    )


def second_kernel(core_ref, shift_ref, share_ref, got_ref, factor_ref, inverse_ref, final_ref, share_all_ref):
    width = factor_ref.shape[1]
    count = width // TILE
    keep = jnp.where(core_ref[0] == 1, 1.0, 0.0)
    right = jnp.concatenate([got_ref[...], share_ref[...]], axis=1) * keep
    share_all_ref[...] = right
    moved = [right[:, j * TILE : j * TILE + TILE] for j in range(count)]
    for k in range(count):
        moved[k] = dot_rows(moved[k], inverse_ref[k], NT)
        lo = (k + 1) * TILE
        if lo < width:
            change_by = dot_rows(moved[k], factor_ref[lo:width, k * TILE : lo], NT)
            for j in range(k + 1, count):
                moved[j] = moved[j] - change_by[:, (j - k - 1) * TILE : (j - k) * TILE]
    for j, part in enumerate(backward(moved, factor_ref, inverse_ref, count)):
        cols = slice(j * TILE, j * TILE + TILE)
        final_ref[:, cols] = shift_ref[:, cols] - part


def squares_kernel(layout, final_ref, share_ref, packed_ref, squares_ref):
    count, chains = layout.count, layout.chains
    change = final_ref[...].astype(BF16)
    value = change.astype(F32)
    total = jnp.zeros((chains, TILE), F32)
    for row in range(count):
        cols = slice(row * TILE, row * TILE + TILE)
        triangle, middle = get_diagonal(packed_ref, layout, row)
        tiles = [packed_ref[layout.lower(row, col) : layout.lower(row, col) + TILE, :] for col in range(row)]
        strip = jnp.concatenate([tile + tile for tile in tiles] + [triangle + triangle + middle], axis=1)
        product = sum(dot_bf16(change[:, : (row + 1) * TILE], part, NT) for part in pieces_of(strip))
        at = layout.scores + row * chains
        score = packed_ref[at : at + chains, :] - share_ref[:, cols]
        total = total + value[:, cols] * (product - (score + score))
    squares_ref[...] = jnp.broadcast_to(jnp.sum(total, axis=1, keepdims=True), (chains, TILE))


def update_kernel(block, own_ref, other_ref, change_ref, residual_ref, new_ref, x, sems):
    rows = own_ref.shape[1]
    sources, places = [own_ref.at[block], other_ref.at[block]], [x.at[0], x.at[1]]
    start_copies(sources, places, sems, rows)
    for i, start in enumerate(range(0, rows, CHUNK)):
        size = min(CHUNK, rows - start)
        wait_copies(sources, places, sems, i, start, size)
        at = pl.ds(start, size)
        update = dot_bf16(change_ref[0], x[0, at, :], NT) + dot_bf16(change_ref[1], x[1, at, :], NT)
        new_ref[:, at] = residual_ref[:, at] - update


def update(block, genotypes, other, change, residual):
    rows, half = genotypes.shape[1:]
    return pl.pallas_call(
        functools.partial(update_kernel, block),
        out_shape=jax.ShapeDtypeStruct(residual.shape, F32),
        in_specs=[ANY, ANY, VMEM, VMEM],
        out_specs=VMEM,
        scratch_shapes=[
            pltpu.VMEM((2, rows, half), BF16),
            pltpu.SemaphoreType.DMA((-(-rows // CHUNK), 2)),
        ],
        compiler_params=PARAMS,
        cost_estimate=pl.CostEstimate(flops=64 * rows * half * 8, bytes_accessed=4 * rows * half, transcendentals=0),
        name="update",
    )(genotypes, other, change, residual)


def halves_of(shift, core, half):
    change = shift.astype(BF16)
    first, last = change[:, :half], change[:, half:]
    return jnp.where(core == 0, jnp.stack([first, last]), jnp.stack([last, first]))


def line_sums(value, beside, spots):
    stride = 1
    while stride < spots:
        at = [i // stride % LINE for i in range(spots)]
        one, two, three = (
            lax.ppermute(value, "ind", [(i, i + ((at[i] + step) % LINE - at[i]) * stride) for i in range(spots)])
            for step in range(1, LINE)
        )
        if stride == 1:
            one, two, three, beside = lax.optimization_barrier((one, two, three, beside))
        even = lax.axis_index("ind") // stride % 2 == 0
        value = (value + jnp.where(even, three, one)) + (two + jnp.where(even, one, three))
        stride *= LINE
    return value, beside


def local(genotypes, residual, effects, noise, prior_var, block_snps, noise_var, chi_scaled):
    blocks, rows, half = genotypes.shape
    chains = residual.shape[0]
    width = 2 * half
    count = width // TILE
    spots = lax.axis_size("ind")
    core = lax.axis_index("snp")
    core_arg = jnp.reshape(core.astype(jnp.int32), (1,))
    swap = [(0, 1), (1, 0)]
    pieces = -(-rows // CHUNK)

    other = lax.ppermute(genotypes, "snp", swap)
    other_effects = lax.ppermute(effects, "snp", swap)

    layout = Layout(count, chains, spots)
    piece = layout.piece
    square, own_score, own_cross = pl.pallas_call(
        own_kernel,
        out_shape=(
            jax.ShapeDtypeStruct((half, half), F32),
            jax.ShapeDtypeStruct((chains, half), F32),
            jax.ShapeDtypeStruct((half, half), F32),
        ),
        in_specs=[SMEM, ANY, VMEM],
        out_specs=(VMEM,) * 3,
        scratch_shapes=[pltpu.VMEM((2, rows, half), BF16), pltpu.SemaphoreType.DMA((pieces, 2))],
        compiler_params=PARAMS,
        cost_estimate=pl.CostEstimate(flops=2 * rows * half * half, bytes_accessed=2 * rows * half, transcendentals=0),
        name="own",
    )(core_arg, genotypes, residual)
    packed = pl.pallas_call(
        functools.partial(gram_kernel, layout),
        out_shape=jax.ShapeDtypeStruct((spots * piece, TILE), F32),
        in_specs=[SMEM, ANY, ANY, VMEM, VMEM, VMEM],
        out_specs=VMEM,
        scratch_shapes=[
            pltpu.VMEM((rows, width), BF16),
            pltpu.VMEM((half, width), F32),
            pltpu.VMEM((chains, half), F32),
            pltpu.VMEM((chains, 1), F32),
            pltpu.SemaphoreType.DMA((pieces, 2)),
        ],
        compiler_params=PARAMS,
        cost_estimate=pl.CostEstimate(flops=0, bytes_accessed=0, transcendentals=0),
        name="gram",
    )(core_arg, genotypes, other, residual, square, own_score)
    late_other, packed = lax.optimization_barrier((other, packed))
    cross = pl.pallas_call(
        cross_kernel,
        out_shape=jax.ShapeDtypeStruct((2, half, half), F32),
        in_specs=[ANY, ANY, VMEM],
        out_specs=VMEM,
        scratch_shapes=[
            pltpu.VMEM((2, rows, half), BF16),
            pltpu.SemaphoreType.DMA((pieces, 2)),
        ],
        compiler_params=PARAMS,
        cost_estimate=pl.CostEstimate(flops=2 * rows * half * half, bytes_accessed=4 * rows * half, transcendentals=0),
        name="cross",
    )(genotypes, late_other, own_cross)
    packed = lax.all_to_all(packed.reshape(spots, piece, TILE), "ind", 0, 0)
    packed, cross = lax.optimization_barrier((packed, cross))
    packed = jnp.broadcast_to(jnp.sum(packed, axis=0)[None], (spots, piece, TILE))
    packed = lax.all_to_all(packed, "ind", 0, 0).reshape(spots * piece, TILE)

    own_effects = lax.dynamic_index_in_dim(effects, core, 0, keepdims=False)
    got_effects = lax.dynamic_index_in_dim(other_effects, core, 0, keepdims=False)
    block_effects = jnp.where(
        core == 0,
        jnp.concatenate([own_effects, got_effects], axis=1),
        jnp.concatenate([got_effects, own_effects], axis=1),
    )
    block_noise = lax.dynamic_index_in_dim(noise, core, 0, keepdims=False)
    block_rows = lax.dynamic_index_in_dim(block_snps.reshape(blocks, count, TILE), core, 0, keepdims=False)
    scale = jnp.sqrt(noise_var)[:, None]
    factor, inverse, shift = pl.pallas_call(
        functools.partial(factor_kernel, layout),
        out_shape=(
            jax.ShapeDtypeStruct((width + chains, width), F32),
            jax.ShapeDtypeStruct((count, TILE, TILE), F32),
            jax.ShapeDtypeStruct((chains, width), F32),
        ),
        in_specs=[VMEM] * 6,
        out_specs=(VMEM,) * 3,
        scratch_shapes=[pltpu.VMEM((SUB, TILE), F32)],
        compiler_params=PARAMS,
        cost_estimate=pl.CostEstimate(flops=0, bytes_accessed=0, transcendentals=0),
        name="factor",
    )(packed, prior_var.reshape(-1, TILE), block_rows, block_effects, block_noise, scale)

    got_shift = lax.ppermute(shift, "snp", swap)
    share = pl.pallas_call(
        cross_share_kernel,
        out_shape=jax.ShapeDtypeStruct((chains, half), F32),
        in_specs=[SMEM] + [VMEM] * 3,
        out_specs=VMEM,
        compiler_params=PARAMS,
        name="cross_share",
    )(core_arg, shift, got_shift, cross)
    shift_0 = jnp.where(core == 0, shift, got_shift)
    after_0 = update(0, genotypes, other, halves_of(shift_0, core, half), residual)
    share, after_0 = line_sums(share, after_0, spots)
    got = lax.ppermute(share, "snp", swap)
    final, share_all = pl.pallas_call(
        second_kernel,
        out_shape=(jax.ShapeDtypeStruct((chains, width), F32),) * 2,
        in_specs=[SMEM] + [VMEM] * 5,
        out_specs=(VMEM, VMEM),
        compiler_params=PARAMS,
        name="second",
    )(core_arg, shift, share, got, factor, inverse)
    got_final = lax.ppermute(final, "snp", swap)
    added = pl.pallas_call(
        functools.partial(squares_kernel, layout),
        out_shape=jax.ShapeDtypeStruct((chains, TILE), F32),
        in_specs=[VMEM] * 3,
        out_specs=VMEM,
        compiler_params=PARAMS,
        name="squares",
    )(final, share_all, packed)
    got_added = lax.ppermute(added, "snp", swap)
    shift_1 = jnp.where(core == 0, got_final, final)
    new_residual = update(1, genotypes, other, halves_of(shift_1, core, half), after_0)
    squares = packed[layout.squares : layout.used, 0] + (added[:, 0] + got_added[:, 0])
    variance_draw = squares / (rows * spots * chi_scaled)
    own_shift = jnp.stack(
        [lax.dynamic_slice_in_dim(block_shift, core * half, half, 1) for block_shift in (shift_0, shift_1)]
    )
    return (effects + own_shift, new_residual, variance_draw)


def solution(mesh):
    placed = (P(None, "ind", "snp"), P(None, "ind"), P(None, None, "snp"), P(), P(), P(), P(), P())
    return jax.shard_map(
        local,
        mesh=mesh,
        in_specs=placed,
        out_specs=(P(None, None, "snp"), P(None, "ind"), P()),
        check_vma=False,
    )
```

```python
import functools

import jax
import jax.numpy as jnp
from jax import lax
from jax.experimental import pallas as pl
from jax.experimental.pallas import tpu as pltpu
from jax.sharding import PartitionSpec as P

F32 = jnp.float32
BF16 = jnp.bfloat16
TILE = 128
SUB = 8
STRIP = 256
CHUNK = 1024
LINE = 4
NT = (((1,), (1,)), ((), ()))
NN = (((1,), (0,)), ((), ()))
TN = (((0,), (0,)), ((), ()))
VMEM = pl.BlockSpec(memory_space=pltpu.VMEM)
SMEM = pl.BlockSpec(memory_space=pltpu.SMEM)
ANY = pl.BlockSpec(memory_space=pl.ANY)
PARAMS = pltpu.CompilerParams(vmem_limit_bytes=52 * 2**20)


def dot_exact(left, right, dims):
    return lax.dot_general(
        left, right, dims, preferred_element_type=F32, precision=lax.Precision.HIGHEST
    )


def dot_bf16(left, right, dims):
    return lax.dot_general(left, right, dims, preferred_element_type=F32)


def spread(row):
    return jnp.broadcast_to(row, (SUB, TILE))


def pieces_of(value):
    high = value.astype(BF16)
    rest = value - high.astype(F32)
    middle = rest.astype(BF16)
    return high, middle, (rest - middle.astype(F32)).astype(BF16)


def dot_rows(left, right, dims):
    rows = left.shape[0]
    parts = pieces_of(left)
    high, middle, low = pieces_of(right)
    one = dot_bf16(jnp.concatenate(parts, axis=0), high, dims)
    two = dot_bf16(jnp.concatenate(parts[:2], axis=0), middle, dims)
    three = dot_bf16(parts[0], low, dims)
    return one[:rows] + ((one[rows : 2 * rows] + two[:rows]) + (one[2 * rows :] + two[rows:] + three))


def tree_sum(terms):
    while len(terms) > 1:
        terms = [terms[i] + terms[i + 1] if i + 1 < len(terms) else terms[i] for i in range(0, len(terms), 2)]
    return terms[0]


def inverse_factor(tile, zero):
    groups = TILE // SUB
    sub = lax.broadcasted_iota(jnp.int32, (SUB, TILE), 0)
    lane = lax.broadcasted_iota(jnp.int32, (SUB, TILE), 1)
    left = [tile[SUB * r : SUB * r + SUB, :] for r in range(groups)]
    done = []
    for g in range(groups):
        first = g * SUB
        inside = (lane >= first) & (lane < first + SUB)
        pivot_cols = [spread(left[g][:, first + j : first + j + 1]) + zero for j in range(SUB)]
        cols = [[spread(left[r][:, first + j : first + j + 1]) for r in range(g + 1, groups)] for j in range(SUB)]
        square = {(i, j): spread(pivot_cols[j][i : i + 1, :]) for j in range(SUB) for i in range(j + 1)}
        own = jnp.where(inside, jnp.where(lane == sub + first, 1.0, 0.0), left[g])
        rows = [spread(own[j : j + 1, :]) for j in range(SUB)]
        last = g + 1 == groups
        near = None if last else [cols[j][0] for j in range(SUB)]
        near_terms = []
        share = {}
        solved = [None] * SUB
        pivots = jnp.zeros((SUB, TILE), F32)
        finished = pivots
        for j in range(0, SUB, 2):
            p, q, r = square[j, j], square[j, j + 1], square[j + 1, j + 1]
            minor = p * r - q * q
            over_minor = pltpu.reciprocal(minor, approx=True)
            over_p = pltpu.reciprocal(p, approx=True)
            ip, iq, ir = r * over_minor, -q * over_minor, p * over_minor
            pivots = jnp.where(sub == j, p, jnp.where(sub == j + 1, minor * over_p, pivots))
            second_row = rows[j + 1] - (q * over_p) * rows[j]
            finished = jnp.where(sub == j, rows[j], jnp.where(sub == j + 1, second_row, finished))
            for k in range(j + 2, SUB):
                upper, lower = square[j, k], square[j + 1, k]
                share[j, k], share[j + 1, k] = upper * ip + lower * iq, upper * iq + lower * ir
            for k in range(j + 2, SUB):
                one, two = share[j, k], share[j + 1, k]
                for i in range(j + 2, k + 1):
                    square[i, k] = square[i, k] - (square[j, i] * one + square[j + 1, i] * two)
                rows[k] = rows[k] - (rows[j] * one + rows[j + 1] * two)
                if not last:
                    near[k] = near[k] - (near[j] * one + near[j + 1] * two)
            solved[j], solved[j + 1] = rows[j] * ip + rows[j + 1] * iq, rows[j] * iq + rows[j + 1] * ir
            if not last:
                near_terms.append(near[j] * solved[j] + near[j + 1] * solved[j + 1])
        if not last:
            left[g + 1] = jnp.where(inside, 0.0, left[g + 1]) - tree_sum(near_terms)
        for j in (4, 5, 2, 3, 0, 1):
            solved[j] = solved[j] - tree_sum([share[j, k] * solved[k] for k in range(j // 2 * 2 + 2, SUB)])
        for r in range(g + 2, groups):
            left[r] = jnp.where(inside, 0.0, left[r]) - tree_sum([cols[j][r - g - 1] * solved[j] for j in range(SUB)])
        root = lax.rsqrt(pivots)
        root = root * (1.5 - 0.5 * pivots * root * root)
        done.append(jnp.where(lane < first + SUB, finished * root, 0.0))
    return jnp.concatenate(done, axis=0)


def split_scores(residual, x):
    high, middle, _ = pieces_of(residual)
    return dot_bf16(high, x, NN) + dot_bf16(middle, x, NN)


def chunk_loop(rows, body):
    whole = rows // CHUNK

    @pl.loop(0, whole)
    def _(i):
        body(i, pl.multiple_of(i * CHUNK, CHUNK), CHUNK)

    if rows % CHUNK:
        body(whole, whole * CHUNK, rows % CHUNK)


def start_copies(sources, places, sems, rows):
    copies = []
    for i, lo in enumerate(range(0, rows, CHUNK)):
        at = pl.ds(lo, min(CHUNK, rows - lo))
        for k, (source, place) in enumerate(zip(sources, places)):
            pltpu.make_async_copy(source.at[at, :], place.at[at, :], sems.at[i, k]).start()


def wait_copies(sources, places, sems, i, start, size):
    at = pl.ds(start, size)
    for k, (source, place) in enumerate(zip(sources, places)):
        pltpu.make_async_copy(source.at[at, :], place.at[at, :], sems.at[i, k]).wait()


def own_kernel(core_ref, own_ref, residual_ref, square_ref, score_ref, cross_ref, mine, sems):
    core = core_ref[0]
    rows, half = own_ref.shape[1:]
    sources, places = [own_ref.at[0], own_ref.at[1]], [mine.at[0], mine.at[1]]
    start_copies(sources, places, sems, rows)
    for ref in (square_ref, score_ref, cross_ref):
        ref[...] = jnp.zeros_like(ref)

    def body(i, start, size):
        wait_copies(sources, places, sems, i, start, size)
        at = pl.ds(start, size)
        score_ref[...] += split_scores(residual_ref[:, at], mine[core, at, :])
        cross_ref[...] += dot_bf16(mine[0, at, :], mine[1, at, :], TN)
        for c in range(0, half, STRIP):
            square_ref[c:, c : c + STRIP] += dot_bf16(mine[core, at, c:], mine[core, at, c : c + STRIP], TN)

    chunk_loop(rows, body)


class Layout:
    def __init__(self, count, chains, spots):
        self.count, self.chains = count, chains
        self.pairs = count * (count - 1) // 2 * TILE
        self.diagonals = self.pairs + count // 2 * TILE
        self.scores = self.diagonals + SUB
        self.squares = self.scores + count * chains
        self.used = self.squares + chains
        self.piece = -(-self.used // (spots * SUB)) * SUB
        self.rows = self.piece * spots

    def lower(self, row, col):
        return (row * (row - 1) // 2 + col) * TILE


def put_diagonal(packed_ref, layout, half_at, block):
    count = layout.count // 2
    row_id = lax.broadcasted_iota(jnp.int32, (TILE, TILE), 0)
    col_id = lax.broadcasted_iota(jnp.int32, (TILE, TILE), 1)
    for r in range(count):
        for c in range(r):
            row, col = half_at * count + r, half_at * count + c
            at = pl.multiple_of((lax.shift_right_logical(row * (row - 1), 1) + col) * TILE, TILE)
            packed_ref[pl.ds(at, TILE), :] = block[r * TILE : r * TILE + TILE, c * TILE : c * TILE + TILE]
    for r in range(0, count, 2):
        one = block[r * TILE : r * TILE + TILE, r * TILE : r * TILE + TILE]
        two = block[(r + 1) * TILE : (r + 2) * TILE, (r + 1) * TILE : (r + 2) * TILE]
        place = half_at * (count // 2) + r // 2
        at = pl.multiple_of(layout.pairs + place * TILE, TILE)
        packed_ref[pl.ds(at, TILE), :] = jnp.where(row_id > col_id, one, two)
        packed_ref[pl.ds(layout.diagonals + place, 1), :] = jnp.sum(
            jnp.where(row_id == col_id, one, 0.0), axis=0, keepdims=True
        )


def get_diagonal(packed_ref, layout, tile):
    row_id = lax.broadcasted_iota(jnp.int32, (TILE, TILE), 0)
    col_id = lax.broadcasted_iota(jnp.int32, (TILE, TILE), 1)
    at = layout.pairs + tile // 2 * TILE
    pair = packed_ref[at : at + TILE, :]
    if tile % 2:
        return jnp.where(row_id < col_id, pair, 0.0), jnp.where(row_id == col_id, pair, 0.0)
    row = layout.diagonals + tile // 2
    return jnp.where(row_id > col_id, pair, 0.0), jnp.where(row_id == col_id, packed_ref[row : row + 1, :], 0.0)


def gram_kernel(
    layout, core_ref, own_ref, other_ref, residual_ref, square_ref, own_score_ref, packed_ref, x, total, score, norm, sems
):
    core = core_ref[0]
    rows, half = own_ref.shape[1:]
    sources = [own_ref.at[core], other_ref.at[core]]
    places = [x.at[:, :half], x.at[:, half:]]
    start_copies(sources, places, sems, rows)
    for ref in (total, score, norm):
        ref[...] = jnp.zeros_like(ref)

    def body(i, start, size):
        wait_copies(sources, places, sems, i, start, size)
        at = pl.ds(start, size)
        total[...] += dot_bf16(x[at, half:], x[at, :], TN)
        score[...] += split_scores(residual_ref[:, at], x[at, half:])
        norm[...] += jnp.sum(jnp.square(residual_ref[:, at]), axis=1, keepdims=True)

    chunk_loop(rows, body)
    count, chains = layout.count, layout.chains
    put_diagonal(packed_ref, layout, core, square_ref)
    put_diagonal(packed_ref, layout, 1 - core, total.at[:, half:])
    for r in range(count // 2):
        for c in range(count // 2):
            at = layout.lower(count // 2 + r, c)

            @pl.when(core == 0)
            def _():
                packed_ref[at : at + TILE, :] = total[r * TILE : r * TILE + TILE, c * TILE : c * TILE + TILE]

            @pl.when(core == 1)
            def _():
                packed_ref[at : at + TILE, :] = total[c * TILE : c * TILE + TILE, r * TILE : r * TILE + TILE].T

    for k, part in ((core, own_score_ref), (1 - core, score)):
        for col in range(count // 2):
            start_row = pl.multiple_of(layout.scores + (k * (count // 2) + col) * chains, SUB)
            packed_ref[pl.ds(start_row, chains), :] = part[:, col * TILE : col * TILE + TILE]
    packed_ref[layout.squares : layout.used, :] = jnp.broadcast_to(norm[...], (chains, TILE))
    packed_ref[layout.used :, :] = jnp.zeros((layout.rows - layout.used, TILE), F32)


def sum_kernel(parts_ref, sums_ref, parts, copies, in_sems, out_sems):
    count, each = parts.shape[0], copies.shape[0]
    moves = [
        pltpu.make_async_copy(parts_ref.at[i : i + each], parts.at[i : i + each], in_sems.at[i // each])
        for i in range(0, count, each)
    ]
    for move in moves:
        move.start()
    total = None
    for i, move in enumerate(moves):
        move.wait()
        group = tree_sum([parts[i * each + j] for j in range(each)])
        total = group if total is None else total + group
    for i in range(each):
        copies[i] = total
    moves = [
        pltpu.make_async_copy(copies, sums_ref.at[i : i + each], out_sems.at[i // each]) for i in range(0, count, each)
    ]
    for move in moves:
        move.start()
    for move in moves:
        move.wait()


def cross_kernel(own_ref, other_ref, own_cross_ref, cross_ref, x, sems):
    rows = own_ref.shape[1]
    sources, places = [other_ref.at[0], own_ref.at[1]], [x.at[0], x.at[1]]
    start_copies(sources, places, sems, rows)
    cross_ref[0] = own_cross_ref[...]
    cross_ref[1] = jnp.zeros(own_cross_ref.shape, F32)

    def body(i, start, size):
        wait_copies(sources, places, sems, i, start, size)
        at = pl.ds(start, size)
        cross_ref[1] += dot_bf16(x[0, at, :], x[1, at, :], TN)

    chunk_loop(rows, body)


def panel_rows(width, k):
    start = sum(width - j * STRIP for j in range(1, k + 1))
    return slice(start, start + width - (k + 1) * STRIP)


def backward(moved, panels_ref, inverse_ref):
    width = len(moved) * STRIP
    solved = [None] * len(moved)
    for k in reversed(range(len(moved))):
        solved[k] = dot_rows(moved[k], inverse_ref[k], NN)
        if k:
            for j in range(k):
                at = panel_rows(width, j).start + (k - j - 1) * STRIP
                moved[j] = moved[j] - dot_rows(solved[k], panels_ref[at : at + STRIP, :], NN)
    return solved


def factor_kernel(
    layout, packed_ref, prior_ref, rows_ref, effects_ref, noise_ref, scale_ref, panels_ref, inverse_ref, shift_ref, factor_ref, zero_ref
):
    width = factor_ref.shape[1]
    count = width // TILE
    chains = effects_ref.shape[0]
    table_rows = rows_ref[...]
    high = lax.shift_right_logical(table_rows, 7)
    low = lax.bitwise_and(table_rows, TILE - 1)
    prior = jnp.zeros((count, TILE), F32)
    for t in range(prior_ref.shape[0]):
        entry = jnp.broadcast_to(prior_ref[t : t + 1, :], (count, TILE))
        prior = jnp.where(high == t, jnp.take_along_axis(entry, low, axis=1), prior)
    inverse_prior = 1.0 / prior
    diagonal = lax.broadcasted_iota(jnp.int32, (TILE, TILE), 0) == lax.broadcasted_iota(jnp.int32, (TILE, TILE), 1)
    for row in range(count):
        rows = slice(row * TILE, row * TILE + TILE)
        for col in range(row):
            at = layout.lower(row, col)
            factor_ref[rows, col * TILE : col * TILE + TILE] = packed_ref[at : at + TILE, :]
        triangle, middle = get_diagonal(packed_ref, layout, row)
        middle = middle + jnp.where(diagonal, inverse_prior[row : row + 1, :], 0.0)
        factor_ref[rows, rows] = triangle + triangle.T + middle
        at = layout.scores + row * chains
        factor_ref[width : width + chains, rows] = (
            packed_ref[at : at + chains, :] - inverse_prior[row : row + 1, :] * effects_ref[:, rows]
        )
    zero_ref[...] = jnp.zeros_like(zero_ref)

    @pl.loop(0, count)
    def _(k):
        at = pl.multiple_of(k * TILE, TILE)
        pair, side = lax.shift_right_logical(k, 1), pl.ds(pl.multiple_of(lax.bitwise_and(k, 1) * TILE, TILE), TILE)
        inverse_ref[pair, side, side] = inverse_factor(factor_ref[pl.ds(at, TILE), pl.ds(at, TILE)], zero_ref[...])
        for step in range(count):

            @pl.when(k == step)
            def _():
                lo, hi = step * TILE, (step + 1) * TILE
                side = slice(step % 2 * TILE, step % 2 * TILE + TILE)
                inverse = inverse_ref[step // 2, side, side]
                factor_ref[hi:, lo:hi] = dot_exact(factor_ref[hi:, lo:hi], inverse, NT)
                if step % 2 == 0:
                    panel = factor_ref[hi:, lo:hi]
                    factor_ref[hi:, hi : hi + TILE] = factor_ref[hi:, hi : hi + TILE] - dot_exact(panel, panel[:TILE, :], NT)
                else:
                    for c in range(hi, width, STRIP):
                        panel = factor_ref[c:, lo - TILE : hi]
                        factor_ref[c:, c : c + STRIP] = factor_ref[c:, c : c + STRIP] - dot_exact(
                            panel, panel[:STRIP, :], NT
                        )
                    below = dot_exact(factor_ref[lo:hi, lo - TILE : lo], inverse_ref[step // 2, :TILE, :TILE], NN)
                    inverse_ref[step // 2, TILE:, :TILE] = -dot_exact(inverse, below, NN)
                    inverse_ref[step // 2, :TILE, TILE:] = jnp.zeros((TILE, TILE), F32)

    scale = scale_ref[...]
    moved = [
        factor_ref[width : width + chains, j : j + STRIP] + scale * noise_ref[:, j : j + STRIP]
        for j in range(0, width, STRIP)
    ]
    for k in range(width // STRIP - 1):
        panels_ref[panel_rows(width, k), :] = factor_ref[(k + 1) * STRIP : width, k * STRIP : (k + 1) * STRIP]
    for j, part in enumerate(backward(moved, panels_ref, inverse_ref)):
        shift_ref[:, j * STRIP : j * STRIP + STRIP] = part


def cross_share_kernel(core_ref, shift_ref, got_ref, cross_ref, share_ref):
    core = core_ref[0]
    half = cross_ref.shape[1]
    shift = jnp.where(core == 0, shift_ref[...], got_ref[...])
    change = shift.astype(BF16)
    first, last = change[:, :half], change[:, half:]
    mine = jnp.where(core == 0, first, last)
    theirs = jnp.where(core == 0, last, first)
    share_ref[...] = sum(
        dot_bf16(change, part, NN) for change, ref in ((mine, cross_ref[0]), (theirs, cross_ref[1])) for part in pieces_of(ref)
    )


def second_kernel(layout, core_ref, shift_ref, share_ref, got_ref, panels_ref, inverse_ref, packed_ref, final_ref):
    width, count, chains = shift_ref.shape[1], layout.count, layout.chains
    keep = jnp.where(core_ref[0] == 1, 1.0, 0.0)
    right = jnp.concatenate([got_ref[...], share_ref[...]], axis=1) * keep
    moved = [right[:, j : j + STRIP] for j in range(0, width, STRIP)]
    for k in range(len(moved)):
        moved[k] = dot_rows(moved[k], inverse_ref[k], NT)
        lo = (k + 1) * STRIP
        if lo < width:
            change_by = dot_rows(moved[k], panels_ref[panel_rows(width, k), :], NT)
            for j in range(k + 1, len(moved)):
                moved[j] = moved[j] - change_by[:, (j - k - 1) * STRIP : (j - k) * STRIP]
    for j, part in enumerate(backward(moved, panels_ref, inverse_ref)):
        cols = slice(j * STRIP, j * STRIP + STRIP)
        final_ref[:, cols] = shift_ref[:, cols] - part
    change = final_ref[:, :width].astype(BF16)
    value = change.astype(F32)
    total = jnp.zeros((chains, TILE), F32)
    for row in range(count):
        cols = slice(row * TILE, row * TILE + TILE)
        triangle, middle = get_diagonal(packed_ref, layout, row)
        tiles = [packed_ref[layout.lower(row, col) : layout.lower(row, col) + TILE, :] for col in range(row)]
        strip = jnp.concatenate([tile + tile for tile in tiles] + [triangle + triangle + middle], axis=1)
        product = sum(dot_bf16(change[:, : (row + 1) * TILE], part, NT) for part in pieces_of(strip))
        at = layout.scores + row * chains
        score = packed_ref[at : at + chains, :] - right[:, cols]
        total = total + value[:, cols] * (product - (score + score))
    final_ref[:, width:] = jnp.broadcast_to(jnp.sum(total, axis=1, keepdims=True), (chains, TILE))


def update_rows(block, core, own_ref, other_ref, shift, residual_ref, new_ref, x, sems):
    rows, half = own_ref.shape[1:]
    sources, places = [own_ref.at[block], other_ref.at[block]], [x.at[0], x.at[1]]
    start_copies(sources, places, sems, rows)
    mine = jnp.where(core == 0, shift[:, :half], shift[:, half:])
    theirs = jnp.where(core == 0, shift[:, half:], shift[:, :half])
    own_change, their_change = mine.astype(BF16), theirs.astype(BF16)
    for i, start in enumerate(range(0, rows, CHUNK)):
        size = min(CHUNK, rows - start)
        wait_copies(sources, places, sems, i, start, size)
        at = pl.ds(start, size)
        change = dot_bf16(own_change, x[0, at, :], NT) + dot_bf16(their_change, x[1, at, :], NT)
        new_ref[:, at] = residual_ref[:, at] - change
    return mine


def first_update_kernel(core_ref, own_ref, other_ref, here_ref, there_ref, residual_ref, new_ref, mine_ref, x, sems):
    core = core_ref[0]
    shift = jnp.where(core == 0, here_ref[...], there_ref[...])
    mine_ref[...] = update_rows(0, core, own_ref, other_ref, shift, residual_ref, new_ref, x, sems)


def last_update_kernel(
    layout, people, core_ref, own_ref, other_ref, here_ref, there_ref, residual_ref, effects_ref, first_ref, norm_ref,
    chi_ref, new_ref, new_effects_ref, draw_ref, x, sems
):
    core, width = core_ref[0], 2 * own_ref.shape[2]
    squares = norm_ref[...] + (here_ref[:, width:] + there_ref[:, width:])
    draw_ref[...] = squares.T[:1, :] / (people * chi_ref[...])
    shift = jnp.where(core == 1, here_ref[:, :width], there_ref[:, :width])
    mine = update_rows(1, core, own_ref, other_ref, shift, residual_ref, new_ref, x, sems)
    new_effects_ref[0] = effects_ref[0] + first_ref[...]
    new_effects_ref[1] = effects_ref[1] + mine


def update_call(kernel, out_shape, genotypes, name, *operands):
    rows, half = genotypes.shape[1:]
    return pl.pallas_call(
        kernel,
        out_shape=out_shape,
        in_specs=[SMEM, ANY, ANY] + [VMEM] * (len(operands) - 2),
        out_specs=(VMEM,) * len(out_shape),
        scratch_shapes=[
            pltpu.VMEM((2, rows, half), BF16),
            pltpu.SemaphoreType.DMA((-(-rows // CHUNK), 2)),
        ],
        compiler_params=PARAMS,
        cost_estimate=pl.CostEstimate(flops=64 * rows * half * 8, bytes_accessed=4 * rows * half, transcendentals=0),
        name=name,
    )(operands[0], genotypes, *operands[1:])


def line_sums(value, beside, spots):
    stride = 1
    while stride < spots:
        at = [i // stride % LINE for i in range(spots)]
        one, two, three = (
            lax.ppermute(value, "ind", [(i, i + ((at[i] + step) % LINE - at[i]) * stride) for i in range(spots)])
            for step in range(1, LINE)
        )
        if stride == 1:
            one, two, three, beside = lax.optimization_barrier((one, two, three, beside))
        even = lax.axis_index("ind") // stride % 2 == 0
        value = (value + jnp.where(even, three, one)) + (two + jnp.where(even, one, three))
        stride *= LINE
    return value, beside


def local(genotypes, residual, effects, noise, prior_var, block_snps, noise_var, chi_scaled):
    blocks, rows, half = genotypes.shape
    chains = residual.shape[0]
    width = 2 * half
    count = width // TILE
    spots = lax.axis_size("ind")
    core = lax.axis_index("snp")
    core_arg = jnp.reshape(core.astype(jnp.int32), (1,))
    swap = [(0, 1), (1, 0)]
    pieces = -(-rows // CHUNK)

    other = lax.ppermute(genotypes, "snp", swap)
    other_effects = lax.ppermute(effects, "snp", swap)

    layout = Layout(count, chains, spots)
    piece = layout.piece
    square, own_score, own_cross = pl.pallas_call(
        own_kernel,
        out_shape=(
            jax.ShapeDtypeStruct((half, half), F32),
            jax.ShapeDtypeStruct((chains, half), F32),
            jax.ShapeDtypeStruct((half, half), F32),
        ),
        in_specs=[SMEM, ANY, VMEM],
        out_specs=(VMEM,) * 3,
        scratch_shapes=[pltpu.VMEM((2, rows, half), BF16), pltpu.SemaphoreType.DMA((pieces, 2))],
        compiler_params=PARAMS,
        cost_estimate=pl.CostEstimate(flops=2 * rows * half * half, bytes_accessed=2 * rows * half, transcendentals=0),
        name="own",
    )(core_arg, genotypes, residual)
    packed = pl.pallas_call(
        functools.partial(gram_kernel, layout),
        out_shape=jax.ShapeDtypeStruct((spots * piece, TILE), F32),
        in_specs=[SMEM, ANY, ANY, VMEM, VMEM, VMEM],
        out_specs=VMEM,
        scratch_shapes=[
            pltpu.VMEM((rows, width), BF16),
            pltpu.VMEM((half, width), F32),
            pltpu.VMEM((chains, half), F32),
            pltpu.VMEM((chains, 1), F32),
            pltpu.SemaphoreType.DMA((pieces, 2)),
        ],
        compiler_params=PARAMS,
        cost_estimate=pl.CostEstimate(flops=0, bytes_accessed=0, transcendentals=0),
        name="gram",
    )(core_arg, genotypes, other, residual, square, own_score)
    late_other, packed = lax.optimization_barrier((other, packed))
    cross = pl.pallas_call(
        cross_kernel,
        out_shape=jax.ShapeDtypeStruct((2, half, half), F32),
        in_specs=[ANY, ANY, VMEM],
        out_specs=VMEM,
        scratch_shapes=[
            pltpu.VMEM((2, rows, half), BF16),
            pltpu.SemaphoreType.DMA((pieces, 2)),
        ],
        compiler_params=PARAMS,
        cost_estimate=pl.CostEstimate(flops=2 * rows * half * half, bytes_accessed=4 * rows * half, transcendentals=0),
        name="cross",
    )(genotypes, late_other, own_cross)
    packed = lax.all_to_all(packed.reshape(spots, piece, TILE), "ind", 0, 0)
    packed, cross = lax.optimization_barrier((packed, cross))
    packed = pl.pallas_call(
        sum_kernel,
        out_shape=jax.ShapeDtypeStruct(packed.shape, F32),
        in_specs=[ANY],
        out_specs=ANY,
        scratch_shapes=[
            pltpu.VMEM((spots, piece, TILE), F32),
            pltpu.VMEM((SUB, piece, TILE), F32),
            pltpu.SemaphoreType.DMA((spots // SUB,)),
            pltpu.SemaphoreType.DMA((spots // SUB,)),
        ],
        compiler_params=PARAMS,
        name="sums",
    )(packed)
    packed = lax.all_to_all(packed, "ind", 0, 0).reshape(spots * piece, TILE)

    own_effects = lax.dynamic_index_in_dim(effects, core, 0, keepdims=False)
    got_effects = lax.dynamic_index_in_dim(other_effects, core, 0, keepdims=False)
    block_effects = jnp.where(
        core == 0,
        jnp.concatenate([own_effects, got_effects], axis=1),
        jnp.concatenate([got_effects, own_effects], axis=1),
    )
    block_noise = lax.dynamic_index_in_dim(noise, core, 0, keepdims=False)
    block_rows = lax.dynamic_index_in_dim(block_snps.reshape(blocks, count, TILE), core, 0, keepdims=False)
    scale = jnp.sqrt(noise_var)[:, None]
    panels, inverse, shift = pl.pallas_call(
        functools.partial(factor_kernel, layout),
        out_shape=(
            jax.ShapeDtypeStruct((panel_rows(width, width // STRIP - 1).start, STRIP), F32),
            jax.ShapeDtypeStruct((width // STRIP, STRIP, STRIP), F32),
            jax.ShapeDtypeStruct((chains, width), F32),
        ),
        in_specs=[VMEM] * 6,
        out_specs=(VMEM,) * 3,
        scratch_shapes=[pltpu.VMEM((width + chains, width), F32), pltpu.VMEM((SUB, TILE), F32)],
        compiler_params=PARAMS,
        cost_estimate=pl.CostEstimate(flops=0, bytes_accessed=0, transcendentals=0),
        name="factor",
    )(packed, prior_var.reshape(-1, TILE), block_rows, block_effects, block_noise, scale)

    got_shift = lax.ppermute(shift, "snp", swap)
    share = pl.pallas_call(
        cross_share_kernel,
        out_shape=jax.ShapeDtypeStruct((chains, half), F32),
        in_specs=[SMEM] + [VMEM] * 3,
        out_specs=VMEM,
        compiler_params=PARAMS,
        name="cross_share",
    )(core_arg, shift, got_shift, cross)
    after_0, first_shift = update_call(
        first_update_kernel,
        (jax.ShapeDtypeStruct(residual.shape, F32), jax.ShapeDtypeStruct((chains, half), F32)),
        genotypes,
        "first_update",
        core_arg,
        other,
        shift,
        got_shift,
        residual,
    )
    share, after_0 = line_sums(share, after_0, spots)
    got = lax.ppermute(share, "snp", swap)
    final = pl.pallas_call(
        functools.partial(second_kernel, layout),
        out_shape=jax.ShapeDtypeStruct((chains, width + TILE), F32),
        in_specs=[SMEM] + [VMEM] * 6,
        out_specs=VMEM,
        compiler_params=PARAMS,
        name="second",
    )(core_arg, shift, share, got, panels, inverse, packed)
    got_final = lax.ppermute(final, "snp", swap)
    new_residual, new_effects, draw = update_call(
        functools.partial(last_update_kernel, layout, rows * spots),
        (
            jax.ShapeDtypeStruct(residual.shape, F32),
            jax.ShapeDtypeStruct(effects.shape, F32),
            jax.ShapeDtypeStruct((1, chains), F32),
        ),
        genotypes,
        "last_update",
        core_arg,
        other,
        final,
        got_final,
        after_0,
        effects,
        first_shift,
        packed[layout.squares : layout.used],
        chi_scaled[None, :],
    )
    return (new_effects, new_residual, draw[0])


def solution(mesh):
    placed = (P(None, "ind", "snp"), P(None, "ind"), P(None, None, "snp"), P(), P(), P(), P(), P())
    return jax.shard_map(
        local,
        mesh=mesh,
        in_specs=placed,
        out_specs=(P(None, None, "snp"), P(None, "ind"), P()),
        check_vma=False,
    )
```

```python
import functools

import jax
import jax.numpy as jnp
from jax import lax
from jax.experimental import pallas as pl
from jax.experimental.pallas import tpu as pltpu
from jax.sharding import PartitionSpec as P

F32 = jnp.float32
BF16 = jnp.bfloat16
TILE = 128
SUB = 8
STRIP = 256
CHUNK = 1024
LINE = 4
NT = (((1,), (1,)), ((), ()))
NN = (((1,), (0,)), ((), ()))
TN = (((0,), (0,)), ((), ()))
VMEM = pl.BlockSpec(memory_space=pltpu.VMEM)
SMEM = pl.BlockSpec(memory_space=pltpu.SMEM)
ANY = pl.BlockSpec(memory_space=pl.ANY)
PARAMS = pltpu.CompilerParams(vmem_limit_bytes=52 * 2**20)


def dot_exact(left, right, dims):
    return lax.dot_general(
        left, right, dims, preferred_element_type=F32, precision=lax.Precision.HIGHEST
    )


def dot_bf16(left, right, dims):
    return lax.dot_general(left, right, dims, preferred_element_type=F32)


def spread(row):
    return jnp.broadcast_to(row, (SUB, TILE))


def pieces_of(value):
    high = value.astype(BF16)
    rest = value - high.astype(F32)
    middle = rest.astype(BF16)
    return high, middle, (rest - middle.astype(F32)).astype(BF16)


def dot_rows(left, right, dims):
    rows = left.shape[0]
    parts = pieces_of(left)
    high, middle, low = pieces_of(right)
    one = dot_bf16(jnp.concatenate(parts, axis=0), high, dims)
    two = dot_bf16(jnp.concatenate(parts[:2], axis=0), middle, dims)
    three = dot_bf16(parts[0], low, dims)
    return one[:rows] + ((one[rows : 2 * rows] + two[:rows]) + (one[2 * rows :] + two[rows:] + three))


def tree_sum(terms):
    while len(terms) > 1:
        terms = [terms[i] + terms[i + 1] if i + 1 < len(terms) else terms[i] for i in range(0, len(terms), 2)]
    return terms[0]


def inverse_factor(tile, zero):
    groups = TILE // SUB
    sub = lax.broadcasted_iota(jnp.int32, (SUB, TILE), 0)
    lane = lax.broadcasted_iota(jnp.int32, (SUB, TILE), 1)
    left = [tile[SUB * r : SUB * r + SUB, :] for r in range(groups)]
    done = []
    pivot_cols = [spread(left[0][:, j : j + 1]) + zero for j in range(SUB)]
    for g in range(groups):
        first, after = g * SUB, (g + 1) * SUB
        last = g + 1 == groups
        inside = (lane >= first) & (lane < after)
        near = [] if last else [spread(left[g + 1][:, first + j : first + j + 1]) for j in range(SUB)]
        coming = [] if last else [spread(left[g + 1][:, after + j : after + j + 1]) + zero for j in range(SUB)]
        cols = [[spread(left[r][:, first + j : first + j + 1]) for r in range(g + 2, groups)] for j in range(SUB)]
        square = {(i, j): spread(pivot_cols[j][i : i + 1, :]) for j in range(SUB) for i in range(j + 1)}
        own = jnp.where(inside, jnp.where(lane == sub + first, 1.0, 0.0), left[g])
        rows = [spread(own[j : j + 1, :]) for j in range(SUB)]
        near_terms = []
        near_solved = []
        share = {}
        solved = [None] * SUB
        pivots = jnp.zeros((SUB, TILE), F32)
        finished = pivots
        for j in range(0, SUB, 2):
            p, q, r = square[j, j], square[j, j + 1], square[j + 1, j + 1]
            minor = p * r - q * q
            over_minor = pltpu.reciprocal(minor, approx=True)
            over_p = pltpu.reciprocal(p, approx=True)
            ip, iq, ir = r * over_minor, -q * over_minor, p * over_minor
            pivots = jnp.where(sub == j, p, jnp.where(sub == j + 1, minor * over_p, pivots))
            second_row = rows[j + 1] - (q * over_p) * rows[j]
            finished = jnp.where(sub == j, rows[j], jnp.where(sub == j + 1, second_row, finished))
            for k in range(j + 2, SUB):
                upper, lower = square[j, k], square[j + 1, k]
                share[j, k], share[j + 1, k] = upper * ip + lower * iq, upper * iq + lower * ir
            for k in range(j + 2, SUB):
                one, two = share[j, k], share[j + 1, k]
                for i in range(j + 2, k + 1):
                    square[i, k] = square[i, k] - (square[j, i] * one + square[j + 1, i] * two)
                rows[k] = rows[k] - (rows[j] * one + rows[j + 1] * two)
                if not last:
                    near[k] = near[k] - (near[j] * one + near[j + 1] * two)
            solved[j], solved[j + 1] = rows[j] * ip + rows[j + 1] * iq, rows[j] * iq + rows[j + 1] * ir
            if not last:
                near_solved += [near[j] * ip + near[j + 1] * iq, near[j] * iq + near[j + 1] * ir]
                near_terms.append(near[j] * solved[j] + near[j + 1] * solved[j + 1])
        if not last:
            pivot_cols = [
                coming[j] - tree_sum([near[k] * spread(near_solved[k][j : j + 1, :]) for k in range(SUB)])
                for j in range(SUB)
            ]
            left[g + 1] = jnp.where(inside, 0.0, left[g + 1]) - tree_sum(near_terms)
        for j in (4, 5, 2, 3, 0, 1):
            solved[j] = solved[j] - tree_sum([share[j, k] * solved[k] for k in range(j // 2 * 2 + 2, SUB)])
        for r in range(g + 2, groups):
            left[r] = jnp.where(inside, 0.0, left[r]) - tree_sum([cols[j][r - g - 2] * solved[j] for j in range(SUB)])
        root = lax.rsqrt(pivots)
        root = root * (1.5 - 0.5 * pivots * root * root)
        done.append(jnp.where(lane < after, finished * root, 0.0))
    return jnp.concatenate(done, axis=0)


def split_scores(residual, x):
    chains = residual.shape[0]
    high, middle, _ = pieces_of(residual)
    both = dot_bf16(jnp.concatenate([high, middle], axis=0), x, NN)
    return both[:chains] + both[chains:]


def chunk_loop(rows, body):
    whole = rows // CHUNK

    @pl.loop(0, whole)
    def _(i):
        body(i, pl.multiple_of(i * CHUNK, CHUNK), CHUNK)

    if rows % CHUNK:
        body(whole, whole * CHUNK, rows % CHUNK)


def start_copies(sources, places, sems, rows):
    for i, lo in enumerate(range(0, rows, CHUNK)):
        at = pl.ds(lo, min(CHUNK, rows - lo))
        for k, (source, place) in enumerate(zip(sources, places)):
            pltpu.make_async_copy(source.at[at, :], place.at[at, :], sems.at[i, k]).start()


def wait_copies(sources, places, sems, i, start, size):
    at = pl.ds(start, size)
    for k, (source, place) in enumerate(zip(sources, places)):
        pltpu.make_async_copy(source.at[at, :], place.at[at, :], sems.at[i, k]).wait()


def own_kernel(core_ref, own_ref, residual_ref, square_ref, score_ref, cross_ref, mine, sems):
    core = core_ref[0]
    rows, half = own_ref.shape[1:]
    sources, places = [own_ref.at[0], own_ref.at[1]], [mine.at[0], mine.at[1]]
    start_copies(sources, places, sems, rows)
    for ref in (square_ref, score_ref, cross_ref):
        ref[...] = jnp.zeros_like(ref)

    def body(i, start, size):
        wait_copies(sources, places, sems, i, start, size)
        at = pl.ds(start, size)
        score_ref[...] += split_scores(residual_ref[:, at], mine[core, at, :])
        cross_ref[...] += dot_bf16(mine[0, at, :], mine[1, at, :], TN)
        for c in range(0, half, STRIP):
            square_ref[c:, c : c + STRIP] += dot_bf16(mine[core, at, c:], mine[core, at, c : c + STRIP], TN)

    chunk_loop(rows, body)


class Layout:
    def __init__(self, count, chains, spots):
        self.count, self.chains = count, chains
        self.pairs = count * (count - 1) // 2 * TILE
        self.diagonals = self.pairs + count // 2 * TILE
        self.scores = self.diagonals + SUB
        self.squares = self.scores + count * chains
        self.used = self.squares + chains
        self.piece = -(-self.used // (spots * SUB)) * SUB
        self.rows = self.piece * spots

    def lower(self, row, col):
        return (row * (row - 1) // 2 + col) * TILE


def put_diagonal(packed_ref, layout, half_at, block):
    count = layout.count // 2
    row_id = lax.broadcasted_iota(jnp.int32, (TILE, TILE), 0)
    col_id = lax.broadcasted_iota(jnp.int32, (TILE, TILE), 1)
    for r in range(count):
        for c in range(r):
            row, col = half_at * count + r, half_at * count + c
            at = pl.multiple_of((lax.shift_right_logical(row * (row - 1), 1) + col) * TILE, TILE)
            packed_ref[pl.ds(at, TILE), :] = block[r * TILE : r * TILE + TILE, c * TILE : c * TILE + TILE]
    for r in range(0, count, 2):
        one = block[r * TILE : r * TILE + TILE, r * TILE : r * TILE + TILE]
        two = block[(r + 1) * TILE : (r + 2) * TILE, (r + 1) * TILE : (r + 2) * TILE]
        place = half_at * (count // 2) + r // 2
        at = pl.multiple_of(layout.pairs + place * TILE, TILE)
        packed_ref[pl.ds(at, TILE), :] = jnp.where(row_id > col_id, one, two)
        packed_ref[pl.ds(layout.diagonals + place, 1), :] = jnp.sum(
            jnp.where(row_id == col_id, one, 0.0), axis=0, keepdims=True
        )


def get_diagonal(packed_ref, layout, tile):
    row_id = lax.broadcasted_iota(jnp.int32, (TILE, TILE), 0)
    col_id = lax.broadcasted_iota(jnp.int32, (TILE, TILE), 1)
    at = layout.pairs + tile // 2 * TILE
    pair = packed_ref[at : at + TILE, :]
    if tile % 2:
        return jnp.where(row_id < col_id, pair, 0.0), jnp.where(row_id == col_id, pair, 0.0)
    row = layout.diagonals + tile // 2
    return jnp.where(row_id > col_id, pair, 0.0), jnp.where(row_id == col_id, packed_ref[row : row + 1, :], 0.0)


def gram_kernel(
    layout, core_ref, own_ref, other_ref, residual_ref, square_ref, own_score_ref, packed_ref, x, total, score, norm, sems
):
    core = core_ref[0]
    rows, half = own_ref.shape[1:]
    sources = [own_ref.at[core], other_ref.at[core]]
    places = [x.at[:, :half], x.at[:, half:]]
    start_copies(sources, places, sems, rows)
    for ref in (total, score, norm):
        ref[...] = jnp.zeros_like(ref)

    def body(i, start, size):
        wait_copies(sources, places, sems, i, start, size)
        at = pl.ds(start, size)
        total[...] += dot_bf16(x[at, half:], x[at, :], TN)
        score[...] += split_scores(residual_ref[:, at], x[at, half:])
        norm[...] += jnp.sum(jnp.square(residual_ref[:, at]), axis=1, keepdims=True)

    chunk_loop(rows, body)
    count, chains = layout.count, layout.chains
    put_diagonal(packed_ref, layout, core, square_ref)
    put_diagonal(packed_ref, layout, 1 - core, total.at[:, half:])
    below = [(r, c, layout.lower(count // 2 + r, c)) for r in range(count // 2) for c in range(count // 2)]

    @pl.when(core == 0)
    def _():
        for r, c, at in below:
            packed_ref[at : at + TILE, :] = total[r * TILE : r * TILE + TILE, c * TILE : c * TILE + TILE]

    @pl.when(core == 1)
    def _():
        for r, c, at in below:
            packed_ref[at : at + TILE, :] = total[c * TILE : c * TILE + TILE, r * TILE : r * TILE + TILE].T

    for k, part in ((core, own_score_ref), (1 - core, score)):
        for col in range(count // 2):
            start_row = pl.multiple_of(layout.scores + (k * (count // 2) + col) * chains, SUB)
            packed_ref[pl.ds(start_row, chains), :] = part[:, col * TILE : col * TILE + TILE]
    packed_ref[layout.squares : layout.used, :] = jnp.broadcast_to(norm[...], (chains, TILE))
    packed_ref[layout.used :, :] = jnp.zeros((layout.rows - layout.used, TILE), F32)


def sum_kernel(parts_ref, sums_ref, parts, copies, in_sems, out_sems):
    count, each = parts.shape[0], copies.shape[0]
    moves = [
        pltpu.make_async_copy(parts_ref.at[i : i + each], parts.at[i : i + each], in_sems.at[i // each])
        for i in range(0, count, each)
    ]
    for move in moves:
        move.start()
    total = None
    for i, move in enumerate(moves):
        move.wait()
        group = tree_sum([parts[i * each + j] for j in range(each)])
        total = group if total is None else total + group
    for i in range(each):
        copies[i] = total
    moves = [
        pltpu.make_async_copy(copies, sums_ref.at[i : i + each], out_sems.at[i // each]) for i in range(0, count, each)
    ]
    for move in moves:
        move.start()
    for move in moves:
        move.wait()


def cross_kernel(own_ref, other_ref, own_cross_ref, cross_ref, x, sems):
    rows = own_ref.shape[1]
    sources, places = [other_ref.at[0], own_ref.at[1]], [x.at[0], x.at[1]]
    start_copies(sources, places, sems, rows)
    cross_ref[0] = own_cross_ref[...]
    cross_ref[1] = jnp.zeros(own_cross_ref.shape, F32)

    def body(i, start, size):
        wait_copies(sources, places, sems, i, start, size)
        at = pl.ds(start, size)
        cross_ref[1] += dot_bf16(x[0, at, :], x[1, at, :], TN)

    chunk_loop(rows, body)


def panel_rows(width, k):
    start = sum(width - j * STRIP for j in range(1, k + 1))
    return slice(start, start + width - (k + 1) * STRIP)


def backward(moved, panels_ref, inverse_ref):
    width = len(moved) * STRIP
    solved = [None] * len(moved)
    for k in reversed(range(len(moved))):
        solved[k] = dot_rows(moved[k], inverse_ref[k], NN)
        if k:
            for j in range(k):
                at = panel_rows(width, j).start + (k - j - 1) * STRIP
                moved[j] = moved[j] - dot_rows(solved[k], panels_ref[at : at + STRIP, :], NN)
    return solved


def factor_kernel(
    layout, packed_hbm, prior_ref, rows_ref, effects_ref, noise_ref, scale_ref, panels_hbm, inverse_hbm, shift_ref,
    packed_ref, panels_ref, inverse_ref, factor_ref, zero_ref, sems
):
    width = factor_ref.shape[1]
    count = width // TILE
    chains = effects_ref.shape[0]
    halfway = layout.lower(count * 3 // 4, 0)
    parts = [slice(0, halfway), slice(halfway, layout.pairs), slice(layout.pairs, layout.rows)]
    arrivals = [pltpu.make_async_copy(packed_hbm.at[at], packed_ref.at[at], sems.at[i]) for i, at in enumerate(parts)]
    for arrival in arrivals:
        arrival.start()
    table_rows = rows_ref[...]
    high = lax.shift_right_logical(table_rows, 7)
    low = lax.bitwise_and(table_rows, TILE - 1)
    prior = jnp.zeros((count, TILE), F32)
    for t in range(prior_ref.shape[0]):
        entry = jnp.broadcast_to(prior_ref[t : t + 1, :], (count, TILE))
        prior = jnp.where(high == t, jnp.take_along_axis(entry, low, axis=1), prior)
    inverse_prior = 1.0 / prior
    diagonal = lax.broadcasted_iota(jnp.int32, (TILE, TILE), 0) == lax.broadcasted_iota(jnp.int32, (TILE, TILE), 1)
    for row in range(count):
        rows = slice(row * TILE, row * TILE + TILE)
        if row in (0, count * 3 // 4):
            arrivals[0 if row == 0 else 1].wait()
        for col in range(row):
            at = layout.lower(row, col)
            factor_ref[rows, col * TILE : col * TILE + TILE] = packed_ref[at : at + TILE, :]
    arrivals[2].wait()
    for row in range(count):
        rows = slice(row * TILE, row * TILE + TILE)
        triangle, middle = get_diagonal(packed_ref, layout, row)
        middle = middle + jnp.where(diagonal, inverse_prior[row : row + 1, :], 0.0)
        factor_ref[rows, rows] = triangle + triangle.T + middle
        at = layout.scores + row * chains
        factor_ref[width : width + chains, rows] = (
            packed_ref[at : at + chains, :] - inverse_prior[row : row + 1, :] * effects_ref[:, rows]
        )
    zero_ref[...] = jnp.zeros_like(zero_ref)

    @pl.loop(0, count)
    def _(k):
        at = pl.multiple_of(k * TILE, TILE)
        pair, side = lax.shift_right_logical(k, 1), pl.ds(pl.multiple_of(lax.bitwise_and(k, 1) * TILE, TILE), TILE)
        inverse_ref[pair, side, side] = inverse_factor(factor_ref[pl.ds(at, TILE), pl.ds(at, TILE)], zero_ref[...])
        for step in range(count):

            @pl.when(k == step)
            def _():
                lo, hi = step * TILE, (step + 1) * TILE
                side = slice(step % 2 * TILE, step % 2 * TILE + TILE)
                inverse = inverse_ref[step // 2, side, side]
                factor_ref[hi:, lo:hi] = dot_exact(factor_ref[hi:, lo:hi], inverse, NT)
                if step % 2 == 0:
                    panel = factor_ref[hi:, lo:hi]
                    factor_ref[hi:, hi : hi + TILE] = factor_ref[hi:, hi : hi + TILE] - dot_exact(panel, panel[:TILE, :], NT)
                else:
                    for c in range(hi, width, STRIP):
                        panel = factor_ref[c:, lo - TILE : hi]
                        factor_ref[c:, c : c + STRIP] = factor_ref[c:, c : c + STRIP] - dot_exact(
                            panel, panel[:STRIP, :], NT
                        )
                    below = dot_exact(factor_ref[lo:hi, lo - TILE : lo], inverse_ref[step // 2, :TILE, :TILE], NN)
                    inverse_ref[step // 2, TILE:, :TILE] = -dot_exact(inverse, below, NN)
                    inverse_ref[step // 2, :TILE, TILE:] = jnp.zeros((TILE, TILE), F32)

    scale = scale_ref[...]
    moved = [
        factor_ref[width : width + chains, j : j + STRIP] + scale * noise_ref[:, j : j + STRIP]
        for j in range(0, width, STRIP)
    ]
    for k in range(width // STRIP - 1):
        panels_ref[panel_rows(width, k), :] = factor_ref[(k + 1) * STRIP : width, k * STRIP : (k + 1) * STRIP]
    departures = [
        pltpu.make_async_copy(panels_ref, panels_hbm, sems.at[3]),
        pltpu.make_async_copy(inverse_ref, inverse_hbm, sems.at[4]),
    ]
    for departure in departures:
        departure.start()
    for j, part in enumerate(backward(moved, panels_ref, inverse_ref)):
        shift_ref[:, j * STRIP : j * STRIP + STRIP] = part
    for departure in departures:
        departure.wait()


def cross_share_kernel(core_ref, shift_ref, got_ref, cross_hbm, share_ref, cross_ref, sems):
    core = core_ref[0]
    half = cross_ref.shape[1]
    arrivals = [pltpu.make_async_copy(cross_hbm.at[i], cross_ref.at[i], sems.at[i]) for i in range(2)]
    for arrival in arrivals:
        arrival.start()
    shift = jnp.where(core == 0, shift_ref[...], got_ref[...])
    change = shift.astype(BF16)
    first, last = change[:, :half], change[:, half:]
    mine = jnp.where(core == 0, first, last)
    theirs = jnp.where(core == 0, last, first)
    total = None
    for i, part in enumerate((mine, theirs)):
        arrivals[i].wait()
        product = sum(dot_bf16(part, piece, NN) for piece in pieces_of(cross_ref[i]))
        total = product if total is None else total + product
    share_ref[...] = total


def second_kernel(
    layout, core_ref, shift_ref, share_ref, got_ref, panels_hbm, inverse_hbm, packed_hbm, final_ref,
    panels_ref, inverse_ref, packed_ref, sems
):
    width, count, chains = shift_ref.shape[1], layout.count, layout.chains
    pairs = ((inverse_hbm, inverse_ref), (panels_hbm, panels_ref), (packed_hbm, packed_ref))
    arrivals = [pltpu.make_async_copy(source, place, sems.at[i]) for i, (source, place) in enumerate(pairs)]
    for arrival in arrivals:
        arrival.start()
    keep = jnp.where(core_ref[0] == 1, 1.0, 0.0)
    right = jnp.concatenate([got_ref[...], share_ref[...]], axis=1) * keep
    moved = [right[:, j : j + STRIP] for j in range(0, width, STRIP)]
    arrivals[0].wait()
    for k in range(len(moved)):
        moved[k] = dot_rows(moved[k], inverse_ref[k], NT)
        if k == 0:
            arrivals[1].wait()
        lo = (k + 1) * STRIP
        if lo < width:
            change_by = dot_rows(moved[k], panels_ref[panel_rows(width, k), :], NT)
            for j in range(k + 1, len(moved)):
                moved[j] = moved[j] - change_by[:, (j - k - 1) * STRIP : (j - k) * STRIP]
    for j, part in enumerate(backward(moved, panels_ref, inverse_ref)):
        cols = slice(j * STRIP, j * STRIP + STRIP)
        final_ref[:, cols] = shift_ref[:, cols] - part
    change = final_ref[:, :width].astype(BF16)
    value = change.astype(F32)
    total = jnp.zeros((chains, TILE), F32)
    arrivals[2].wait()
    for row in range(count):
        cols = slice(row * TILE, row * TILE + TILE)
        triangle, middle = get_diagonal(packed_ref, layout, row)
        tiles = [packed_ref[layout.lower(row, col) : layout.lower(row, col) + TILE, :] for col in range(row)]
        strip = jnp.concatenate([tile + tile for tile in tiles] + [triangle + triangle + middle], axis=1)
        product = sum(dot_bf16(change[:, : (row + 1) * TILE], part, NT) for part in pieces_of(strip))
        at = layout.scores + row * chains
        score = packed_ref[at : at + chains, :] - right[:, cols]
        total = total + value[:, cols] * (product - (score + score))
    final_ref[:, width:] = jnp.broadcast_to(jnp.sum(total, axis=1, keepdims=True), (chains, TILE))


def update_rows(block, core, own_ref, other_ref, shift, residual_ref, new_ref, x, sems):
    rows, half = own_ref.shape[1:]
    sources, places = [own_ref.at[block], other_ref.at[block]], [x.at[0], x.at[1]]
    start_copies(sources, places, sems, rows)
    mine = jnp.where(core == 0, shift[:, :half], shift[:, half:])
    theirs = jnp.where(core == 0, shift[:, half:], shift[:, :half])
    own_change, their_change = mine.astype(BF16), theirs.astype(BF16)
    for i, start in enumerate(range(0, rows, CHUNK)):
        size = min(CHUNK, rows - start)
        wait_copies(sources, places, sems, i, start, size)
        at = pl.ds(start, size)
        change = dot_bf16(own_change, x[0, at, :], NT) + dot_bf16(their_change, x[1, at, :], NT)
        new_ref[:, at] = residual_ref[:, at] - change
    return mine


def first_update_kernel(core_ref, own_ref, other_ref, here_ref, there_ref, residual_ref, new_ref, mine_ref, x, sems):
    core = core_ref[0]
    shift = jnp.where(core == 0, here_ref[...], there_ref[...])
    mine_ref[...] = update_rows(0, core, own_ref, other_ref, shift, residual_ref, new_ref, x, sems)


def last_update_kernel(
    layout, people, core_ref, own_ref, other_ref, here_ref, there_ref, residual_ref, effects_ref, first_ref, norm_ref,
    chi_ref, new_ref, new_effects_ref, draw_ref, x, sems
):
    core, width = core_ref[0], 2 * own_ref.shape[2]
    squares = norm_ref[...] + (here_ref[:, width:] + there_ref[:, width:])
    draw_ref[...] = squares.T[:1, :] / (people * chi_ref[...])
    shift = jnp.where(core == 1, here_ref[:, :width], there_ref[:, :width])
    mine = update_rows(1, core, own_ref, other_ref, shift, residual_ref, new_ref, x, sems)
    new_effects_ref[0] = effects_ref[0] + first_ref[...]
    new_effects_ref[1] = effects_ref[1] + mine


def update_call(kernel, out_shape, genotypes, name, *operands):
    rows, half = genotypes.shape[1:]
    return pl.pallas_call(
        kernel,
        out_shape=out_shape,
        in_specs=[SMEM, ANY, ANY] + [VMEM] * (len(operands) - 2),
        out_specs=(VMEM,) * len(out_shape),
        scratch_shapes=[
            pltpu.VMEM((2, rows, half), BF16),
            pltpu.SemaphoreType.DMA((-(-rows // CHUNK), 2)),
        ],
        compiler_params=PARAMS,
        cost_estimate=pl.CostEstimate(flops=64 * rows * half * 8, bytes_accessed=4 * rows * half, transcendentals=0),
        name=name,
    )(operands[0], genotypes, *operands[1:])


def line_sums(value, beside, spots):
    stride = 1
    while stride < spots:
        at = [i // stride % LINE for i in range(spots)]
        one, two, three = (
            lax.ppermute(value, "ind", [(i, i + ((at[i] + step) % LINE - at[i]) * stride) for i in range(spots)])
            for step in range(1, LINE)
        )
        if stride == 1:
            one, two, three, beside = lax.optimization_barrier((one, two, three, beside))
        even = lax.axis_index("ind") // stride % 2 == 0
        value = (value + jnp.where(even, three, one)) + (two + jnp.where(even, one, three))
        stride *= LINE
    return value, beside


def local(genotypes, residual, effects, noise, prior_var, block_snps, noise_var, chi_scaled):
    blocks, rows, half = genotypes.shape
    chains = residual.shape[0]
    width = 2 * half
    count = width // TILE
    spots = lax.axis_size("ind")
    core = lax.axis_index("snp")
    core_arg = jnp.reshape(core.astype(jnp.int32), (1,))
    swap = [(0, 1), (1, 0)]
    pieces = -(-rows // CHUNK)

    other = lax.ppermute(genotypes, "snp", swap)
    other_effects = lax.ppermute(effects, "snp", swap)

    layout = Layout(count, chains, spots)
    piece = layout.piece
    square, own_score, own_cross = pl.pallas_call(
        own_kernel,
        out_shape=(
            jax.ShapeDtypeStruct((half, half), F32),
            jax.ShapeDtypeStruct((chains, half), F32),
            jax.ShapeDtypeStruct((half, half), F32),
        ),
        in_specs=[SMEM, ANY, VMEM],
        out_specs=(VMEM,) * 3,
        scratch_shapes=[pltpu.VMEM((2, rows, half), BF16), pltpu.SemaphoreType.DMA((pieces, 2))],
        compiler_params=PARAMS,
        cost_estimate=pl.CostEstimate(flops=2 * rows * half * half, bytes_accessed=2 * rows * half, transcendentals=0),
        name="own",
    )(core_arg, genotypes, residual)
    packed = pl.pallas_call(
        functools.partial(gram_kernel, layout),
        out_shape=jax.ShapeDtypeStruct((spots * piece, TILE), F32),
        in_specs=[SMEM, ANY, ANY, VMEM, VMEM, VMEM],
        out_specs=VMEM,
        scratch_shapes=[
            pltpu.VMEM((rows, width), BF16),
            pltpu.VMEM((half, width), F32),
            pltpu.VMEM((chains, half), F32),
            pltpu.VMEM((chains, 1), F32),
            pltpu.SemaphoreType.DMA((pieces, 2)),
        ],
        compiler_params=PARAMS,
        cost_estimate=pl.CostEstimate(flops=0, bytes_accessed=0, transcendentals=0),
        name="gram",
    )(core_arg, genotypes, other, residual, square, own_score)
    late_other, packed = lax.optimization_barrier((other, packed))
    cross = pl.pallas_call(
        cross_kernel,
        out_shape=jax.ShapeDtypeStruct((2, half, half), F32),
        in_specs=[ANY, ANY, VMEM],
        out_specs=VMEM,
        scratch_shapes=[
            pltpu.VMEM((2, rows, half), BF16),
            pltpu.SemaphoreType.DMA((pieces, 2)),
        ],
        compiler_params=PARAMS,
        cost_estimate=pl.CostEstimate(flops=2 * rows * half * half, bytes_accessed=4 * rows * half, transcendentals=0),
        name="cross",
    )(genotypes, late_other, own_cross)
    packed = lax.all_to_all(packed.reshape(spots, piece, TILE), "ind", 0, 0)
    packed, cross = lax.optimization_barrier((packed, cross))
    packed = pl.pallas_call(
        sum_kernel,
        out_shape=jax.ShapeDtypeStruct(packed.shape, F32),
        in_specs=[ANY],
        out_specs=ANY,
        scratch_shapes=[
            pltpu.VMEM((spots, piece, TILE), F32),
            pltpu.VMEM((SUB, piece, TILE), F32),
            pltpu.SemaphoreType.DMA((spots // SUB,)),
            pltpu.SemaphoreType.DMA((spots // SUB,)),
        ],
        compiler_params=PARAMS,
        name="sums",
    )(packed)
    packed = lax.all_to_all(packed, "ind", 0, 0).reshape(spots * piece, TILE)

    own_effects = lax.dynamic_index_in_dim(effects, core, 0, keepdims=False)
    got_effects = lax.dynamic_index_in_dim(other_effects, core, 0, keepdims=False)
    block_effects = jnp.where(
        core == 0,
        jnp.concatenate([own_effects, got_effects], axis=1),
        jnp.concatenate([got_effects, own_effects], axis=1),
    )
    block_noise = lax.dynamic_index_in_dim(noise, core, 0, keepdims=False)
    block_rows = lax.dynamic_index_in_dim(block_snps.reshape(blocks, count, TILE), core, 0, keepdims=False)
    scale = jnp.sqrt(noise_var)[:, None]
    panels_shape = (panel_rows(width, width // STRIP - 1).start, STRIP)
    inverse_shape = (width // STRIP, STRIP, STRIP)
    panels, inverse, shift = pl.pallas_call(
        functools.partial(factor_kernel, layout),
        out_shape=(
            jax.ShapeDtypeStruct(panels_shape, F32),
            jax.ShapeDtypeStruct(inverse_shape, F32),
            jax.ShapeDtypeStruct((chains, width), F32),
        ),
        in_specs=[ANY] + [VMEM] * 5,
        out_specs=(ANY, ANY, VMEM),
        scratch_shapes=[
            pltpu.VMEM(packed.shape, F32),
            pltpu.VMEM(panels_shape, F32),
            pltpu.VMEM(inverse_shape, F32),
            pltpu.VMEM((width + chains, width), F32),
            pltpu.VMEM((SUB, TILE), F32),
            pltpu.SemaphoreType.DMA((5,)),
        ],
        compiler_params=PARAMS,
        cost_estimate=pl.CostEstimate(flops=0, bytes_accessed=0, transcendentals=0),
        name="factor",
    )(packed, prior_var.reshape(-1, TILE), block_rows, block_effects, block_noise, scale)

    got_shift = lax.ppermute(shift, "snp", swap)
    share = pl.pallas_call(
        cross_share_kernel,
        out_shape=jax.ShapeDtypeStruct((chains, half), F32),
        in_specs=[SMEM] + [VMEM] * 2 + [ANY],
        out_specs=VMEM,
        scratch_shapes=[pltpu.VMEM(cross.shape, F32), pltpu.SemaphoreType.DMA((2,))],
        compiler_params=PARAMS,
        name="cross_share",
    )(core_arg, shift, got_shift, cross)
    after_0, first_shift = update_call(
        first_update_kernel,
        (jax.ShapeDtypeStruct(residual.shape, F32), jax.ShapeDtypeStruct((chains, half), F32)),
        genotypes,
        "first_update",
        core_arg,
        other,
        shift,
        got_shift,
        residual,
    )
    share, after_0 = line_sums(share, after_0, spots)
    got = lax.ppermute(share, "snp", swap)
    final = pl.pallas_call(
        functools.partial(second_kernel, layout),
        out_shape=jax.ShapeDtypeStruct((chains, width + TILE), F32),
        in_specs=[SMEM] + [VMEM] * 3 + [ANY] * 3,
        out_specs=VMEM,
        scratch_shapes=[
            pltpu.VMEM(panels_shape, F32),
            pltpu.VMEM(inverse_shape, F32),
            pltpu.VMEM(packed.shape, F32),
            pltpu.SemaphoreType.DMA((3,)),
        ],
        compiler_params=PARAMS,
        name="second",
    )(core_arg, shift, share, got, panels, inverse, packed)
    got_final = lax.ppermute(final, "snp", swap)
    new_residual, new_effects, draw = update_call(
        functools.partial(last_update_kernel, layout, rows * spots),
        (
            jax.ShapeDtypeStruct(residual.shape, F32),
            jax.ShapeDtypeStruct(effects.shape, F32),
            jax.ShapeDtypeStruct((1, chains), F32),
        ),
        genotypes,
        "last_update",
        core_arg,
        other,
        final,
        got_final,
        after_0,
        effects,
        first_shift,
        packed[layout.squares : layout.used],
        chi_scaled[None, :],
    )
    return (new_effects, new_residual, draw[0])


def solution(mesh):
    placed = (P(None, "ind", "snp"), P(None, "ind"), P(None, None, "snp"), P(), P(), P(), P(), P())
    return jax.shard_map(
        local,
        mesh=mesh,
        in_specs=placed,
        out_specs=(P(None, None, "snp"), P(None, "ind"), P()),
        check_vma=False,
    )
```

```python
import functools

import jax
import jax.numpy as jnp
from jax import lax
from jax.experimental import pallas as pl
from jax.experimental.pallas import tpu as pltpu
from jax.sharding import PartitionSpec as P

F32 = jnp.float32
BF16 = jnp.bfloat16
TILE = 128
SUB = 8
STRIP = 256
CHUNK = 1024
LINE = 4
NT = (((1,), (1,)), ((), ()))
NN = (((1,), (0,)), ((), ()))
TN = (((0,), (0,)), ((), ()))
VMEM = pl.BlockSpec(memory_space=pltpu.VMEM)
SMEM = pl.BlockSpec(memory_space=pltpu.SMEM)
ANY = pl.BlockSpec(memory_space=pl.ANY)
PARAMS = pltpu.CompilerParams(vmem_limit_bytes=52 * 2**20)


def dot_exact(left, right, dims):
    return lax.dot_general(
        left, right, dims, preferred_element_type=F32, precision=lax.Precision.HIGHEST
    )


def dot_bf16(left, right, dims):
    return lax.dot_general(left, right, dims, preferred_element_type=F32)


def spread(row):
    return jnp.broadcast_to(row, (SUB, TILE))


def pieces_of(value):
    high = value.astype(BF16)
    rest = value - high.astype(F32)
    middle = rest.astype(BF16)
    return high, middle, (rest - middle.astype(F32)).astype(BF16)


def dot_rows(left, right, dims):
    rows = left.shape[0]
    parts = pieces_of(left)
    high, middle, low = pieces_of(right)
    one = dot_bf16(jnp.concatenate(parts, axis=0), high, dims)
    two = dot_bf16(jnp.concatenate(parts[:2], axis=0), middle, dims)
    three = dot_bf16(parts[0], low, dims)
    return one[:rows] + ((one[rows : 2 * rows] + two[:rows]) + (one[2 * rows :] + two[rows:] + three))


def dot_narrow(left, right):
    high, middle, low = pieces_of(left)
    right_high, right_middle, right_low = pieces_of(right)
    columns = right.shape[0]
    both = jnp.concatenate([jnp.concatenate([part, part], axis=1) for part in (right_high, right_middle)], axis=0)
    one = dot_bf16(jnp.concatenate([high, middle], axis=1), both, NT)
    two = dot_bf16(jnp.concatenate([high, low], axis=1), jnp.concatenate([right_low, right_high], axis=1), NT)
    return one[:, :columns] + (one[:, columns:] + two)


def tree_sum(terms):
    while len(terms) > 1:
        terms = [terms[i] + terms[i + 1] if i + 1 < len(terms) else terms[i] for i in range(0, len(terms), 2)]
    return terms[0]


def inverse_factor(tile, zero):
    groups = TILE // SUB
    sub = lax.broadcasted_iota(jnp.int32, (SUB, TILE), 0)
    lane = lax.broadcasted_iota(jnp.int32, (SUB, TILE), 1)
    left = [tile[SUB * r : SUB * r + SUB, :] for r in range(groups)]
    done = []
    pivot_cols = [spread(left[0][:, j : j + 1]) + zero for j in range(SUB)]
    for g in range(groups):
        first, after = g * SUB, (g + 1) * SUB
        last = g + 1 == groups
        inside = (lane >= first) & (lane < after)
        near = [] if last else [spread(left[g + 1][:, first + j : first + j + 1]) for j in range(SUB)]
        coming = [] if last else [spread(left[g + 1][:, after + j : after + j + 1]) + zero for j in range(SUB)]
        cols = [[spread(left[r][:, first + j : first + j + 1]) for r in range(g + 2, groups)] for j in range(SUB)]
        square = {(i, j): spread(pivot_cols[j][i : i + 1, :]) for j in range(SUB) for i in range(j + 1)}
        own = jnp.where(inside, jnp.where(lane == sub + first, 1.0, 0.0), left[g])
        rows = [spread(own[j : j + 1, :]) for j in range(SUB)]
        near_terms = []
        near_solved = []
        share = {}
        solved = [None] * SUB
        pivots = jnp.zeros((SUB, TILE), F32)
        finished = pivots
        for j in range(0, SUB, 2):
            p, q, r = square[j, j], square[j, j + 1], square[j + 1, j + 1]
            minor = p * r - q * q
            over_minor = pltpu.reciprocal(minor, approx=True)
            over_p = pltpu.reciprocal(p, approx=True)
            ip, iq, ir = r * over_minor, -q * over_minor, p * over_minor
            pivots = jnp.where(sub == j, p, jnp.where(sub == j + 1, minor * over_p, pivots))
            second_row = rows[j + 1] - (q * over_p) * rows[j]
            finished = jnp.where(sub == j, rows[j], jnp.where(sub == j + 1, second_row, finished))
            for k in range(j + 2, SUB):
                upper, lower = square[j, k], square[j + 1, k]
                share[j, k], share[j + 1, k] = upper * ip + lower * iq, upper * iq + lower * ir
            for k in range(j + 2, SUB):
                one, two = share[j, k], share[j + 1, k]
                for i in range(j + 2, k + 1):
                    square[i, k] = square[i, k] - (square[j, i] * one + square[j + 1, i] * two)
                rows[k] = rows[k] - (rows[j] * one + rows[j + 1] * two)
                if not last:
                    near[k] = near[k] - (near[j] * one + near[j + 1] * two)
            solved[j], solved[j + 1] = rows[j] * ip + rows[j + 1] * iq, rows[j] * iq + rows[j + 1] * ir
            if not last:
                near_solved += [near[j] * ip + near[j + 1] * iq, near[j] * iq + near[j + 1] * ir]
                near_terms.append(near[j] * solved[j] + near[j + 1] * solved[j + 1])
        if not last:
            pivot_cols = [
                coming[j] - tree_sum([near[k] * spread(near_solved[k][j : j + 1, :]) for k in range(SUB)])
                for j in range(SUB)
            ]
            left[g + 1] = jnp.where(inside, 0.0, left[g + 1]) - tree_sum(near_terms)
        for j in (4, 5, 2, 3, 0, 1):
            solved[j] = solved[j] - tree_sum([share[j, k] * solved[k] for k in range(j // 2 * 2 + 2, SUB)])
        for r in range(g + 2, groups):
            left[r] = jnp.where(inside, 0.0, left[r]) - tree_sum([cols[j][r - g - 2] * solved[j] for j in range(SUB)])
        root = lax.rsqrt(pivots)
        root = root * (1.5 - 0.5 * pivots * root * root)
        done.append(jnp.where(lane < after, finished * root, 0.0))
    return jnp.concatenate(done, axis=0)


def split_scores(residual, x):
    chains = residual.shape[0]
    high, middle, _ = pieces_of(residual)
    both = dot_bf16(jnp.concatenate([high, middle], axis=0), x, NN)
    return both[:chains] + both[chains:]


def chunk_loop(rows, body):
    whole = rows // CHUNK

    @pl.loop(0, whole)
    def _(i):
        body(i, pl.multiple_of(i * CHUNK, CHUNK), CHUNK)

    if rows % CHUNK:
        body(whole, whole * CHUNK, rows % CHUNK)


def start_copies(sources, places, sems, rows):
    for i, lo in enumerate(range(0, rows, CHUNK)):
        at = pl.ds(lo, min(CHUNK, rows - lo))
        for k, (source, place) in enumerate(zip(sources, places)):
            pltpu.make_async_copy(source.at[at, :], place.at[at, :], sems.at[i, k]).start()


def wait_copies(sources, places, sems, i, start, size):
    at = pl.ds(start, size)
    for k, (source, place) in enumerate(zip(sources, places)):
        pltpu.make_async_copy(source.at[at, :], place.at[at, :], sems.at[i, k]).wait()


def own_kernel(core_ref, own_ref, residual_ref, square_ref, score_ref, cross_ref, mine, sems):
    core = core_ref[0]
    rows, half = own_ref.shape[1:]
    sources, places = [own_ref.at[0], own_ref.at[1]], [mine.at[0], mine.at[1]]
    start_copies(sources, places, sems, rows)
    for ref in (square_ref, score_ref, cross_ref):
        ref[...] = jnp.zeros_like(ref)

    def body(i, start, size):
        wait_copies(sources, places, sems, i, start, size)
        at = pl.ds(start, size)
        score_ref[...] += split_scores(residual_ref[:, at], mine[core, at, :])
        cross_ref[...] += dot_bf16(mine[0, at, :], mine[1, at, :], TN)
        for c in range(0, half, STRIP):
            square_ref[c:, c : c + STRIP] += dot_bf16(mine[core, at, c:], mine[core, at, c : c + STRIP], TN)

    chunk_loop(rows, body)


class Layout:
    def __init__(self, count, chains, spots):
        self.count, self.chains = count, chains
        self.pairs = count * (count - 1) // 2 * TILE
        self.diagonals = self.pairs + count // 2 * TILE
        self.scores = self.diagonals + SUB
        self.squares = self.scores + count * chains
        self.used = self.squares + chains
        self.piece = -(-self.used // (spots * SUB)) * SUB
        self.rows = self.piece * spots

    def lower(self, row, col):
        return (row * (row - 1) // 2 + col) * TILE


def put_diagonal(packed_ref, layout, half_at, block):
    count = layout.count // 2
    row_id = lax.broadcasted_iota(jnp.int32, (TILE, TILE), 0)
    col_id = lax.broadcasted_iota(jnp.int32, (TILE, TILE), 1)
    for r in range(count):
        for c in range(r):
            row, col = half_at * count + r, half_at * count + c
            at = pl.multiple_of((lax.shift_right_logical(row * (row - 1), 1) + col) * TILE, TILE)
            packed_ref[pl.ds(at, TILE), :] = block[r * TILE : r * TILE + TILE, c * TILE : c * TILE + TILE]
    for r in range(0, count, 2):
        one = block[r * TILE : r * TILE + TILE, r * TILE : r * TILE + TILE]
        two = block[(r + 1) * TILE : (r + 2) * TILE, (r + 1) * TILE : (r + 2) * TILE]
        place = half_at * (count // 2) + r // 2
        at = pl.multiple_of(layout.pairs + place * TILE, TILE)
        packed_ref[pl.ds(at, TILE), :] = jnp.where(row_id > col_id, one, two)
        packed_ref[pl.ds(layout.diagonals + place, 1), :] = jnp.sum(
            jnp.where(row_id == col_id, one, 0.0), axis=0, keepdims=True
        )


def get_diagonal(packed_ref, layout, tile):
    row_id = lax.broadcasted_iota(jnp.int32, (TILE, TILE), 0)
    col_id = lax.broadcasted_iota(jnp.int32, (TILE, TILE), 1)
    at = layout.pairs + tile // 2 * TILE
    pair = packed_ref[at : at + TILE, :]
    if tile % 2:
        return jnp.where(row_id < col_id, pair, 0.0), jnp.where(row_id == col_id, pair, 0.0)
    row = layout.diagonals + tile // 2
    return jnp.where(row_id > col_id, pair, 0.0), jnp.where(row_id == col_id, packed_ref[row : row + 1, :], 0.0)


def gram_kernel(
    layout, core_ref, own_ref, other_ref, residual_ref, square_ref, own_score_ref, packed_ref, x, total, score, norm, sems
):
    core = core_ref[0]
    rows, half = own_ref.shape[1:]
    sources = [own_ref.at[core], other_ref.at[core]]
    places = [x.at[:, :half], x.at[:, half:]]
    start_copies(sources, places, sems, rows)
    for ref in (total, score, norm):
        ref[...] = jnp.zeros_like(ref)

    def body(i, start, size):
        wait_copies(sources, places, sems, i, start, size)
        at = pl.ds(start, size)
        total[...] += dot_bf16(x[at, half:], x[at, :], TN)
        score[...] += split_scores(residual_ref[:, at], x[at, half:])
        norm[...] += jnp.sum(jnp.square(residual_ref[:, at]), axis=1, keepdims=True)

    chunk_loop(rows, body)
    count, chains = layout.count, layout.chains
    put_diagonal(packed_ref, layout, core, square_ref)
    put_diagonal(packed_ref, layout, 1 - core, total.at[:, half:])
    below = [(r, c, layout.lower(count // 2 + r, c)) for r in range(count // 2) for c in range(count // 2)]

    @pl.when(core == 0)
    def _():
        for r, c, at in below:
            packed_ref[at : at + TILE, :] = total[r * TILE : r * TILE + TILE, c * TILE : c * TILE + TILE]

    @pl.when(core == 1)
    def _():
        for r, c, at in below:
            packed_ref[at : at + TILE, :] = total[c * TILE : c * TILE + TILE, r * TILE : r * TILE + TILE].T

    for k, part in ((core, own_score_ref), (1 - core, score)):
        for col in range(count // 2):
            start_row = pl.multiple_of(layout.scores + (k * (count // 2) + col) * chains, SUB)
            packed_ref[pl.ds(start_row, chains), :] = part[:, col * TILE : col * TILE + TILE]
    packed_ref[layout.squares : layout.used, :] = jnp.broadcast_to(norm[...], (chains, TILE))
    packed_ref[layout.used :, :] = jnp.zeros((layout.rows - layout.used, TILE), F32)


def sum_kernel(parts_ref, sums_ref, parts, copies, in_sems, out_sems):
    count, each = parts.shape[0], copies.shape[0]
    moves = [
        pltpu.make_async_copy(parts_ref.at[i : i + each], parts.at[i : i + each], in_sems.at[i // each])
        for i in range(0, count, each)
    ]
    for move in moves:
        move.start()
    total = None
    for i, move in enumerate(moves):
        move.wait()
        group = tree_sum([parts[i * each + j] for j in range(each)])
        total = group if total is None else total + group
    for i in range(each):
        copies[i] = total
    moves = [
        pltpu.make_async_copy(copies, sums_ref.at[i : i + each], out_sems.at[i // each]) for i in range(0, count, each)
    ]
    for move in moves:
        move.start()
    for move in moves:
        move.wait()


def cross_kernel(own_ref, other_ref, own_cross_ref, cross_ref, x, sems):
    rows = own_ref.shape[1]
    sources, places = [other_ref.at[0], own_ref.at[1]], [x.at[0], x.at[1]]
    start_copies(sources, places, sems, rows)
    cross_ref[0] = own_cross_ref[...]
    cross_ref[1] = jnp.zeros(own_cross_ref.shape, F32)

    def body(i, start, size):
        wait_copies(sources, places, sems, i, start, size)
        at = pl.ds(start, size)
        cross_ref[1] += dot_bf16(x[0, at, :], x[1, at, :], TN)

    chunk_loop(rows, body)


def panel_rows(width, k):
    start = sum(width - j * STRIP for j in range(1, k + 1))
    return slice(start, start + width - (k + 1) * STRIP)


def backward(moved, panels_ref, inverse_ref):
    width = len(moved) * STRIP
    solved = [None] * len(moved)
    for k in reversed(range(len(moved))):
        solved[k] = dot_rows(moved[k], inverse_ref[k], NN)
        if k:
            for j in range(k):
                at = panel_rows(width, j).start + (k - j - 1) * STRIP
                moved[j] = moved[j] - dot_rows(solved[k], panels_ref[at : at + STRIP, :], NN)
    return solved


def factor_kernel(
    layout, packed_hbm, prior_ref, rows_ref, effects_ref, noise_ref, scale_ref, panels_hbm, inverse_hbm, shift_ref,
    packed_ref, panels_ref, inverse_ref, factor_ref, zero_ref, sems
):
    width = factor_ref.shape[1]
    count = width // TILE
    chains = effects_ref.shape[0]
    halfway = layout.lower(count * 3 // 4, 0)
    parts = [slice(0, halfway), slice(halfway, layout.pairs), slice(layout.pairs, layout.rows)]
    arrivals = [pltpu.make_async_copy(packed_hbm.at[at], packed_ref.at[at], sems.at[i]) for i, at in enumerate(parts)]
    for arrival in arrivals:
        arrival.start()
    table_rows = rows_ref[...]
    high = lax.shift_right_logical(table_rows, 7)
    low = lax.bitwise_and(table_rows, TILE - 1)
    prior = jnp.zeros((count, TILE), F32)
    for t in range(prior_ref.shape[0]):
        entry = jnp.broadcast_to(prior_ref[t : t + 1, :], (count, TILE))
        prior = jnp.where(high == t, jnp.take_along_axis(entry, low, axis=1), prior)
    inverse_prior = 1.0 / prior
    diagonal = lax.broadcasted_iota(jnp.int32, (TILE, TILE), 0) == lax.broadcasted_iota(jnp.int32, (TILE, TILE), 1)
    for row in range(count):
        rows = slice(row * TILE, row * TILE + TILE)
        if row in (0, count * 3 // 4):
            arrivals[0 if row == 0 else 1].wait()
        for col in range(row):
            at = layout.lower(row, col)
            factor_ref[rows, col * TILE : col * TILE + TILE] = packed_ref[at : at + TILE, :]
    arrivals[2].wait()
    for row in range(count):
        rows = slice(row * TILE, row * TILE + TILE)
        triangle, middle = get_diagonal(packed_ref, layout, row)
        middle = middle + jnp.where(diagonal, inverse_prior[row : row + 1, :], 0.0)
        factor_ref[rows, rows] = triangle + triangle.T + middle
        at = layout.scores + row * chains
        factor_ref[width : width + chains, rows] = (
            packed_ref[at : at + chains, :] - inverse_prior[row : row + 1, :] * effects_ref[:, rows]
        )
    zero_ref[...] = jnp.zeros_like(zero_ref)

    @pl.loop(0, count)
    def _(k):
        at = pl.multiple_of(k * TILE, TILE)
        pair, side = lax.shift_right_logical(k, 1), pl.ds(pl.multiple_of(lax.bitwise_and(k, 1) * TILE, TILE), TILE)
        inverse_ref[pair, side, side] = inverse_factor(factor_ref[pl.ds(at, TILE), pl.ds(at, TILE)], zero_ref[...])
        for step in range(count):

            @pl.when(k == step)
            def _():
                lo, hi = step * TILE, (step + 1) * TILE
                side = slice(step % 2 * TILE, step % 2 * TILE + TILE)
                inverse = inverse_ref[step // 2, side, side]
                factor_ref[hi:, lo:hi] = dot_narrow(factor_ref[hi:, lo:hi], inverse)
                if step % 2 == 0:
                    panel = factor_ref[hi:, lo:hi]
                    factor_ref[hi:, hi : hi + TILE] = factor_ref[hi:, hi : hi + TILE] - dot_narrow(panel, panel[:TILE, :])
                else:
                    for c in range(hi, width, STRIP):
                        panel = factor_ref[c:, lo - TILE : hi]
                        factor_ref[c:, c : c + STRIP] = factor_ref[c:, c : c + STRIP] - dot_exact(
                            panel, panel[:STRIP, :], NT
                        )
                    below = dot_exact(factor_ref[lo:hi, lo - TILE : lo], inverse_ref[step // 2, :TILE, :TILE], NN)
                    inverse_ref[step // 2, TILE:, :TILE] = -dot_exact(inverse, below, NN)
                    inverse_ref[step // 2, :TILE, TILE:] = jnp.zeros((TILE, TILE), F32)

    scale = scale_ref[...]
    moved = [
        factor_ref[width : width + chains, j : j + STRIP] + scale * noise_ref[:, j : j + STRIP]
        for j in range(0, width, STRIP)
    ]
    for k in range(width // STRIP - 1):
        panels_ref[panel_rows(width, k), :] = factor_ref[(k + 1) * STRIP : width, k * STRIP : (k + 1) * STRIP]
    departures = [
        pltpu.make_async_copy(panels_ref, panels_hbm, sems.at[3]),
        pltpu.make_async_copy(inverse_ref, inverse_hbm, sems.at[4]),
    ]
    for departure in departures:
        departure.start()
    for j, part in enumerate(backward(moved, panels_ref, inverse_ref)):
        shift_ref[:, j * STRIP : j * STRIP + STRIP] = part
    for departure in departures:
        departure.wait()


def cross_share_kernel(core_ref, shift_ref, got_ref, cross_hbm, share_ref, cross_ref, sems):
    core = core_ref[0]
    half = cross_ref.shape[1]
    arrivals = [pltpu.make_async_copy(cross_hbm.at[i], cross_ref.at[i], sems.at[i]) for i in range(2)]
    for arrival in arrivals:
        arrival.start()
    shift = jnp.where(core == 0, shift_ref[...], got_ref[...])
    change = shift.astype(BF16)
    first, last = change[:, :half], change[:, half:]
    mine = jnp.where(core == 0, first, last)
    theirs = jnp.where(core == 0, last, first)
    total = None
    for i, part in enumerate((mine, theirs)):
        arrivals[i].wait()
        product = sum(dot_bf16(part, piece, NN) for piece in pieces_of(cross_ref[i]))
        total = product if total is None else total + product
    share_ref[...] = total


def second_kernel(
    layout, core_ref, shift_ref, share_ref, got_ref, panels_hbm, inverse_hbm, packed_hbm, final_ref,
    panels_ref, inverse_ref, packed_ref, sems
):
    width, count, chains = shift_ref.shape[1], layout.count, layout.chains
    pairs = ((inverse_hbm, inverse_ref), (panels_hbm, panels_ref), (packed_hbm, packed_ref))
    arrivals = [pltpu.make_async_copy(source, place, sems.at[i]) for i, (source, place) in enumerate(pairs)]
    for arrival in arrivals:
        arrival.start()
    keep = jnp.where(core_ref[0] == 1, 1.0, 0.0)
    right = jnp.concatenate([got_ref[...], share_ref[...]], axis=1) * keep
    moved = [right[:, j : j + STRIP] for j in range(0, width, STRIP)]
    arrivals[0].wait()
    for k in range(len(moved)):
        moved[k] = dot_rows(moved[k], inverse_ref[k], NT)
        if k == 0:
            arrivals[1].wait()
        lo = (k + 1) * STRIP
        if lo < width:
            change_by = dot_rows(moved[k], panels_ref[panel_rows(width, k), :], NT)
            for j in range(k + 1, len(moved)):
                moved[j] = moved[j] - change_by[:, (j - k - 1) * STRIP : (j - k) * STRIP]
    for j, part in enumerate(backward(moved, panels_ref, inverse_ref)):
        cols = slice(j * STRIP, j * STRIP + STRIP)
        final_ref[:, cols] = shift_ref[:, cols] - part
    change = final_ref[:, :width].astype(BF16)
    value = change.astype(F32)
    total = jnp.zeros((chains, TILE), F32)
    arrivals[2].wait()
    for row in range(count):
        cols = slice(row * TILE, row * TILE + TILE)
        triangle, middle = get_diagonal(packed_ref, layout, row)
        tiles = [packed_ref[layout.lower(row, col) : layout.lower(row, col) + TILE, :] for col in range(row)]
        strip = jnp.concatenate([tile + tile for tile in tiles] + [triangle + triangle + middle], axis=1)
        product = sum(dot_bf16(change[:, : (row + 1) * TILE], part, NT) for part in pieces_of(strip))
        at = layout.scores + row * chains
        score = packed_ref[at : at + chains, :] - right[:, cols]
        total = total + value[:, cols] * (product - (score + score))
    final_ref[:, width:] = jnp.broadcast_to(jnp.sum(total, axis=1, keepdims=True), (chains, TILE))


def halves(shift, core):
    half = shift.shape[1] // 2
    first, last = shift[:, :half], shift[:, half:]
    return jnp.where(core == 0, first, last), jnp.where(core == 0, last, first)


def update_rows(block, rows, own_ref, other_ref, changes, get, put, x, sems):
    chunks = [(lo, min(lo + CHUNK, rows[1])) for lo in range(rows[0], rows[1], CHUNK)]
    copies = []
    for i, (lo, hi) in enumerate(chunks):
        pair = [
            pltpu.make_async_copy(
                source.at[block, lo:hi, :], x.at[k, lo - rows[0] : hi - rows[0], :], sems.at[i, k]
            )
            for k, source in enumerate((own_ref, other_ref))
        ]
        for copy in pair:
            copy.start()
        copies.append(pair)
    own_change, their_change = (change.astype(BF16) for change in changes())
    for i, (lo, hi) in enumerate(chunks):
        for copy in copies[i]:
            copy.wait()
        at = slice(lo - rows[0], hi - rows[0])
        put(lo, hi, get(lo, hi) - (dot_bf16(own_change, x[0, at, :], NT) + dot_bf16(their_change, x[1, at, :], NT)))


def first_update_kernel(rows, core_ref, own_ref, other_ref, here_ref, there_ref, residual_ref, new_ref, x, sems):
    core = core_ref[0]

    def put(lo, hi, value):
        new_ref[:, lo - rows[0] : hi - rows[0]] = value

    update_rows(
        0, rows, own_ref, other_ref, lambda: halves(jnp.where(core == 0, here_ref[...], there_ref[...]), core),
        lambda lo, hi: residual_ref[:, lo:hi], put, x, sems,
    )


def last_update_kernel(
    layout, people, cut, core_ref, own_ref, other_ref, here_ref, there_ref, low_ref, high_ref, effects_ref,
    first_here_ref, first_there_ref, norm_ref, chi_ref, new_ref, new_effects_ref, draw_ref, x, sems
):
    core, width = core_ref[0], 2 * own_ref.shape[2]

    def changes():
        mine, theirs = halves(jnp.where(core == 1, here_ref[:, :width], there_ref[:, :width]), core)
        new_effects_ref[1] = effects_ref[1] + mine
        return mine, theirs

    def get(lo, hi):
        return low_ref[:, lo:hi] if lo < cut else high_ref[:, lo - cut : hi - cut]

    def put(lo, hi, value):
        new_ref[:, lo:hi] = value

    update_rows(1, (0, own_ref.shape[1]), own_ref, other_ref, changes, get, put, x, sems)
    first = halves(jnp.where(core == 0, first_here_ref[...], first_there_ref[...]), core)[0]
    new_effects_ref[0] = effects_ref[0] + first
    squares = norm_ref[...] + (here_ref[:, width:] + there_ref[:, width:])
    draw_ref[...] = squares.T[:1, :] / (people * chi_ref[...])


def update_call(kernel, out_shape, rows, genotypes, name, *operands):
    half = genotypes.shape[2]
    return pl.pallas_call(
        kernel,
        out_shape=out_shape,
        in_specs=[SMEM, ANY, ANY] + [VMEM] * (len(operands) - 2),
        out_specs=(VMEM,) * len(out_shape),
        scratch_shapes=[
            pltpu.VMEM((2, rows, half), BF16),
            pltpu.SemaphoreType.DMA((-(-rows // CHUNK), 2)),
        ],
        compiler_params=PARAMS,
        cost_estimate=pl.CostEstimate(flops=64 * rows * half * 8, bytes_accessed=4 * rows * half, transcendentals=0),
        name=name,
    )(operands[0], genotypes, *operands[1:])


def line_sums(value, beside, spots):
    stride = 1
    beside = list(beside)
    ready = []
    while stride < spots:
        at = [i // stride % LINE for i in range(spots)]
        one, two, three = (
            lax.ppermute(value, "ind", [(i, i + ((at[i] + step) % LINE - at[i]) * stride) for i in range(spots)])
            for step in range(1, LINE)
        )
        if beside:
            one, two, three, done = lax.optimization_barrier((one, two, three, beside.pop(0)))
            ready.append(done)
        even = lax.axis_index("ind") // stride % 2 == 0
        value = (value + jnp.where(even, three, one)) + (two + jnp.where(even, one, three))
        stride *= LINE
    return value, ready + beside


def local(genotypes, residual, effects, noise, prior_var, block_snps, noise_var, chi_scaled):
    blocks, rows, half = genotypes.shape
    chains = residual.shape[0]
    width = 2 * half
    count = width // TILE
    spots = lax.axis_size("ind")
    core = lax.axis_index("snp")
    core_arg = jnp.reshape(core.astype(jnp.int32), (1,))
    swap = [(0, 1), (1, 0)]
    pieces = -(-rows // CHUNK)

    other = lax.ppermute(genotypes, "snp", swap)
    other_effects = lax.ppermute(effects, "snp", swap)

    layout = Layout(count, chains, spots)
    piece = layout.piece
    square, own_score, own_cross = pl.pallas_call(
        own_kernel,
        out_shape=(
            jax.ShapeDtypeStruct((half, half), F32),
            jax.ShapeDtypeStruct((chains, half), F32),
            jax.ShapeDtypeStruct((half, half), F32),
        ),
        in_specs=[SMEM, ANY, VMEM],
        out_specs=(VMEM,) * 3,
        scratch_shapes=[pltpu.VMEM((2, rows, half), BF16), pltpu.SemaphoreType.DMA((pieces, 2))],
        compiler_params=PARAMS,
        cost_estimate=pl.CostEstimate(flops=2 * rows * half * half, bytes_accessed=2 * rows * half, transcendentals=0),
        name="own",
    )(core_arg, genotypes, residual)
    packed = pl.pallas_call(
        functools.partial(gram_kernel, layout),
        out_shape=jax.ShapeDtypeStruct((spots * piece, TILE), F32),
        in_specs=[SMEM, ANY, ANY, VMEM, VMEM, VMEM],
        out_specs=VMEM,
        scratch_shapes=[
            pltpu.VMEM((rows, width), BF16),
            pltpu.VMEM((half, width), F32),
            pltpu.VMEM((chains, half), F32),
            pltpu.VMEM((chains, 1), F32),
            pltpu.SemaphoreType.DMA((pieces, 2)),
        ],
        compiler_params=PARAMS,
        cost_estimate=pl.CostEstimate(flops=0, bytes_accessed=0, transcendentals=0),
        name="gram",
    )(core_arg, genotypes, other, residual, square, own_score)
    late_other, packed = lax.optimization_barrier((other, packed))
    cross = pl.pallas_call(
        cross_kernel,
        out_shape=jax.ShapeDtypeStruct((2, half, half), F32),
        in_specs=[ANY, ANY, VMEM],
        out_specs=VMEM,
        scratch_shapes=[
            pltpu.VMEM((2, rows, half), BF16),
            pltpu.SemaphoreType.DMA((pieces, 2)),
        ],
        compiler_params=PARAMS,
        cost_estimate=pl.CostEstimate(flops=2 * rows * half * half, bytes_accessed=4 * rows * half, transcendentals=0),
        name="cross",
    )(genotypes, late_other, own_cross)
    packed = lax.all_to_all(packed.reshape(spots, piece, TILE), "ind", 0, 0)
    packed, cross = lax.optimization_barrier((packed, cross))
    packed = pl.pallas_call(
        sum_kernel,
        out_shape=jax.ShapeDtypeStruct(packed.shape, F32),
        in_specs=[ANY],
        out_specs=ANY,
        scratch_shapes=[
            pltpu.VMEM((spots, piece, TILE), F32),
            pltpu.VMEM((SUB, piece, TILE), F32),
            pltpu.SemaphoreType.DMA((spots // SUB,)),
            pltpu.SemaphoreType.DMA((spots // SUB,)),
        ],
        compiler_params=PARAMS,
        name="sums",
    )(packed)
    packed = lax.all_to_all(packed, "ind", 0, 0).reshape(spots * piece, TILE)

    own_effects = lax.dynamic_index_in_dim(effects, core, 0, keepdims=False)
    got_effects = lax.dynamic_index_in_dim(other_effects, core, 0, keepdims=False)
    block_effects = jnp.where(
        core == 0,
        jnp.concatenate([own_effects, got_effects], axis=1),
        jnp.concatenate([got_effects, own_effects], axis=1),
    )
    block_noise = lax.dynamic_index_in_dim(noise, core, 0, keepdims=False)
    block_rows = lax.dynamic_index_in_dim(block_snps.reshape(blocks, count, TILE), core, 0, keepdims=False)
    scale = jnp.sqrt(noise_var)[:, None]
    panels_shape = (panel_rows(width, width // STRIP - 1).start, STRIP)
    inverse_shape = (width // STRIP, STRIP, STRIP)
    panels, inverse, shift = pl.pallas_call(
        functools.partial(factor_kernel, layout),
        out_shape=(
            jax.ShapeDtypeStruct(panels_shape, F32),
            jax.ShapeDtypeStruct(inverse_shape, F32),
            jax.ShapeDtypeStruct((chains, width), F32),
        ),
        in_specs=[ANY] + [VMEM] * 5,
        out_specs=(ANY, ANY, VMEM),
        scratch_shapes=[
            pltpu.VMEM(packed.shape, F32),
            pltpu.VMEM(panels_shape, F32),
            pltpu.VMEM(inverse_shape, F32),
            pltpu.VMEM((width + chains, width), F32),
            pltpu.VMEM((SUB, TILE), F32),
            pltpu.SemaphoreType.DMA((5,)),
        ],
        compiler_params=PARAMS,
        cost_estimate=pl.CostEstimate(flops=0, bytes_accessed=0, transcendentals=0),
        name="factor",
    )(packed, prior_var.reshape(-1, TILE), block_rows, block_effects, block_noise, scale)

    got_shift = lax.ppermute(shift, "snp", swap)
    share = pl.pallas_call(
        cross_share_kernel,
        out_shape=jax.ShapeDtypeStruct((chains, half), F32),
        in_specs=[SMEM] + [VMEM] * 2 + [ANY],
        out_specs=VMEM,
        scratch_shapes=[pltpu.VMEM(cross.shape, F32), pltpu.SemaphoreType.DMA((2,))],
        compiler_params=PARAMS,
        name="cross_share",
    )(core_arg, shift, got_shift, cross)
    cut = rows // 2 // CHUNK * CHUNK + CHUNK if rows > CHUNK else rows
    after = [
        update_call(
            functools.partial(first_update_kernel, part),
            (jax.ShapeDtypeStruct((chains, part[1] - part[0]), F32),),
            part[1] - part[0],
            genotypes,
            "first_update",
            core_arg,
            other,
            shift,
            got_shift,
            residual,
        )[0]
        for part in ((0, cut), (cut, rows))
    ]
    share, after = line_sums(share, after, spots)
    got = lax.ppermute(share, "snp", swap)
    final = pl.pallas_call(
        functools.partial(second_kernel, layout),
        out_shape=jax.ShapeDtypeStruct((chains, width + TILE), F32),
        in_specs=[SMEM] + [VMEM] * 3 + [ANY] * 3,
        out_specs=VMEM,
        scratch_shapes=[
            pltpu.VMEM(panels_shape, F32),
            pltpu.VMEM(inverse_shape, F32),
            pltpu.VMEM(packed.shape, F32),
            pltpu.SemaphoreType.DMA((3,)),
        ],
        compiler_params=PARAMS,
        name="second",
    )(core_arg, shift, share, got, panels, inverse, packed)
    got_final = lax.ppermute(final, "snp", swap)
    new_residual, new_effects, draw = update_call(
        functools.partial(last_update_kernel, layout, rows * spots, cut),
        (
            jax.ShapeDtypeStruct(residual.shape, F32),
            jax.ShapeDtypeStruct(effects.shape, F32),
            jax.ShapeDtypeStruct((1, chains), F32),
        ),
        rows,
        genotypes,
        "last_update",
        core_arg,
        other,
        final,
        got_final,
        *after,
        effects,
        shift,
        got_shift,
        packed[layout.squares : layout.used],
        chi_scaled[None, :],
    )
    return (new_effects, new_residual, draw[0])


def solution(mesh):
    placed = (P(None, "ind", "snp"), P(None, "ind"), P(None, None, "snp"), P(), P(), P(), P(), P())
    return jax.shard_map(
        local,
        mesh=mesh,
        in_specs=placed,
        out_specs=(P(None, None, "snp"), P(None, "ind"), P()),
        check_vma=False,
    )
```

```python
import functools

import jax
import jax.numpy as jnp
from jax import lax
from jax.experimental import pallas as pl
from jax.experimental.pallas import tpu as pltpu
from jax.sharding import PartitionSpec as P

F32 = jnp.float32
BF16 = jnp.bfloat16
TILE = 128
SUB = 8
STRIP = 256
CHUNK = 1024
LINE = 4
NT = (((1,), (1,)), ((), ()))
NN = (((1,), (0,)), ((), ()))
TN = (((0,), (0,)), ((), ()))
VMEM = pl.BlockSpec(memory_space=pltpu.VMEM)
SMEM = pl.BlockSpec(memory_space=pltpu.SMEM)
ANY = pl.BlockSpec(memory_space=pl.ANY)
PARAMS = pltpu.CompilerParams(vmem_limit_bytes=52 * 2**20)


def dot_exact(left, right, dims):
    return lax.dot_general(
        left, right, dims, preferred_element_type=F32, precision=lax.Precision.HIGHEST
    )


def dot_bf16(left, right, dims):
    return lax.dot_general(left, right, dims, preferred_element_type=F32)


def spread(row):
    return jnp.broadcast_to(row, (SUB, TILE))


def pieces_of(value):
    high = value.astype(BF16)
    rest = value - high.astype(F32)
    middle = rest.astype(BF16)
    return high, middle, (rest - middle.astype(F32)).astype(BF16)


def dot_rows(left, right, dims):
    rows = left.shape[0]
    parts = pieces_of(left)
    high, middle, low = pieces_of(right)
    one = dot_bf16(jnp.concatenate(parts, axis=0), high, dims)
    two = dot_bf16(jnp.concatenate(parts[:2], axis=0), middle, dims)
    three = dot_bf16(parts[0], low, dims)
    return one[:rows] + ((one[rows : 2 * rows] + two[:rows]) + (one[2 * rows :] + two[rows:] + three))


def dot_narrow(left, right):
    high, middle, low = pieces_of(left)
    right_high, right_middle, right_low = pieces_of(right)
    columns = right.shape[0]
    both = jnp.concatenate([jnp.concatenate([part, part], axis=1) for part in (right_high, right_middle)], axis=0)
    one = dot_bf16(jnp.concatenate([high, middle], axis=1), both, NT)
    two = dot_bf16(jnp.concatenate([high, low], axis=1), jnp.concatenate([right_low, right_high], axis=1), NT)
    return one[:, :columns] + (one[:, columns:] + two)


def tree_sum(terms):
    while len(terms) > 1:
        terms = [terms[i] + terms[i + 1] if i + 1 < len(terms) else terms[i] for i in range(0, len(terms), 2)]
    return terms[0]


def inverse_factor(tile, zero):
    groups = TILE // SUB
    sub = lax.broadcasted_iota(jnp.int32, (SUB, TILE), 0)
    lane = lax.broadcasted_iota(jnp.int32, (SUB, TILE), 1)
    left = [tile[SUB * r : SUB * r + SUB, :] for r in range(groups)]
    done = []
    pivot_cols = [spread(left[0][:, j : j + 1]) + zero for j in range(SUB)]
    for g in range(groups):
        first, after = g * SUB, (g + 1) * SUB
        last = g + 1 == groups
        inside = (lane >= first) & (lane < after)
        near = [] if last else [spread(left[g + 1][:, first + j : first + j + 1]) for j in range(SUB)]
        coming = [] if last else [spread(left[g + 1][:, after + j : after + j + 1]) + zero for j in range(SUB)]
        cols = [[spread(left[r][:, first + j : first + j + 1]) for r in range(g + 2, groups)] for j in range(SUB)]
        square = {(i, j): spread(pivot_cols[j][i : i + 1, :]) for j in range(SUB) for i in range(j + 1)}
        own = jnp.where(inside, jnp.where(lane == sub + first, 1.0, 0.0), left[g])
        rows = [spread(own[j : j + 1, :]) for j in range(SUB)]
        near_terms = []
        near_solved = []
        share = {}
        solved = [None] * SUB
        pivots = jnp.zeros((SUB, TILE), F32)
        finished = pivots
        for j in range(0, SUB, 2):
            p, q, r = square[j, j], square[j, j + 1], square[j + 1, j + 1]
            minor = p * r - q * q
            over_minor = pltpu.reciprocal(minor, approx=True)
            over_p = pltpu.reciprocal(p, approx=True)
            ip, iq, ir = r * over_minor, -q * over_minor, p * over_minor
            pivots = jnp.where(sub == j, p, jnp.where(sub == j + 1, minor * over_p, pivots))
            second_row = rows[j + 1] - (q * over_p) * rows[j]
            finished = jnp.where(sub == j, rows[j], jnp.where(sub == j + 1, second_row, finished))
            for k in range(j + 2, SUB):
                upper, lower = square[j, k], square[j + 1, k]
                share[j, k], share[j + 1, k] = upper * ip + lower * iq, upper * iq + lower * ir
            for k in range(j + 2, SUB):
                one, two = share[j, k], share[j + 1, k]
                for i in range(j + 2, k + 1):
                    square[i, k] = square[i, k] - (square[j, i] * one + square[j + 1, i] * two)
                rows[k] = rows[k] - (rows[j] * one + rows[j + 1] * two)
                if not last:
                    near[k] = near[k] - (near[j] * one + near[j + 1] * two)
            solved[j], solved[j + 1] = rows[j] * ip + rows[j + 1] * iq, rows[j] * iq + rows[j + 1] * ir
            if not last:
                near_solved += [near[j] * ip + near[j + 1] * iq, near[j] * iq + near[j + 1] * ir]
                near_terms.append(near[j] * solved[j] + near[j + 1] * solved[j + 1])
        if not last:
            pivot_cols = [
                coming[j] - tree_sum([near[k] * spread(near_solved[k][j : j + 1, :]) for k in range(SUB)])
                for j in range(SUB)
            ]
            left[g + 1] = jnp.where(inside, 0.0, left[g + 1]) - tree_sum(near_terms)
        for j in (4, 5, 2, 3, 0, 1):
            solved[j] = solved[j] - tree_sum([share[j, k] * solved[k] for k in range(j // 2 * 2 + 2, SUB)])
        for r in range(g + 2, groups):
            left[r] = jnp.where(inside, 0.0, left[r]) - tree_sum([cols[j][r - g - 2] * solved[j] for j in range(SUB)])
        root = lax.rsqrt(pivots)
        root = root * (1.5 - 0.5 * pivots * root * root)
        done.append(jnp.where(lane < after, finished * root, 0.0))
    return jnp.concatenate(done, axis=0)


def split_scores(residual, x):
    chains = residual.shape[0]
    high, middle, _ = pieces_of(residual)
    both = dot_bf16(jnp.concatenate([high, middle], axis=0), x, NN)
    return both[:chains] + both[chains:]


def chunk_loop(rows, body):
    whole = rows // CHUNK

    @pl.loop(0, whole)
    def _(i):
        body(i, pl.multiple_of(i * CHUNK, CHUNK), CHUNK)

    if rows % CHUNK:
        body(whole, whole * CHUNK, rows % CHUNK)


def start_copies(sources, places, sems, rows):
    for i, lo in enumerate(range(0, rows, CHUNK)):
        at = pl.ds(lo, min(CHUNK, rows - lo))
        for k, (source, place) in enumerate(zip(sources, places)):
            pltpu.make_async_copy(source.at[at, :], place.at[at, :], sems.at[i, k]).start()


def wait_copies(sources, places, sems, i, start, size):
    at = pl.ds(start, size)
    for k, (source, place) in enumerate(zip(sources, places)):
        pltpu.make_async_copy(source.at[at, :], place.at[at, :], sems.at[i, k]).wait()


def own_kernel(core_ref, own_ref, residual_ref, square_ref, score_ref, cross_ref, mine, sems):
    core = core_ref[0]
    rows, half = own_ref.shape[1:]
    sources, places = [own_ref.at[0], own_ref.at[1]], [mine.at[0], mine.at[1]]
    start_copies(sources, places, sems, rows)
    for ref in (square_ref, score_ref, cross_ref):
        ref[...] = jnp.zeros_like(ref)

    def body(i, start, size):
        wait_copies(sources, places, sems, i, start, size)
        at = pl.ds(start, size)
        score_ref[...] += split_scores(residual_ref[:, at], mine[core, at, :])
        cross_ref[...] += dot_bf16(mine[0, at, :], mine[1, at, :], TN)
        for c in range(0, half, STRIP):
            square_ref[c:, c : c + STRIP] += dot_bf16(mine[core, at, c:], mine[core, at, c : c + STRIP], TN)

    chunk_loop(rows, body)


class Layout:
    def __init__(self, count, chains, spots):
        self.count, self.chains = count, chains
        self.pairs = count * (count - 1) // 2 * TILE
        self.diagonals = self.pairs + count // 2 * TILE
        self.scores = self.diagonals + SUB
        self.squares = self.scores + count * chains
        self.used = self.squares + chains
        self.piece = -(-self.used // (spots * SUB)) * SUB
        self.rows = self.piece * spots

    def lower(self, row, col):
        return (row * (row - 1) // 2 + col) * TILE


def put_diagonal(packed_ref, layout, half_at, block):
    count = layout.count // 2
    row_id = lax.broadcasted_iota(jnp.int32, (TILE, TILE), 0)
    col_id = lax.broadcasted_iota(jnp.int32, (TILE, TILE), 1)
    for r in range(count):
        for c in range(r):
            row, col = half_at * count + r, half_at * count + c
            at = pl.multiple_of((lax.shift_right_logical(row * (row - 1), 1) + col) * TILE, TILE)
            packed_ref[pl.ds(at, TILE), :] = block[r * TILE : r * TILE + TILE, c * TILE : c * TILE + TILE]
    for r in range(0, count, 2):
        one = block[r * TILE : r * TILE + TILE, r * TILE : r * TILE + TILE]
        two = block[(r + 1) * TILE : (r + 2) * TILE, (r + 1) * TILE : (r + 2) * TILE]
        place = half_at * (count // 2) + r // 2
        at = pl.multiple_of(layout.pairs + place * TILE, TILE)
        packed_ref[pl.ds(at, TILE), :] = jnp.where(row_id > col_id, one, two)
        packed_ref[pl.ds(layout.diagonals + place, 1), :] = jnp.sum(
            jnp.where(row_id == col_id, one, 0.0), axis=0, keepdims=True
        )


def get_diagonal(packed_ref, layout, tile):
    row_id = lax.broadcasted_iota(jnp.int32, (TILE, TILE), 0)
    col_id = lax.broadcasted_iota(jnp.int32, (TILE, TILE), 1)
    at = layout.pairs + tile // 2 * TILE
    pair = packed_ref[at : at + TILE, :]
    if tile % 2:
        return jnp.where(row_id < col_id, pair, 0.0), jnp.where(row_id == col_id, pair, 0.0)
    row = layout.diagonals + tile // 2
    return jnp.where(row_id > col_id, pair, 0.0), jnp.where(row_id == col_id, packed_ref[row : row + 1, :], 0.0)


def gram_kernel(
    layout, core_ref, own_ref, other_ref, residual_ref, square_ref, own_score_ref, packed_ref, x, total, score, norm, sems
):
    core = core_ref[0]
    rows, half = own_ref.shape[1:]
    sources = [own_ref.at[core], other_ref.at[core]]
    places = [x.at[:, :half], x.at[:, half:]]
    start_copies(sources, places, sems, rows)
    for ref in (total, score, norm):
        ref[...] = jnp.zeros_like(ref)

    def body(i, start, size):
        wait_copies(sources, places, sems, i, start, size)
        at = pl.ds(start, size)
        total[...] += dot_bf16(x[at, half:], x[at, :], TN)
        score[...] += split_scores(residual_ref[:, at], x[at, half:])
        norm[...] += jnp.sum(jnp.square(residual_ref[:, at]), axis=1, keepdims=True)

    chunk_loop(rows, body)
    count, chains = layout.count, layout.chains
    put_diagonal(packed_ref, layout, core, square_ref)
    put_diagonal(packed_ref, layout, 1 - core, total.at[:, half:])
    below = [(r, c, layout.lower(count // 2 + r, c)) for r in range(count // 2) for c in range(count // 2)]

    @pl.when(core == 0)
    def _():
        for r, c, at in below:
            packed_ref[at : at + TILE, :] = total[r * TILE : r * TILE + TILE, c * TILE : c * TILE + TILE]

    @pl.when(core == 1)
    def _():
        for r, c, at in below:
            packed_ref[at : at + TILE, :] = total[c * TILE : c * TILE + TILE, r * TILE : r * TILE + TILE].T

    for k, part in ((core, own_score_ref), (1 - core, score)):
        for col in range(count // 2):
            start_row = pl.multiple_of(layout.scores + (k * (count // 2) + col) * chains, SUB)
            packed_ref[pl.ds(start_row, chains), :] = part[:, col * TILE : col * TILE + TILE]
    packed_ref[layout.squares : layout.used, :] = jnp.broadcast_to(norm[...], (chains, TILE))
    packed_ref[layout.used :, :] = jnp.zeros((layout.rows - layout.used, TILE), F32)


def sum_kernel(parts_ref, sums_ref, parts, copies, in_sems, out_sems):
    count, each = parts.shape[0], copies.shape[0]
    moves = [
        pltpu.make_async_copy(parts_ref.at[i : i + each], parts.at[i : i + each], in_sems.at[i // each])
        for i in range(0, count, each)
    ]
    for move in moves:
        move.start()
    total = None
    for i, move in enumerate(moves):
        move.wait()
        group = tree_sum([parts[i * each + j] for j in range(each)])
        total = group if total is None else total + group
    for i in range(each):
        copies[i] = total
    moves = [
        pltpu.make_async_copy(copies, sums_ref.at[i : i + each], out_sems.at[i // each]) for i in range(0, count, each)
    ]
    for move in moves:
        move.start()
    for move in moves:
        move.wait()


def cross_kernel(own_ref, other_ref, own_cross_ref, cross_ref, x, sems):
    rows = own_ref.shape[1]
    sources, places = [other_ref.at[0], own_ref.at[1]], [x.at[0], x.at[1]]
    start_copies(sources, places, sems, rows)
    cross_ref[0] = own_cross_ref[...]
    cross_ref[1] = jnp.zeros(own_cross_ref.shape, F32)

    def body(i, start, size):
        wait_copies(sources, places, sems, i, start, size)
        at = pl.ds(start, size)
        cross_ref[1] += dot_bf16(x[0, at, :], x[1, at, :], TN)

    chunk_loop(rows, body)


def panel_rows(width, k):
    start = sum(width - j * STRIP for j in range(1, k + 1))
    return slice(start, start + width - (k + 1) * STRIP)


def backward(moved, panels_ref, inverse_ref):
    width = len(moved) * STRIP
    solved = [None] * len(moved)
    for k in reversed(range(len(moved))):
        solved[k] = dot_rows(moved[k], inverse_ref[k], NN)
        if k:
            for j in range(k):
                at = panel_rows(width, j).start + (k - j - 1) * STRIP
                moved[j] = moved[j] - dot_rows(solved[k], panels_ref[at : at + STRIP, :], NN)
    return solved


def factor_kernel(
    layout, packed_hbm, prior_ref, rows_ref, effects_ref, noise_ref, scale_ref, panels_hbm, inverse_hbm, shift_ref,
    packed_ref, panels_ref, inverse_ref, factor_ref, zero_ref, sems
):
    width = factor_ref.shape[1]
    count = width // TILE
    chains = effects_ref.shape[0]
    halfway = layout.lower(count * 3 // 4, 0)
    parts = [slice(0, halfway), slice(halfway, layout.pairs), slice(layout.pairs, layout.rows)]
    arrivals = [pltpu.make_async_copy(packed_hbm.at[at], packed_ref.at[at], sems.at[i]) for i, at in enumerate(parts)]
    for arrival in arrivals:
        arrival.start()
    table_rows = rows_ref[...]
    high = lax.shift_right_logical(table_rows, 7)
    low = lax.bitwise_and(table_rows, TILE - 1)
    prior = jnp.zeros((count, TILE), F32)
    for t in range(prior_ref.shape[0]):
        entry = jnp.broadcast_to(prior_ref[t : t + 1, :], (count, TILE))
        prior = jnp.where(high == t, jnp.take_along_axis(entry, low, axis=1), prior)
    inverse_prior = 1.0 / prior
    diagonal = lax.broadcasted_iota(jnp.int32, (TILE, TILE), 0) == lax.broadcasted_iota(jnp.int32, (TILE, TILE), 1)
    for row in range(count):
        rows = slice(row * TILE, row * TILE + TILE)
        if row in (0, count * 3 // 4):
            arrivals[0 if row == 0 else 1].wait()
        for col in range(row):
            at = layout.lower(row, col)
            factor_ref[rows, col * TILE : col * TILE + TILE] = packed_ref[at : at + TILE, :]
    arrivals[2].wait()
    for row in range(count):
        rows = slice(row * TILE, row * TILE + TILE)
        triangle, middle = get_diagonal(packed_ref, layout, row)
        middle = middle + jnp.where(diagonal, inverse_prior[row : row + 1, :], 0.0)
        factor_ref[rows, rows] = triangle + triangle.T + middle
        at = layout.scores + row * chains
        factor_ref[width : width + chains, rows] = (
            packed_ref[at : at + chains, :] - inverse_prior[row : row + 1, :] * effects_ref[:, rows]
        )
    zero_ref[...] = jnp.zeros_like(zero_ref)

    @pl.loop(0, count)
    def _(k):
        at = pl.multiple_of(k * TILE, TILE)
        pair, side = lax.shift_right_logical(k, 1), pl.ds(pl.multiple_of(lax.bitwise_and(k, 1) * TILE, TILE), TILE)
        inverse_ref[pair, side, side] = inverse_factor(factor_ref[pl.ds(at, TILE), pl.ds(at, TILE)], zero_ref[...])
        for step in range(count):

            @pl.when(k == step)
            def _():
                lo, hi = step * TILE, (step + 1) * TILE
                side = slice(step % 2 * TILE, step % 2 * TILE + TILE)
                inverse = inverse_ref[step // 2, side, side]
                factor_ref[hi:, lo:hi] = dot_narrow(factor_ref[hi:, lo:hi], inverse)
                if step % 2 == 0:
                    panel = factor_ref[hi:, lo:hi]
                    factor_ref[hi:, hi : hi + TILE] = factor_ref[hi:, hi : hi + TILE] - dot_narrow(panel, panel[:TILE, :])
                else:
                    for c in range(hi, width, STRIP):
                        panel = factor_ref[c:, lo - TILE : hi]
                        factor_ref[c:, c : c + STRIP] = factor_ref[c:, c : c + STRIP] - dot_exact(
                            panel, panel[:STRIP, :], NT
                        )
                    below = dot_exact(factor_ref[lo:hi, lo - TILE : lo], inverse_ref[step // 2, :TILE, :TILE], NN)
                    inverse_ref[step // 2, TILE:, :TILE] = -dot_exact(inverse, below, NN)
                    inverse_ref[step // 2, :TILE, TILE:] = jnp.zeros((TILE, TILE), F32)

    scale = scale_ref[...]
    moved = [
        factor_ref[width : width + chains, j : j + STRIP] + scale * noise_ref[:, j : j + STRIP]
        for j in range(0, width, STRIP)
    ]
    for k in range(width // STRIP - 1):
        panels_ref[panel_rows(width, k), :] = factor_ref[(k + 1) * STRIP : width, k * STRIP : (k + 1) * STRIP]
    departures = [
        pltpu.make_async_copy(panels_ref, panels_hbm, sems.at[3]),
        pltpu.make_async_copy(inverse_ref, inverse_hbm, sems.at[4]),
    ]
    for departure in departures:
        departure.start()
    for j, part in enumerate(backward(moved, panels_ref, inverse_ref)):
        shift_ref[:, j * STRIP : j * STRIP + STRIP] = part
    for departure in departures:
        departure.wait()


def cross_share_kernel(core_ref, shift_ref, got_ref, cross_hbm, share_ref, cross_ref, sems):
    core = core_ref[0]
    half = cross_ref.shape[1]
    arrivals = [pltpu.make_async_copy(cross_hbm.at[i], cross_ref.at[i], sems.at[i]) for i in range(2)]
    for arrival in arrivals:
        arrival.start()
    shift = jnp.where(core == 0, shift_ref[...], got_ref[...])
    change = shift.astype(BF16)
    first, last = change[:, :half], change[:, half:]
    mine = jnp.where(core == 0, first, last)
    theirs = jnp.where(core == 0, last, first)
    total = None
    for i, part in enumerate((mine, theirs)):
        arrivals[i].wait()
        product = sum(dot_bf16(part, piece, NN) for piece in pieces_of(cross_ref[i]))
        total = product if total is None else total + product
    share_ref[...] = total


def second_kernel(
    layout, core_ref, shift_ref, share_ref, got_ref, panels_hbm, inverse_hbm, packed_hbm, final_ref,
    panels_ref, inverse_ref, packed_ref, sems
):
    width, count, chains = shift_ref.shape[1], layout.count, layout.chains
    pairs = ((inverse_hbm, inverse_ref), (panels_hbm, panels_ref), (packed_hbm, packed_ref))
    arrivals = [pltpu.make_async_copy(source, place, sems.at[i]) for i, (source, place) in enumerate(pairs)]
    for arrival in arrivals:
        arrival.start()
    keep = jnp.where(core_ref[0] == 1, 1.0, 0.0)
    right = jnp.concatenate([got_ref[...], share_ref[...]], axis=1) * keep
    moved = [right[:, j : j + STRIP] for j in range(0, width, STRIP)]
    arrivals[0].wait()
    for k in range(len(moved)):
        moved[k] = dot_rows(moved[k], inverse_ref[k], NT)
        if k == 0:
            arrivals[1].wait()
        lo = (k + 1) * STRIP
        if lo < width:
            change_by = dot_rows(moved[k], panels_ref[panel_rows(width, k), :], NT)
            for j in range(k + 1, len(moved)):
                moved[j] = moved[j] - change_by[:, (j - k - 1) * STRIP : (j - k) * STRIP]
    for j, part in enumerate(backward(moved, panels_ref, inverse_ref)):
        cols = slice(j * STRIP, j * STRIP + STRIP)
        final_ref[:, cols] = shift_ref[:, cols] - part
    change = final_ref[:, :width].astype(BF16)
    value = change.astype(F32)
    total = jnp.zeros((chains, TILE), F32)
    arrivals[2].wait()
    for row in range(count):
        cols = slice(row * TILE, row * TILE + TILE)
        triangle, middle = get_diagonal(packed_ref, layout, row)
        tiles = [packed_ref[layout.lower(row, col) : layout.lower(row, col) + TILE, :] for col in range(row)]
        strip = jnp.concatenate([tile + tile for tile in tiles] + [triangle + triangle + middle], axis=1)
        product = sum(dot_bf16(change[:, : (row + 1) * TILE], part, NT) for part in pieces_of(strip))
        at = layout.scores + row * chains
        score = packed_ref[at : at + chains, :] - right[:, cols]
        total = total + value[:, cols] * (product - (score + score))
    final_ref[:, width:] = jnp.broadcast_to(jnp.sum(total, axis=1, keepdims=True), (chains, TILE))


def halves(shift, core):
    half = shift.shape[1] // 2
    first, last = shift[:, :half], shift[:, half:]
    return jnp.where(core == 0, first, last), jnp.where(core == 0, last, first)


def update_rows(block, rows, own_ref, other_ref, changes, get, put, x, sems):
    half = own_ref.shape[2]
    chunks = [(lo, min(lo + CHUNK, rows[1])) for lo in range(rows[0], rows[1], CHUNK)]
    copies = []
    for i, (lo, hi) in enumerate(chunks):
        pair = [
            pltpu.make_async_copy(
                source.at[block, lo:hi, :], x.at[lo - rows[0] : hi - rows[0], k * half : (k + 1) * half], sems.at[i, k]
            )
            for k, source in enumerate((own_ref, other_ref))
        ]
        for copy in pair:
            copy.start()
        copies.append(pair)
    change = jnp.concatenate(changes(), axis=1).astype(BF16)
    for i, (lo, hi) in enumerate(chunks):
        for copy in copies[i]:
            copy.wait()
        at = slice(lo - rows[0], hi - rows[0])
        put(lo, hi, get(lo, hi) - dot_bf16(change, x[at, :], NT))


def first_update_kernel(rows, core_ref, own_ref, other_ref, here_ref, there_ref, residual_ref, new_ref, x, sems):
    core = core_ref[0]

    def put(lo, hi, value):
        new_ref[:, lo - rows[0] : hi - rows[0]] = value

    update_rows(
        0, rows, own_ref, other_ref, lambda: halves(jnp.where(core == 0, here_ref[...], there_ref[...]), core),
        lambda lo, hi: residual_ref[:, lo:hi], put, x, sems,
    )


def last_update_kernel(
    layout, people, cut, core_ref, own_ref, other_ref, here_ref, there_ref, low_ref, high_ref, effects_ref,
    first_here_ref, first_there_ref, norm_ref, chi_ref, new_ref, new_effects_ref, draw_ref, x, sems
):
    core, width = core_ref[0], 2 * own_ref.shape[2]

    def changes():
        mine, theirs = halves(jnp.where(core == 1, here_ref[:, :width], there_ref[:, :width]), core)
        new_effects_ref[1] = effects_ref[1] + mine
        return mine, theirs

    def get(lo, hi):
        return low_ref[:, lo:hi] if lo < cut else high_ref[:, lo - cut : hi - cut]

    def put(lo, hi, value):
        new_ref[:, lo:hi] = value

    update_rows(1, (0, own_ref.shape[1]), own_ref, other_ref, changes, get, put, x, sems)
    first = halves(jnp.where(core == 0, first_here_ref[...], first_there_ref[...]), core)[0]
    new_effects_ref[0] = effects_ref[0] + first
    squares = norm_ref[...] + (here_ref[:, width:] + there_ref[:, width:])
    draw_ref[...] = squares.T[:1, :] / (people * chi_ref[...])


def update_call(kernel, out_shape, rows, genotypes, name, *operands):
    half = genotypes.shape[2]
    return pl.pallas_call(
        kernel,
        out_shape=out_shape,
        in_specs=[SMEM, ANY, ANY] + [VMEM] * (len(operands) - 2),
        out_specs=(VMEM,) * len(out_shape),
        scratch_shapes=[
            pltpu.VMEM((rows, 2 * half), BF16),
            pltpu.SemaphoreType.DMA((-(-rows // CHUNK), 2)),
        ],
        compiler_params=PARAMS,
        cost_estimate=pl.CostEstimate(flops=64 * rows * half * 8, bytes_accessed=4 * rows * half, transcendentals=0),
        name=name,
    )(operands[0], genotypes, *operands[1:])


def line_sums(value, beside, spots):
    stride = 1
    beside = list(beside)
    ready = []
    while stride < spots:
        at = [i // stride % LINE for i in range(spots)]
        one, two, three = (
            lax.ppermute(value, "ind", [(i, i + ((at[i] + step) % LINE - at[i]) * stride) for i in range(spots)])
            for step in range(1, LINE)
        )
        if beside:
            one, two, three, done = lax.optimization_barrier((one, two, three, beside.pop(0)))
            ready.append(done)
        even = lax.axis_index("ind") // stride % 2 == 0
        value = (value + jnp.where(even, three, one)) + (two + jnp.where(even, one, three))
        stride *= LINE
    return value, ready + beside


def local(genotypes, residual, effects, noise, prior_var, block_snps, noise_var, chi_scaled):
    blocks, rows, half = genotypes.shape
    chains = residual.shape[0]
    width = 2 * half
    count = width // TILE
    spots = lax.axis_size("ind")
    core = lax.axis_index("snp")
    core_arg = jnp.reshape(core.astype(jnp.int32), (1,))
    swap = [(0, 1), (1, 0)]
    pieces = -(-rows // CHUNK)

    other = lax.ppermute(genotypes, "snp", swap)
    other_effects = lax.ppermute(effects, "snp", swap)

    layout = Layout(count, chains, spots)
    piece = layout.piece
    square, own_score, own_cross = pl.pallas_call(
        own_kernel,
        out_shape=(
            jax.ShapeDtypeStruct((half, half), F32),
            jax.ShapeDtypeStruct((chains, half), F32),
            jax.ShapeDtypeStruct((half, half), F32),
        ),
        in_specs=[SMEM, ANY, VMEM],
        out_specs=(VMEM,) * 3,
        scratch_shapes=[pltpu.VMEM((2, rows, half), BF16), pltpu.SemaphoreType.DMA((pieces, 2))],
        compiler_params=PARAMS,
        cost_estimate=pl.CostEstimate(flops=2 * rows * half * half, bytes_accessed=2 * rows * half, transcendentals=0),
        name="own",
    )(core_arg, genotypes, residual)
    packed = pl.pallas_call(
        functools.partial(gram_kernel, layout),
        out_shape=jax.ShapeDtypeStruct((spots * piece, TILE), F32),
        in_specs=[SMEM, ANY, ANY, VMEM, VMEM, VMEM],
        out_specs=VMEM,
        scratch_shapes=[
            pltpu.VMEM((rows, width), BF16),
            pltpu.VMEM((half, width), F32),
            pltpu.VMEM((chains, half), F32),
            pltpu.VMEM((chains, 1), F32),
            pltpu.SemaphoreType.DMA((pieces, 2)),
        ],
        compiler_params=PARAMS,
        cost_estimate=pl.CostEstimate(flops=0, bytes_accessed=0, transcendentals=0),
        name="gram",
    )(core_arg, genotypes, other, residual, square, own_score)
    late_other, packed = lax.optimization_barrier((other, packed))
    cross = pl.pallas_call(
        cross_kernel,
        out_shape=jax.ShapeDtypeStruct((2, half, half), F32),
        in_specs=[ANY, ANY, VMEM],
        out_specs=VMEM,
        scratch_shapes=[
            pltpu.VMEM((2, rows, half), BF16),
            pltpu.SemaphoreType.DMA((pieces, 2)),
        ],
        compiler_params=PARAMS,
        cost_estimate=pl.CostEstimate(flops=2 * rows * half * half, bytes_accessed=4 * rows * half, transcendentals=0),
        name="cross",
    )(genotypes, late_other, own_cross)
    packed = lax.all_to_all(packed.reshape(spots, piece, TILE), "ind", 0, 0)
    packed, cross = lax.optimization_barrier((packed, cross))
    packed = pl.pallas_call(
        sum_kernel,
        out_shape=jax.ShapeDtypeStruct(packed.shape, F32),
        in_specs=[ANY],
        out_specs=ANY,
        scratch_shapes=[
            pltpu.VMEM((spots, piece, TILE), F32),
            pltpu.VMEM((SUB, piece, TILE), F32),
            pltpu.SemaphoreType.DMA((spots // SUB,)),
            pltpu.SemaphoreType.DMA((spots // SUB,)),
        ],
        compiler_params=PARAMS,
        name="sums",
    )(packed)
    packed = lax.all_to_all(packed, "ind", 0, 0).reshape(spots * piece, TILE)

    own_effects = lax.dynamic_index_in_dim(effects, core, 0, keepdims=False)
    got_effects = lax.dynamic_index_in_dim(other_effects, core, 0, keepdims=False)
    block_effects = jnp.where(
        core == 0,
        jnp.concatenate([own_effects, got_effects], axis=1),
        jnp.concatenate([got_effects, own_effects], axis=1),
    )
    block_noise = lax.dynamic_index_in_dim(noise, core, 0, keepdims=False)
    block_rows = lax.dynamic_index_in_dim(block_snps.reshape(blocks, count, TILE), core, 0, keepdims=False)
    scale = jnp.sqrt(noise_var)[:, None]
    panels_shape = (panel_rows(width, width // STRIP - 1).start, STRIP)
    inverse_shape = (width // STRIP, STRIP, STRIP)
    panels, inverse, shift = pl.pallas_call(
        functools.partial(factor_kernel, layout),
        out_shape=(
            jax.ShapeDtypeStruct(panels_shape, F32),
            jax.ShapeDtypeStruct(inverse_shape, F32),
            jax.ShapeDtypeStruct((chains, width), F32),
        ),
        in_specs=[ANY] + [VMEM] * 5,
        out_specs=(ANY, ANY, VMEM),
        scratch_shapes=[
            pltpu.VMEM(packed.shape, F32),
            pltpu.VMEM(panels_shape, F32),
            pltpu.VMEM(inverse_shape, F32),
            pltpu.VMEM((width + chains, width), F32),
            pltpu.VMEM((SUB, TILE), F32),
            pltpu.SemaphoreType.DMA((5,)),
        ],
        compiler_params=PARAMS,
        cost_estimate=pl.CostEstimate(flops=0, bytes_accessed=0, transcendentals=0),
        name="factor",
    )(packed, prior_var.reshape(-1, TILE), block_rows, block_effects, block_noise, scale)

    got_shift = lax.ppermute(shift, "snp", swap)
    share = pl.pallas_call(
        cross_share_kernel,
        out_shape=jax.ShapeDtypeStruct((chains, half), F32),
        in_specs=[SMEM] + [VMEM] * 2 + [ANY],
        out_specs=VMEM,
        scratch_shapes=[pltpu.VMEM(cross.shape, F32), pltpu.SemaphoreType.DMA((2,))],
        compiler_params=PARAMS,
        name="cross_share",
    )(core_arg, shift, got_shift, cross)
    cut = rows // 2 // CHUNK * CHUNK + CHUNK if rows > CHUNK else rows
    after = [
        update_call(
            functools.partial(first_update_kernel, part),
            (jax.ShapeDtypeStruct((chains, part[1] - part[0]), F32),),
            part[1] - part[0],
            genotypes,
            "first_update",
            core_arg,
            other,
            shift,
            got_shift,
            residual,
        )[0]
        for part in ((0, cut), (cut, rows))
    ]
    share, after = line_sums(share, after, spots)
    got = lax.ppermute(share, "snp", swap)
    final = pl.pallas_call(
        functools.partial(second_kernel, layout),
        out_shape=jax.ShapeDtypeStruct((chains, width + TILE), F32),
        in_specs=[SMEM] + [VMEM] * 3 + [ANY] * 3,
        out_specs=VMEM,
        scratch_shapes=[
            pltpu.VMEM(panels_shape, F32),
            pltpu.VMEM(inverse_shape, F32),
            pltpu.VMEM(packed.shape, F32),
            pltpu.SemaphoreType.DMA((3,)),
        ],
        compiler_params=PARAMS,
        name="second",
    )(core_arg, shift, share, got, panels, inverse, packed)
    got_final = lax.ppermute(final, "snp", swap)
    new_residual, new_effects, draw = update_call(
        functools.partial(last_update_kernel, layout, rows * spots, cut),
        (
            jax.ShapeDtypeStruct(residual.shape, F32),
            jax.ShapeDtypeStruct(effects.shape, F32),
            jax.ShapeDtypeStruct((1, chains), F32),
        ),
        rows,
        genotypes,
        "last_update",
        core_arg,
        other,
        final,
        got_final,
        *after,
        effects,
        shift,
        got_shift,
        packed[layout.squares : layout.used],
        chi_scaled[None, :],
    )
    return (new_effects, new_residual, draw[0])


def solution(mesh):
    placed = (P(None, "ind", "snp"), P(None, "ind"), P(None, None, "snp"), P(), P(), P(), P(), P())
    return jax.shard_map(
        local,
        mesh=mesh,
        in_specs=placed,
        out_specs=(P(None, None, "snp"), P(None, "ind"), P()),
        check_vma=False,
    )
```
